32 devices in a mesh: seq: 8 (over z, y), own: 4 (over x, core).
Axes of the slice: x: 2, y: 2, z: 4, core: 2. Of those that a mesh axis runs over, the one named last changes fastest.
Arguments:
- inputs: bfloat16 [24576, 768], P(('seq', 'own')), may hold values from -30 to 30
- cotangent: bfloat16 [12288, 768], P(('seq', 'own')), may hold values from -30 to 30
- small_params: float32 [6, 768], replicated, may hold values from -2 to 2
- small_first: float32 [6, 768], replicated, may hold values from -1 to 1
- small_second: float32 [6, 768], replicated, may hold values from 0 to 0.01
- slot_of_matrix: int32 [7], replicated, may hold values from 0 to 7, as said below
- master: float32 [8, 768, 768], P('own'), may hold values from -3 to 3
- first_moment: float32 [8, 768, 768], P('own'), may hold values from -1 to 1
- second_moment: float32 [8, 768, 768], P('own'), may hold values from 0 to 0.01
- left_basis: float32 [8, 768, 768], P('own'), may hold values from -1 to 1, as said below
- right_basis: float32 [8, 768, 768], P('own'), may hold values from -1 to 1, as said below
Outputs:
- pooled: bfloat16 [12288, 768], P(('seq', 'own'))
- input_grad: bfloat16 [24576, 768], P(('seq', 'own'))
- grad_norm: float32 [], replicated
- new_master: float32 [8, 768, 768], P('own')
- new_first: float32 [8, 768, 768], P('own')
- new_second: float32 [8, 768, 768], P('own')
- new_small: float32 [6, 768], replicated
- new_small_first: float32 [6, 768], replicated
- new_small_second: float32 [6, 768], replicated
The draws below stay inside these ranges and needn't reach their ends.
Inputs may be any that keep to these rules, and one draw needn't show every extreme that they name: `slot_of_matrix`: 7 distinct slot numbers; slot s lies on index s // 2 of own, no index of own holds more than 2 matrices and some index holds exactly 2. `left_basis`: each slot's matrix is orthogonal. `right_basis`: each slot's matrix is orthogonal.
All inputs are finite; a program needn't handle non-finite values.
Results may differ from the reference program's by a relative error of at most 0.011.
Values may be sent and summed in bfloat16 or wider, within the bound.
A program may use at most 192 MiB of HBM per device.

```python
import math
import jax
import jax.numpy as jnp
from jax import lax

C = 768
NMAT = 7
STEP = 10
TOKENS = 24576
SLOTS = 8


def slot_numbers_of(key):
    return jax.random.permutation(jax.random.fold_in(key, 101), SLOTS)[:NMAT].astype(jnp.int32)


def per_slot(key, conv_value, branch_value, pool_value):
    slot_numbers = slot_numbers_of(key)
    scale_table = jnp.array([conv_value, conv_value, conv_value, conv_value, conv_value, branch_value, pool_value], jnp.float32)
    slot_hits = (slot_numbers[:, None] == jnp.arange(SLOTS, dtype=jnp.int32)[None, :]).astype(jnp.float32)
    empty_slot = 1.0 - jnp.sum(slot_hits, axis=0)
    return jnp.sum(slot_hits * scale_table[:, None], axis=0) + empty_slot * conv_value


def draw_noise(key, shape):
    return jax.random.truncated_normal(key, -6.0, 6.0, shape, jnp.float32)


def ramp_of(count):
    ramp_top = 2.0
    return 1.0 + ramp_top * jnp.arange(count, dtype=jnp.float32) / (count - 1)


def orthogonal(key):
    matrix = jnp.eye(C, dtype=jnp.float32)
    for turn_index in range(6):
        key, key_perm, key_angle = jax.random.split(key, 3)
        row_order = jax.random.permutation(key_perm, C)
        matrix = matrix[row_order]
        angles = jax.random.uniform(key_angle, (C // 2, 1), jnp.float32, -math.pi, math.pi)
        paired = matrix.reshape(C // 2, 2, C)
        upper_rows = paired[:, 0]
        lower_rows = paired[:, 1]
        matrix = jnp.stack([jnp.cos(angles) * upper_rows - jnp.sin(angles) * lower_rows, jnp.sin(angles) * upper_rows + jnp.cos(angles) * lower_rows], axis=1).reshape(C, C)
    return matrix


def draw_inputs(key, part):
    offsets = 0.5 * jax.random.truncated_normal(jax.random.fold_in(key, 2), -6.0, 6.0, (1, C), jnp.float32)
    return (ramp_of(TOKENS)[:, None] * (draw_noise(jax.random.fold_in(key, 1), (TOKENS, C)) + offsets)).astype(jnp.bfloat16)


def draw_cotangent(key, part):
    return (ramp_of(TOKENS // 2)[:, None] * draw_noise(jax.random.fold_in(key, 11), (TOKENS // 2, C))).astype(jnp.bfloat16)


def draw_slot_of_matrix(key, part):
    return slot_numbers_of(key)


def draw_master(key, part):
    scales = per_slot(key, 1.0 / math.sqrt(5 * C), 1.0 / math.sqrt(C), 2.0 / math.sqrt(C))
    return draw_noise(jax.random.fold_in(key, 3), (SLOTS, C, C)) * scales[:, None, None]


def draw_first_moment(key, part):
    scales = per_slot(key, 0.55, 0.55, 0.35)
    return 0.11 * draw_noise(jax.random.fold_in(key, 4), (SLOTS, C, C)) * scales[:, None, None]


def draw_second_moment(key, part):
    scales = per_slot(key, 0.55, 0.55, 0.35)
    factors = jax.random.uniform(jax.random.fold_in(key, 5), (SLOTS, C, C), jnp.float32, 1.0, 4.0)
    return 0.001 * factors * (scales * scales)[:, None, None]


def draw_left_basis(key, part):
    return jax.vmap(orthogonal)(jax.random.split(jax.random.fold_in(key, 6), SLOTS))


def draw_right_basis(key, part):
    return jax.vmap(orthogonal)(jax.random.split(jax.random.fold_in(key, 7), SLOTS))


def draw_small_params(key, part):
    bias_rows = 0.3 * draw_noise(jax.random.fold_in(key, 8), (6, C))
    gain_rows = 1.0 + 0.3 * jax.random.uniform(jax.random.fold_in(key, 9), (6, C), jnp.float32, -1.0, 1.0)
    row_index = jnp.arange(6, dtype=jnp.int32)[:, None]
    is_gain = jnp.logical_or(row_index == 0, row_index == 3)
    return jnp.where(is_gain, gain_rows, bias_rows)


def draw_small_first(key, part):
    return 0.09 * draw_noise(jax.random.fold_in(key, 10), (6, C))


def draw_small_second(key, part):
    return 0.00064 * jax.random.uniform(jax.random.fold_in(key, 12), (6, C), jnp.float32, 1.0, 4.0)


def setup_inputs(seed: int = 0) -> dict:
    keys = jax.random.split(jax.random.key(seed), 12)
    return {
        "inputs": draw_inputs(jax.random.fold_in(keys[11], 71), 0),
        "cotangent": draw_cotangent(jax.random.fold_in(keys[11], 71), 0),
        "small_params": draw_small_params(jax.random.fold_in(keys[11], 71), 0),
        "small_first": draw_small_first(jax.random.fold_in(keys[11], 71), 0),
        "small_second": draw_small_second(jax.random.fold_in(keys[11], 71), 0),
        "slot_of_matrix": draw_slot_of_matrix(jax.random.fold_in(keys[11], 71), 0),
        "master": draw_master(jax.random.fold_in(keys[11], 71), 0),
        "first_moment": draw_first_moment(jax.random.fold_in(keys[11], 71), 0),
        "second_moment": draw_second_moment(jax.random.fold_in(keys[11], 71), 0),
        "left_basis": draw_left_basis(jax.random.fold_in(keys[11], 71), 0),
        "right_basis": draw_right_basis(jax.random.fold_in(keys[11], 71), 0),
    }


@jax.custom_vjp
def low(v):
    return lax.optimization_barrier(v.astype(jnp.bfloat16)).astype(jnp.float32)

@jax.custom_vjp
def low_back(v):
    return v

def low_keep(v):
    return (low(v), None)

def low_pass(kept, grad):
    return (grad,)

def back_keep(v):
    return (v, None)

def back_low(kept, grad):
    return (low(grad),)
low.defvjp(low_keep, low_pass)
low_back.defvjp(back_keep, back_low)
NORM_EPS = 1e-05
BETA_ONE = 0.9
BETA_TWO = 0.999
ADAM_EPS = 1e-08
DECAY_RATE = 0.01
LEARN_RATE = 0.02
SMALL_RATE = 0.1
CLIP_RATIO = 0.5
HIGHEST_PREC = lax.Precision.HIGHEST

def gelu_smooth(values):
    return jax.nn.gelu(values, approximate=True)

def adam_moments(grads, first_old, second_old):
    first_new = BETA_ONE * first_old + (1.0 - BETA_ONE) * grads
    second_new = BETA_TWO * second_old + (1.0 - BETA_TWO) * grads * grads
    direction = first_new / (1.0 - BETA_ONE ** STEP) / (jnp.sqrt(second_new / (1.0 - BETA_TWO ** STEP)) + ADAM_EPS)
    return (first_new, second_new, direction)

def reference(inputs, cotangent, small_params, small_first, small_second, slot_of_matrix, master, first_moment, second_moment, left_basis, right_basis):
    length, channels = inputs.shape
    block_rows = math.gcd(length, 4096)
    block_count = length // block_rows
    block_ids = jnp.arange(block_count, dtype=jnp.int32)
    weights = jnp.take(master, slot_of_matrix, axis=0)
    values = inputs.astype(jnp.float32)
    incoming = cotangent.astype(jnp.float32)

    def forward(values, small_vec, weights):
        rounded = low(weights)
        mean_one = lax.optimization_barrier(jnp.mean(values, axis=0))
        rstd_one = lax.rsqrt(lax.optimization_barrier(jnp.mean(values * values, axis=0)) - mean_one * mean_one + NORM_EPS)
        padded = jnp.pad(values, ((2, 2), (0, 0)))

        def conv_block(block_index):
            first_row = block_index * block_rows
            window = lax.dynamic_slice_in_dim(padded, first_row, block_rows + 4, 0)
            where_pos = first_row - 2 + jnp.arange(block_rows + 4, dtype=jnp.int32)
            inside = jnp.logical_and(where_pos >= 0, where_pos < length).astype(jnp.float32)[:, None]
            active = low(gelu_smooth((window - mean_one) * rstd_one * small_vec[0] + small_vec[1]) * inside)
            summed = jnp.zeros((block_rows, channels), jnp.float32)
            for offset in range(5):
                summed = summed + jnp.dot(active[offset:offset + block_rows], rounded[offset], precision=HIGHEST_PREC)
            return low_back(summed) + small_vec[2]
        hidden = lax.map(jax.checkpoint(conv_block), block_ids).reshape(length, channels)
        mean_two = lax.optimization_barrier(jnp.mean(hidden, axis=0))
        rstd_two = lax.rsqrt(lax.optimization_barrier(jnp.mean(hidden * hidden, axis=0)) - mean_two * mean_two + NORM_EPS)

        def pool_block(block_index):
            part_hidden = lax.dynamic_slice_in_dim(hidden, block_index * block_rows, block_rows, 0)
            active = low(gelu_smooth((part_hidden - mean_two) * rstd_two * small_vec[3] + small_vec[4]))
            branch = low_back(jnp.dot(active, rounded[5], precision=HIGHEST_PREC))
            residual = part_hidden + branch + small_vec[5]
            logits = low_back(jnp.dot(low(residual), rounded[6], precision=HIGHEST_PREC))
            pair_prob = jax.nn.softmax(logits.reshape(block_rows // 2, 2, channels), axis=1)
            return lax.optimization_barrier(jnp.sum(pair_prob * residual.reshape(block_rows // 2, 2, channels), axis=1))
        return lax.map(jax.checkpoint(pool_block), block_ids).reshape(length // 2, channels)
    pooled, pullback = jax.vjp(forward, values, small_params, weights)
    input_grad, small_grad, matrix_grad = pullback(incoming)
    grad_norm = jnp.sqrt(jnp.sum(matrix_grad * matrix_grad) + jnp.sum(small_grad * small_grad))
    factor = jnp.minimum(1.0, CLIP_RATIO * channels * math.sqrt(NMAT) / (grad_norm + 1e-06))
    left_turn = jnp.take(left_basis, slot_of_matrix, axis=0)
    right_turn = jnp.take(right_basis, slot_of_matrix, axis=0)
    first_old = jnp.take(first_moment, slot_of_matrix, axis=0)
    second_old = jnp.take(second_moment, slot_of_matrix, axis=0)
    turned = jnp.einsum('kji,kjl->kil', left_turn, matrix_grad * factor, precision=HIGHEST_PREC)
    turned = jnp.einsum('kil,klm->kim', turned, right_turn, precision=HIGHEST_PREC)
    first_new, second_new, direction = adam_moments(turned, first_old, second_old)
    back_turn = jnp.einsum('kij,kjl->kil', left_turn, direction, precision=HIGHEST_PREC)
    back_turn = jnp.einsum('kil,kml->kim', back_turn, right_turn, precision=HIGHEST_PREC)
    master_new = weights - LEARN_RATE * (back_turn + DECAY_RATE * weights)
    new_master = master.at[slot_of_matrix].set(master_new)
    new_first = first_moment.at[slot_of_matrix].set(first_new)
    new_second = second_moment.at[slot_of_matrix].set(second_new)
    small_first_new, small_second_new, small_dir = adam_moments(small_grad * factor, small_first, small_second)
    new_small = small_params - SMALL_RATE * (small_dir + DECAY_RATE * small_params)
    return (pooled.astype(jnp.bfloat16), input_grad.astype(jnp.bfloat16), grad_norm, new_master, new_first, new_second, new_small, small_first_new, small_second_new)
```

```python
import functools
import math

import jax
import jax.numpy as jnp
from jax import lax
from jax.experimental import pallas as pl
from jax.experimental.pallas import tpu as pltpu
from jax.sharding import PartitionSpec as P

NMAT = 7
STEP = 10
NORM_EPS = 1e-05
BETA_ONE = 0.9
BETA_TWO = 0.999
ADAM_EPS = 1e-08
DECAY_RATE = 0.01
LEARN_RATE = 0.02
SMALL_RATE = 0.1
CLIP_RATIO = 0.5
MESH = pl.DeviceIdType.MESH
F32 = jnp.float32
BF16 = jnp.bfloat16

ORDER = (6, 5, 0, 1, 2, 3, 4)
TILE = 256


def mm(a, b):
    return lax.dot_general(a, b, (((1,), (0,)), ((), ())), preferred_element_type=F32)


def mm_t(a, b):
    return lax.dot_general(a, b, (((1,), (1,)), ((), ())), preferred_element_type=F32)


def gelu_both(v):
    k = math.sqrt(2.0 / math.pi)
    sq = v * v
    t = jnp.tanh(v * (k + (k * 0.044715) * sq))
    half = 0.5 + 0.5 * t
    slope = half + (0.5 * v) * (1.0 - t * t) * (k + (3.0 * k * 0.044715) * sq)
    return v * half, slope


def colsum(v):
    return jnp.sum(v, axis=0, keepdims=True)


def kernel(
    dims,
    slot_ref,
    sp_ref,
    dy_ref,
    x_hbm,
    master_hbm,
    pooled_ref,
    ig_ref,
    g_ref,
    gs_ref,
    ssq_ref,
    w,
    mst,
    xf,
    sh,
    d1,
    h,
    a2,
    d2,
    r,
    rd,
    dl,
    dz,
    b,
    a1t,
    rdt,
    snd,
    own,
    rcv,
    fst,
    sec,
    zr,
    zs,
    res,
    stage,
    par,
    ar_val,
    ar_core,
    ar_chip,
    hx_s,
    hx_r,
    hd_s,
    hd_r,
    il,
    sq_all,
    ld_sem,
    w_send,
    w_sib,
    w_x,
    w_y,
    w_z,
    ar_s,
    ar_r,
    ar_s2,
    ar_r2,
    h_s,
    h_r,
    c_s,
    c_r,
    f_s,
    f_r,
    s_s,
    s_r,
    z_s,
    z_r,
    zb_s,
    zb_r,
    g_s,
    g_r,
    q_s,
    q_r,
    g_l,
):
    NX, NY, NZ, cap, rows_total = dims
    pos, ch = dz.shape
    hp = pos // 2
    seq_n, own_n = NZ * NY, NX * 2
    n_dev = seq_n * own_n
    chips = n_dev // 2
    rb = ch // 2 // (NX * NY)
    nt = ch // TILE
    s_ix, o_ix = lax.axis_index("seq"), lax.axis_index("own")
    z, y = s_ix // NY, lax.rem(s_ix, NY)
    x, c = o_ix // 2, lax.rem(o_ix, 2)
    me = s_ix * own_n + o_ix
    inv_n = 1.0 / rows_total

    def dev(z_, y_, x_, c_):
        return (z_ * NY + y_, x_ * 2 + c_)

    def remote(src, dst, ss, rs, to):
        return pltpu.make_async_remote_copy(
            src_ref=src, dst_ref=dst, send_sem=ss, recv_sem=rs, device_id=to, device_id_type=MESH
        )

    def wait_bytes(ref, sem):
        pltpu.make_async_copy(ref, ref, sem).wait()

    sib = dev(z, y, x, 1 - c)

    for j in range(cap):
        pltpu.make_async_copy(master_hbm.at[j], mst.at[j], ld_sem.at[j]).start()
    pltpu.make_async_copy(x_hbm, dz, ld_sem.at[cap]).start()

    barrier = pltpu.get_barrier_semaphore()

    def greet(i, carry):
        p = lax.rem(me + 1 + i, n_dev)
        pl.semaphore_signal(
            barrier, inc=1, device_id=(p // own_n, lax.rem(p, own_n)), device_id_type=MESH
        )
        return carry

    lax.fori_loop(0, n_dev - 1, greet, 0)

    for j in range(cap):
        pltpu.make_async_copy(master_hbm.at[j], mst.at[j], ld_sem.at[j]).wait()
        w[o_ix * cap + j] = mst[j].astype(BF16)
    pl.semaphore_wait(barrier, n_dev - 1)

    thirds = (NX, NY, NZ) == (2, 2, 4)
    QR = 64
    third = ch // 3
    nq = third // QR
    w_base = o_ix * cap
    if thirds:
        is_end = jnp.logical_or(z == 0, z == NZ - 1)
        zp = z + 1 - 2 * lax.rem(z, 2)
        ox = (1 - x) * 2 + c
        to_x, to_y, to_z = dev(z, y, 1 - x, c), dev(z, 1 - y, x, c), dev(zp, y, x, c)
        alpha = jnp.where(is_end, y, 2)
        z_part = jnp.where(is_end, 2, y)

        def piece(slot, part, q):
            return w.at[slot, pl.ds(pl.multiple_of(part * third + q * QR, QR), QR)]

        def each(fn):
            def body(i, carry):
                fn(i, i // nq, lax.rem(i, nq))
                return carry

            lax.fori_loop(0, cap * nq, body, 0)

        def send_x(i, j, q):
            ref = piece(w_base + j, alpha, q)
            remote(ref, ref, w_send.at[0], w_x.at[i], to_x).start()

        each(send_x)
        for j in range(cap):
            ref = w.at[w_base + j]
            remote(ref, ref, w_send.at[0], w_sib.at[0], sib).start()

        def relay(i, j, q):
            rx = piece(ox * cap + j, alpha, q)
            remote(rx, rx, w_send.at[0], w_x.at[i], to_x).wait_recv()
            remote(rx, rx, w_send.at[0], w_z.at[i], to_z).start()

            @pl.when(is_end)
            def _():
                remote(rx, rx, w_send.at[0], w_y.at[i], to_y).start()

            remote(rx, rx, w_send.at[0], w_sib.at[0], sib).start()
            rz = piece(ox * cap + j, z_part, q)
            remote(rz, rz, w_send.at[0], w_z.at[i], to_z).wait_recv()

            @pl.when(jnp.logical_not(is_end))
            def _():
                remote(rz, rz, w_send.at[0], w_y.at[i], to_y).start()

            remote(rz, rz, w_send.at[0], w_sib.at[0], sib).start()

        def last_relay(i, j, q):
            ry = piece(ox * cap + j, 1 - y, q)
            remote(ry, ry, w_send.at[0], w_y.at[i], to_y).wait_recv()
            remote(ry, ry, w_send.at[0], w_sib.at[0], sib).start()

        def weights_first():
            each(relay)

        def weights_end():
            each(last_relay)
            wait_bytes(w.at[pl.ds(0, 2 * cap)], w_sib.at[0])
            wait_bytes(w.at[pl.ds(0, 3 * cap)], w_send.at[0])

    else:

        def send_w(i, carry):
            p = lax.rem(o_ix + 1 + i, own_n)
            ref = w.at[pl.ds(w_base, cap)]
            remote(ref, ref, w_send.at[0], w_sib.at[0], (s_ix, p)).start()
            return carry

        lax.fori_loop(0, own_n - 1, send_w, 0)

        def weights_first():
            pass

        def weights_end():
            wait_bytes(w.at[pl.ds(0, (own_n - 1) * cap)], w_sib.at[0])
            wait_bytes(w.at[pl.ds(0, (own_n - 1) * cap)], w_send.at[0])

    chip = s_ix * NX + x

    def ar_begin(i):
        remote(ar_val.at[i], ar_core.at[i], ar_s.at[i], ar_r.at[i], sib).start()

    def ar_chip_copy(i, k):
        p = lax.rem(chip + 1 + k, chips)
        ref = ar_chip.at[i % ar_chip.shape[0], chip]
        return remote(
            ref, ref, ar_s2.at[i], ar_r2.at[i], (p // NX, lax.rem(p, NX) * 2 + c)
        )

    def ar_mid(i):
        remote(ar_val.at[i], ar_core.at[i], ar_s.at[i], ar_r.at[i], sib).wait()
        ar_chip[i % ar_chip.shape[0], chip] = ar_val[i] + ar_core[i]

        def body(k, carry):
            ar_chip_copy(i, k).start()
            return carry

        lax.fori_loop(0, chips - 1, body, 0)

    def ar_end(i):
        at = i % ar_chip.shape[0]
        wait_bytes(ar_chip.at[at, pl.ds(0, chips - 1)], ar_r2.at[i])
        wait_bytes(ar_chip.at[at, pl.ds(0, chips - 1)], ar_s2.at[i])
        return jnp.sum(ar_chip[at], axis=0)

    pltpu.make_async_copy(x_hbm, dz, ld_sem.at[cap]).wait()
    ts = hp // 3
    total = jnp.zeros((1, ch), F32)
    square = jnp.zeros((1, ch), F32)
    for i in range(3):
        for j in range(ch // 128):
            il[j] = dz[2 * ts * i : 2 * ts * (i + 1), j * 128 : (j + 1) * 128].astype(F32)
        for k in range(2):
            v = jnp.concatenate([il[j, pl.ds(k, ts, stride=2), :] for j in range(ch // 128)], axis=1)
            xf[k * hp + i * ts : k * hp + (i + 1) * ts] = v
            total += colsum(v)
            square += colsum(v * v)
    zero_row = jnp.zeros((1, ch), F32)
    ar_val[0] = jnp.concatenate([total, square, zero_row, zero_row], axis=0)
    ar_begin(0)
    before, after = lax.rem(me + n_dev - 1, n_dev), lax.rem(me + 1, n_dev)
    to_before = (before // own_n, lax.rem(before, own_n))
    to_after = (after // own_n, lax.rem(after, own_n))
    has_before = jnp.where(me > 0, 1.0, 0.0).astype(F32)
    has_after = jnp.where(me < n_dev - 1, 1.0, 0.0).astype(F32)
    hx_s[0] = jnp.concatenate([xf[0:1], xf[hp : hp + 1]], axis=0)
    hx_s[1] = jnp.concatenate([xf[hp - 1 : hp], xf[pos - 1 : pos]], axis=0)
    hx = [
        remote(hx_s.at[0], hx_r.at[1], h_s.at[0], h_r.at[0], to_before),
        remote(hx_s.at[1], hx_r.at[0], h_s.at[1], h_r.at[1], to_after),
    ]
    for cp in hx:
        cp.start()
    ar_mid(0)
    weights_first()
    sums = ar_end(0)
    for cp in hx:
        cp.wait()

    mu1 = sums[0:1] * inv_n
    rstd1 = lax.rsqrt(sums[1:2] * inv_n - mu1 * mu1 + NORM_EPS)
    g1, b1, c1 = sp_ref[0:1], sp_ref[1:2], sp_ref[2:3]
    g2, b2, c2 = sp_ref[3:4], sp_ref[4:5], sp_ref[5:6]
    PAD = 8

    def windows():
        for k in range(2):
            for i in range(3):
                b[k * hp + i * ts : k * hp + (i + 1) * ts] = sh[
                    k, PAD - 1 + i * ts : PAD - 1 + (i + 1) * ts
                ].astype(BF16)
                lo = (4 + k) * hp + i * ts
                b[lo : lo + ts] = sh[k, PAD + 1 + i * ts : PAD + 1 + (i + 1) * ts].astype(BF16)

    for k in range(2):
        for i in range(3):
            lo = k * hp + i * ts
            act, slope = gelu_both((xf[lo : lo + ts] - mu1) * rstd1 * g1 + b1)
            d1[lo : lo + ts] = slope
            b[2 * hp + lo : 2 * hp + lo + ts] = act.astype(BF16)
            sh[k, PAD + i * ts : PAD + (i + 1) * ts] = act
    lead, _ = gelu_both((hx_r[0] - mu1) * rstd1 * g1 + b1)
    trail, _ = gelu_both((hx_r[1] - mu1) * rstd1 * g1 + b1)
    lead, trail = lead * has_before, trail * has_after
    for k in range(2):
        sh[k, PAD - 1 : PAD] = lead[k : k + 1]
        sh[k, PAD + hp : PAD + hp + 1] = trail[k : k + 1]
    windows()
    weights_end()

    slots = [slot_ref[k] for k in range(NMAT)]

    def cols(n):
        return pl.ds(pl.multiple_of(n * TILE, TILE), TILE)

    def over_tiles(fn):
        def body(n, carry):
            fn(cols(n))
            return carry

        lax.fori_loop(0, nt, body, 0)

    def conv_tile(n):
        acc = mm(b[0:pos, :], w[slots[0], :, n])
        for t in range(1, 5):
            acc += mm(b[t * hp : t * hp + pos, :], w[slots[t], :, n])
        acc += sp_ref[2:3, n]
        h[:, n] = acc
        ar_val[1, 0:1, n] = colsum(acc)
        ar_val[1, 1:2, n] = colsum(acc * acc)

    ar_val[1] = jnp.zeros_like(ar_val[1])
    over_tiles(conv_tile)
    ar_begin(1)
    for i in range(nt):
        a1t[i * TILE : (i + 1) * TILE, :] = b[2 * hp : 4 * hp, i * TILE : (i + 1) * TILE].T
    ar_mid(1)
    sums = ar_end(1)
    mu2 = sums[0:1] * inv_n
    rstd2 = lax.rsqrt(sums[1:2] * inv_n - mu2 * mu2 + NORM_EPS)
    for k in range(2):
        for i in range(3):
            lo = k * hp + i * ts
            act, slope = gelu_both((h[lo : lo + ts] - mu2) * rstd2 * g2 + b2)
            d2[lo : lo + ts] = slope
            a2[lo : lo + ts] = act.astype(BF16)

    ar_val[2] = jnp.zeros_like(ar_val[2])
    par[...] = jnp.concatenate([mu2, rstd2, zero_row, zero_row], axis=0)

    def mix_tile(n):
        v = h[:, n] + mm(a2[...], w[slots[5], :, n]) + sp_ref[5:6, n]
        r[:, n] = v
        rd[:, n] = (v[:hp] - v[hp:]).astype(BF16)

    over_tiles(mix_tile)

    def pool_tile(n):
        diff = mm(rd[...], w[slots[6], :, n])
        t = 0.5 * jnp.tanh(0.5 * diff)
        p0, p1 = 0.5 + t, 0.5 - t
        r0, r1 = r[0:hp, n], r[hp:pos, n]
        dy = dy_ref[:, n].astype(F32)
        pooled_ref[:, n] = (p0 * r0 + p1 * r1).astype(BF16)
        dl[:, n] = (p0 * p1 * dy * (r0 - r1)).astype(BF16)
        mst[0, 0:hp, n] = p0 * dy
        mst[0, hp:pos, n] = p1 * dy

    over_tiles(pool_tile)

    def resid_tile(n):
        v = mm_t(dl[...], w[slots[6], n, :])
        v0 = mst[0, 0:hp, n] + v
        v1 = mst[0, hp:pos, n] - v
        mst[0, 0:hp, n] = v0
        mst[0, hp:pos, n] = v1
        dz[0:hp, n] = v0.astype(BF16)
        dz[hp:pos, n] = v1.astype(BF16)
        ar_val[2, 2:3, n] = colsum(v0) + colsum(v1)

    over_tiles(resid_tile)

    def branch_tile(n):
        v = mm_t(dz[...], w[slots[5], n, :]) * d2[:, n]
        mst[1, :, n] = v
        xhat = (h[:, n] - par[0:1, n]) * par[1:2, n]
        ar_val[2, 0:1, n] = colsum(v)
        ar_val[2, 1:2, n] = colsum(v * xhat)

    over_tiles(branch_tile)
    ar_begin(2)
    hd_s[0] = jnp.concatenate(
        [v for ref in (mst.at[0], mst.at[1], h) for v in (ref[0:1], ref[hp : hp + 1])]
        + [zero_row, zero_row],
        axis=0,
    )
    hd_s[1] = jnp.concatenate(
        [v for ref in (mst.at[0], mst.at[1], h) for v in (ref[hp - 1 : hp], ref[pos - 1 : pos])]
        + [zero_row, zero_row],
        axis=0,
    )
    hd = [
        remote(hd_s.at[0], hd_r.at[1], h_s.at[2], h_r.at[2], to_before),
        remote(hd_s.at[1], hd_r.at[0], h_s.at[3], h_r.at[3], to_after),
    ]
    for cp in hd:
        cp.start()

    half = ch // 2

    def put_gradient(p, lhs, rhs):
        for dst, core in ((snd, 1 - c), (own, c)):
            left = lhs(pl.ds(pl.multiple_of(core * half, half), half))

            def tile(n, dst=dst, left=left):
                v = mm(left(), rhs(n)).astype(BF16)
                for i in range(NX * NY):
                    dst[p, i // NY, i % NY, :, n] = v[i * rb : (i + 1) * rb]

            over_tiles(tile)
            if dst is snd:
                core_copy(p).start()

    def core_copy(p):
        return remote(snd.at[p], rcv.at[p], c_s.at[p], c_r.at[p], sib)

    def x_first(p):
        return p % 2 == 0

    def first_copy(p, k):
        if x_first(p):
            to = lax.rem(x + 1 + k, NX)
            return remote(
                own.at[p, to], fst.at[p, NX - 2 - k], f_s.at[p, k], f_r.at[p, NX - 2 - k], dev(z, y, to, c)
            )
        to = lax.rem(y + 1 + k, NY)
        return remote(
            own.at[p, :, to], fst.at[p, NY - 2 - k], f_s.at[p, k], f_r.at[p, NY - 2 - k], dev(z, to, x, c)
        )

    def second_copy(p, k):
        if x_first(p):
            to = lax.rem(y + 1 + k, NY)
            return remote(
                own.at[p, x, to], sec.at[p, NY - 2 - k], s_s.at[p, k], s_r.at[p, NY - 2 - k], dev(z, to, x, c)
            )
        to = lax.rem(x + 1 + k, NX)
        return remote(
            own.at[p, to, y], sec.at[p, NX - 2 - k], s_s.at[p, k], s_r.at[p, NX - 2 - k], dev(z, y, to, c)
        )

    def wait_all(copy, p, n):
        for k in range(n - 1):
            copy(p, k).wait_send()
        for k in range(n - 1):
            copy(p, k).wait_recv()

    def step_first(p):
        core_copy(p).wait()
        for i in range(NX):
            for j in range(NY):
                own[p, i, j] = (own[p, i, j].astype(F32) + rcv[p, i, j].astype(F32)).astype(BF16)
        for k in range((NX if x_first(p) else NY) - 1):
            first_copy(p, k).start()

    def step_second(p):
        n, m = (NX, NY) if x_first(p) else (NY, NX)
        wait_all(first_copy, p, n)
        for j in range(m):
            at = (p, x, j) if x_first(p) else (p, j, y)
            v = own[at].astype(F32)
            for k in range(n - 1):
                v += fst[p, k, j].astype(F32)
            own[at] = v.astype(BF16)
        for k in range(m - 1):
            second_copy(p, k).start()

    root = (NZ - 1) // 2
    up, down = dev(lax.rem(z + 1, NZ), y, x, c), dev(lax.rem(z + NZ - 1, NZ), y, x, c)

    def z_copy(p, side):
        return remote(
            zs.at[p], zr.at[p, side], z_s.at[p], z_r.at[p, side], up if side == 0 else down
        )

    def bc_copy(p, side):
        return remote(
            res.at[p], res.at[p], zb_s.at[p, side], zb_r.at[p], down if side == 0 else up
        )

    def step_sum(p):
        m = NY if x_first(p) else NX
        wait_all(second_copy, p, m)
        v = own[p, x, y].astype(F32)
        for k in range(m - 1):
            v += sec[p, k].astype(F32)
        zs[p] = v.astype(BF16)
        if root > 0:

            @pl.when(z == 0)
            def _():
                z_copy(p, 0).start()

        if root < NZ - 1:

            @pl.when(z == NZ - 1)
            def _():
                z_copy(p, 1).start()

    def step_pass(p):
        for side, inner in ((0, jnp.logical_and(z > 0, z < root)), (1, jnp.logical_and(z > root, z < NZ - 1))):

            @pl.when(inner)
            def _(side=side):
                z_copy(p, side).wait_recv()
                zs[p] = (zs[p].astype(F32) + zr[p, side].astype(F32)).astype(BF16)
                z_copy(p, side).start()

    def step_root(p):
        @pl.when(z == root)
        def _():
            v = zs[p].astype(F32)
            if root > 0:
                z_copy(p, 0).wait_recv()
                v += zr[p, 0].astype(F32)
            if root < NZ - 1:
                z_copy(p, 1).wait_recv()
                v += zr[p, 1].astype(F32)
            res[p] = v.astype(BF16)
            if root > 0:
                bc_copy(p, 0).start()
            if root < NZ - 1:
                bc_copy(p, 1).start()

    def step_spread(p):
        @pl.when(z != root)
        def _():
            bc_copy(p, 0).wait_recv()

        for side, inner in ((0, jnp.logical_and(z > 0, z < root)), (1, jnp.logical_and(z > root, z < NZ - 1))):

            @pl.when(inner)
            def _(side=side):
                bc_copy(p, side).start()

    def step_done(p):
        @pl.when(z != root)
        def _():
            z_copy(p, 0).wait_send()

        for side, sent in ((0, jnp.logical_and(z > 0, z <= root)), (1, jnp.logical_and(z >= root, z < NZ - 1))):

            @pl.when(sent)
            def _(side=side):
                bc_copy(p, side).wait_send()

    for i in range(nt):
        rdt[i * TILE : (i + 1) * TILE, :] = rd[:, i * TILE : (i + 1) * TILE].T
    ar_mid(2)
    put_gradient(0, lambda rows: lambda: rdt[rows, :], lambda n: dl[:, n])
    for i in range(nt):
        b[i * TILE : (i + 1) * TILE, :] = a2[:, i * TILE : (i + 1) * TILE].T
    sums = ar_end(2)
    s2, q2, e2 = sums[0:1], sums[1:2], sums[2:3]
    put_gradient(1, lambda rows: lambda: b[rows, :], lambda n: dz[:, n])
    step_first(0)

    scale2 = rstd2 * g2

    def dh_of(dr, dn, hid):
        xhat = (hid - mu2) * rstd2
        return dr + scale2 * (dn - s2 * inv_n - xhat * (q2 * inv_n))

    e1_local = jnp.zeros((1, ch), F32)
    for k in range(2):
        for i in range(3):
            lo = k * hp + i * ts
            v = dh_of(mst[0, lo : lo + ts], mst[1, lo : lo + ts], h[lo : lo + ts])
            e1_local += colsum(v)
            sh[k, PAD + i * ts : PAD + (i + 1) * ts] = v
            b[2 * hp + lo : 2 * hp + lo + ts] = v.astype(BF16)
    for cp in hd:
        cp.wait()
    lead = dh_of(hd_r[0, 0:2], hd_r[0, 2:4], hd_r[0, 4:6]) * has_before
    trail = dh_of(hd_r[1, 0:2], hd_r[1, 2:4], hd_r[1, 4:6]) * has_after
    for k in range(2):
        sh[k, PAD - 1 : PAD] = lead[k : k + 1]
        sh[k, PAD + hp : PAD + hp + 1] = trail[k : k + 1]
    windows()
    step_first(1)

    def tap(t):
        lo = (4 - t) * hp
        put_gradient(2 + t, lambda rows: lambda: a1t[rows, :], lambda n: b[lo : lo + pos, n])

    tap(0)
    step_second(0)
    tap(1)
    step_first(2)
    step_second(1)
    tap(2)
    step_first(3)
    step_sum(0)
    tap(3)
    step_first(4)
    step_sum(1)
    step_pass(0)
    tap(4)
    step_first(5)
    step_second(2)
    step_root(0)
    step_pass(1)

    ar_val[3] = jnp.zeros_like(ar_val[3])
    ar_val[3, 2:3] = e1_local
    par[...] = jnp.concatenate([mu1, rstd1, zero_row, zero_row], axis=0)

    def input_tile(n):
        acc = mm_t(b[4 * hp : 4 * hp + pos, :], w[slots[0], n, :])
        for t in range(1, 5):
            lo = (4 - t) * hp
            acc += mm_t(b[lo : lo + pos, :], w[slots[t], n, :])
        v = acc * d1[:, n]
        mst[1, :, n] = v
        xhat = (xf[:, n] - par[0:1, n]) * par[1:2, n]
        ar_val[3, 0:1, n] = colsum(v)
        ar_val[3, 1:2, n] = colsum(v * xhat)

    over_tiles(input_tile)
    ar_begin(3)
    step_first(6)
    step_second(3)
    ar_mid(3)
    step_spread(0)
    step_root(1)
    step_sum(2)
    step_second(4)
    sums = ar_end(3)
    s1, q1, e1 = sums[0:1], sums[1:2], sums[2:3]
    gs_ref[...] = jnp.concatenate([q1, s1, e1, q2, s2, e2], axis=0)
    scale1 = rstd1 * g1
    for i in range(3):
        for k in range(2):
            lo = k * hp + i * ts
            xhat = (xf[lo : lo + ts] - mu1) * rstd1
            v = scale1 * (mst[1, lo : lo + ts] - s1 * inv_n - xhat * (q1 * inv_n))
            for j in range(ch // 128):
                il[j, pl.ds(k, ts, stride=2), :] = v[:, j * 128 : (j + 1) * 128]
        for j in range(ch // 128):
            ig_ref[2 * i * ts : 2 * (i + 1) * ts, j * 128 : (j + 1) * 128] = il[j].astype(BF16)

    step_pass(2)
    step_sum(3)
    step_second(5)
    step_spread(1)
    step_root(2)
    step_pass(3)
    step_sum(4)
    step_second(6)
    step_spread(2)
    step_root(3)
    step_pass(4)
    step_sum(5)
    step_spread(3)
    step_root(4)
    step_pass(5)
    step_sum(6)
    step_spread(4)
    step_root(5)
    step_pass(6)
    step_root(6)
    step_spread(5)
    step_spread(6)

    plane = NX * NY * 2
    mine = (x * NY + y) * 2 + c
    for s in range(own_n * cap):
        at = jnp.int32(0)
        for p in range(NMAT):
            at = jnp.maximum(at, jnp.where(slots[ORDER[p]] == s, p, 0))
        stage[s] = res[at]

    def plane_of(k):
        p = lax.rem(mine + 1 + k, plane)
        return p, p // (2 * NY), lax.rem(p // 2, NY), lax.rem(p, 2)

    def gather_send(k):
        _, px, py, pc = plane_of(k)
        src = stage.at[pl.ds((px * 2 + pc) * cap, cap)]
        return remote(src, g_ref.at[:, c, x, y], g_s.at[k], g_r.at[plane - 2 - k], dev(z, py, px, pc))

    def gather_recv(k):
        _, px, py, pc = plane_of(k)
        src = stage.at[pl.ds((px * 2 + pc) * cap, cap)]
        return remote(src, g_ref.at[:, pc, px, py], g_s.at[k], g_r.at[k], dev(z, py, px, pc))

    def square_copy(k):
        _, px, py, pc = plane_of(k)
        ref = sq_all.at[mine]
        return remote(ref, ref, q_s.at[0], q_r.at[0], dev(z, py, px, pc))

    for k in range(plane - 1):
        gather_send(k).start()
    keep = pltpu.make_async_copy(
        stage.at[pl.ds(o_ix * cap, cap)], g_ref.at[:, c, x, y], g_l.at[0]
    )
    keep.start()
    sq = jnp.zeros((8, ch), F32)
    for p in range(NMAT):
        v = res[p].astype(F32)
        v = v * v
        for i in range(rb // 8):
            sq += v[i * 8 : (i + 1) * 8]
    sq_all[mine] = sq
    for k in range(plane - 1):
        square_copy(k).start()
    for p in range(NMAT):
        step_done(p)
    wait_bytes(sq_all.at[pl.ds(0, plane - 1)], q_r.at[0])
    wait_bytes(sq_all.at[pl.ds(0, plane - 1)], q_s.at[0])
    ssq_ref[...] = jnp.sum(sq_all[...], axis=0)
    for k in range(plane - 1):
        gather_send(k).wait_send()
    for k in range(plane - 1):
        gather_recv(k).wait_recv()
    keep.wait()


def adam_moments(grads, first_old, second_old):
    first_new = BETA_ONE * first_old + (1.0 - BETA_ONE) * grads
    second_new = BETA_TWO * second_old + (1.0 - BETA_TWO) * grads * grads
    direction = (
        first_new
        / (1.0 - BETA_ONE**STEP)
        / (jnp.sqrt(second_new / (1.0 - BETA_TWO**STEP)) + ADAM_EPS)
    )
    return (first_new, second_new, direction)


def per_device(
    inputs,
    cotangent,
    small_params,
    small_first,
    small_second,
    slot_of_matrix,
    master,
    first_moment,
    second_moment,
    left_basis,
    right_basis,
):
    pos, ch = inputs.shape
    seq_n, own_n = lax.axis_size("seq"), lax.axis_size("own")
    nx = own_n // 2
    ny = nx
    nz = seq_n // ny
    cap = master.shape[0]
    hp = pos // 2
    slots = cap * own_n
    chips = seq_n * nx
    rb = ch // 2 // (nx * ny)
    plane = nx * ny * 2
    nn = max(nx, ny)
    dma = pltpu.SemaphoreType.DMA
    vm = pltpu.VMEM
    scratch = [
        vm((slots, ch, ch), BF16),
        vm((max(cap, 2), ch, ch), F32),
        vm((pos, ch), F32),
        vm((2, hp + 16, ch), F32),
        vm((pos, ch), F32),
        vm((pos, ch), F32),
        vm((pos, ch), BF16),
        vm((pos, ch), F32),
        vm((pos, ch), F32),
        vm((hp, ch), BF16),
        vm((hp, ch), BF16),
        vm((pos, ch), BF16),
        vm((6 * hp, ch), BF16),
        vm((ch, pos), BF16),
        vm((ch, hp), BF16),
        vm((NMAT, nx, ny, rb, ch), BF16),
        vm((NMAT, nx, ny, rb, ch), BF16),
        vm((NMAT, nx, ny, rb, ch), BF16),
        vm((NMAT, nn - 1, nn, rb, ch), BF16),
        vm((NMAT, nn - 1, rb, ch), BF16),
        vm((NMAT, 2, rb, ch), BF16),
        vm((NMAT, rb, ch), BF16),
        vm((NMAT, rb, ch), BF16),
        vm((slots, rb, ch), BF16),
        vm((4, ch), F32),
        vm((4, 4, ch), F32),
        vm((4, 4, ch), F32),
        vm((4 if chips <= 16 else 2, chips, 4, ch), F32),
        vm((2, 2, ch), F32),
        vm((2, 2, ch), F32),
        vm((2, 8, ch), F32),
        vm((2, 8, ch), F32),
        vm((ch // 128, hp // 3 * 2, 128), F32),
        vm((plane, 8, ch), F32),
        dma((cap + 1,)),
        dma((1,)),
        dma((1,)),
        dma((cap * 4,)),
        dma((cap * 4,)),
        dma((cap * 4,)),
        dma((4,)),
        dma((4,)),
        dma((4,)),
        dma((4,)),
        dma((4,)),
        dma((4,)),
        dma((NMAT,)),
        dma((NMAT,)),
        dma((NMAT, nn - 1)),
        dma((NMAT, nn - 1)),
        dma((NMAT, nn - 1)),
        dma((NMAT, nn - 1)),
        dma((NMAT,)),
        dma((NMAT, 2)),
        dma((NMAT, 2)),
        dma((NMAT,)),
        dma((plane - 1,)),
        dma((plane - 1,)),
        dma((1,)),
        dma((1,)),
        dma((1,)),
    ]
    in_vmem = pl.BlockSpec(memory_space=pltpu.VMEM)
    anywhere = pl.BlockSpec(memory_space=pl.ANY)
    pooled, input_grad, owned, small_grad, squares = pl.pallas_call(
        functools.partial(kernel, (nx, ny, nz, cap, pos * seq_n * own_n)),
        out_shape=(
            jax.ShapeDtypeStruct((hp, ch), BF16),
            jax.ShapeDtypeStruct((pos, ch), BF16),
            jax.ShapeDtypeStruct((cap, 2, nx, ny, rb, ch), BF16),
            jax.ShapeDtypeStruct((6, ch), F32),
            jax.ShapeDtypeStruct((8, ch), F32),
        ),
        in_specs=[pl.BlockSpec(memory_space=pltpu.SMEM), in_vmem, in_vmem, anywhere, anywhere],
        out_specs=(in_vmem, in_vmem, anywhere, in_vmem, in_vmem),
        scratch_shapes=scratch,
        compiler_params=pltpu.CompilerParams(
            collective_id=0, has_side_effects=True, vmem_limit_bytes=63 * 2**20
        ),
    )(slot_of_matrix, small_params, cotangent, inputs, master)
    owned = owned.reshape(cap, ch, ch)
    grad_norm = jnp.sqrt(jnp.sum(squares) + jnp.sum(small_grad * small_grad))
    factor = jnp.minimum(1.0, CLIP_RATIO * ch * math.sqrt(NMAT) / (grad_norm + 1e-06))
    turned = jnp.einsum(
        "kji,kjl->kil", left_basis.astype(BF16), owned, preferred_element_type=F32
    )
    turned = factor * jnp.einsum(
        "kil,klm->kim", turned.astype(BF16), right_basis.astype(BF16), preferred_element_type=F32
    )
    first_new, second_new, direction = adam_moments(turned, first_moment, second_moment)
    back_turn = jnp.einsum(
        "kij,kjl->kil", left_basis.astype(BF16), direction.astype(BF16), preferred_element_type=F32
    )
    back_turn = jnp.einsum(
        "kil,kml->kim", back_turn.astype(BF16), right_basis.astype(BF16), preferred_element_type=F32
    )
    master_new = master - LEARN_RATE * (back_turn + DECAY_RATE * master)
    slot_ids = lax.axis_index("own") * cap + jnp.arange(cap, dtype=jnp.int32)
    is_used = jnp.any(slot_ids[:, None] == slot_of_matrix[None, :], axis=1)[:, None, None]
    new_master = jnp.where(is_used, master_new, master)
    new_first = jnp.where(is_used, first_new, first_moment)
    new_second = jnp.where(is_used, second_new, second_moment)
    small_first_new, small_second_new, small_dir = adam_moments(
        small_grad * factor, small_first, small_second
    )
    new_small = small_params - SMALL_RATE * (small_dir + DECAY_RATE * small_params)
    return (
        pooled,
        input_grad,
        grad_norm,
        new_master,
        new_first,
        new_second,
        new_small,
        small_first_new,
        small_second_new,
    )


def solution(mesh):
    rows, owned, same = P(("seq", "own"), None), P("own", None, None), P()
    return jax.shard_map(
        per_device,
        mesh=mesh,
        in_specs=(rows, rows, same, same, same, same, owned, owned, owned, owned, owned),
        out_specs=(rows, rows, same, owned, owned, owned, same, same, same),
        check_vma=False,
    )
```

```python
import functools
import math

import jax
import jax.numpy as jnp
from jax import lax
from jax.experimental import pallas as pl
from jax.experimental.pallas import tpu as pltpu
from jax.sharding import PartitionSpec as P

NMAT = 7
STEP = 10
NORM_EPS = 1e-05
BETA_ONE = 0.9
BETA_TWO = 0.999
ADAM_EPS = 1e-08
DECAY_RATE = 0.01
LEARN_RATE = 0.02
SMALL_RATE = 0.1
CLIP_RATIO = 0.5
MESH = pl.DeviceIdType.MESH
F32 = jnp.float32
BF16 = jnp.bfloat16

ORDER = (6, 5, 0, 1, 2, 3, 4)
TILE = 256


def mm(a, b):
    return lax.dot_general(a, b, (((1,), (0,)), ((), ())), preferred_element_type=F32)


def mm_t(a, b):
    return lax.dot_general(a, b, (((1,), (1,)), ((), ())), preferred_element_type=F32)


def gelu_both(v):
    k = math.sqrt(2.0 / math.pi)
    sq = v * v
    t = jnp.tanh(v * (k + (k * 0.044715) * sq))
    half = 0.5 + 0.5 * t
    slope = half + (0.5 * v) * (1.0 - t * t) * (k + (3.0 * k * 0.044715) * sq)
    return v * half, slope


def colsum(v):
    return jnp.sum(v, axis=0, keepdims=True)


def kernel(
    dims,
    slot_ref,
    sp_ref,
    dy_ref,
    x_hbm,
    master_hbm,
    pooled_ref,
    ig_ref,
    g_ref,
    gs_ref,
    ssq_ref,
    w,
    mst,
    xf,
    sh,
    d1,
    h,
    a2,
    d2,
    r,
    rd,
    dl,
    dz,
    b,
    a1t,
    rdt,
    snd,
    own,
    rcv,
    fst,
    sec,
    zr,
    zs,
    res,
    stage,
    par,
    ar_val,
    ar_core,
    ar_chip,
    hx_s,
    hx_r,
    hd_s,
    hd_r,
    il,
    sq_all,
    ld_sem,
    w_send,
    w_sib,
    w_xs,
    w_x,
    w_y,
    w_z,
    ar_s,
    ar_r,
    ar_s2,
    ar_r2,
    h_s,
    h_r,
    c_s,
    c_r,
    f_s,
    f_r,
    s_s,
    s_r,
    z_s,
    z_r,
    zb_s,
    zb_r,
    g_s,
    g_r,
    q_s,
    q_r,
    g_l,
):
    NX, NY, NZ, cap, rows_total = dims
    pos, ch = dz.shape
    hp = pos // 2
    seq_n, own_n = NZ * NY, NX * 2
    n_dev = seq_n * own_n
    chips = n_dev // 2
    rb = ch // 2 // (NX * NY)
    nt = ch // TILE
    s_ix, o_ix = lax.axis_index("seq"), lax.axis_index("own")
    z, y = s_ix // NY, lax.rem(s_ix, NY)
    x, c = o_ix // 2, lax.rem(o_ix, 2)
    me = s_ix * own_n + o_ix
    inv_n = 1.0 / rows_total

    def dev(z_, y_, x_, c_):
        return (z_ * NY + y_, x_ * 2 + c_)

    def remote(src, dst, ss, rs, to):
        return pltpu.make_async_remote_copy(
            src_ref=src, dst_ref=dst, send_sem=ss, recv_sem=rs, device_id=to, device_id_type=MESH
        )

    def wait_bytes(ref, sem):
        pltpu.make_async_copy(ref, ref, sem).wait()

    sib = dev(z, y, x, 1 - c)

    for j in range(cap):
        pltpu.make_async_copy(master_hbm.at[j], mst.at[j], ld_sem.at[j]).start()
    pltpu.make_async_copy(x_hbm, dz, ld_sem.at[cap]).start()

    barrier = pltpu.get_barrier_semaphore()

    def greet(i, carry):
        p = lax.rem(me + 1 + i, n_dev)
        pl.semaphore_signal(
            barrier, inc=1, device_id=(p // own_n, lax.rem(p, own_n)), device_id_type=MESH
        )
        return carry

    lax.fori_loop(0, n_dev - 1, greet, 0)

    for j in range(cap):
        pltpu.make_async_copy(master_hbm.at[j], mst.at[j], ld_sem.at[j]).wait()
        w[o_ix * cap + j] = mst[j].astype(BF16)
    pl.semaphore_wait(barrier, n_dev - 1)

    thirds = (NX, NY, NZ) == (2, 2, 4)
    QR = 64
    third = ch // 3
    nq = third // QR
    w_base = o_ix * cap
    if thirds:
        is_end = jnp.logical_or(z == 0, z == NZ - 1)
        zp = z + 1 - 2 * lax.rem(z, 2)
        ox = (1 - x) * 2 + c
        to_x, to_y, to_z = dev(z, y, 1 - x, c), dev(z, 1 - y, x, c), dev(zp, y, x, c)
        alpha = jnp.where(is_end, y, 2)
        z_part = jnp.where(is_end, 2, y)

        def piece(slot, part, q):
            return w.at[slot, pl.ds(pl.multiple_of(part * third + q * QR, QR), QR)]

        WINDOW = 2

        def x_copy(i):
            ref = piece(w_base + i // nq, alpha, i % nq)
            return remote(ref, ref, w_xs.at[i], w_x.at[i], to_x)

        for i in range(WINDOW):
            x_copy(i).start()
        for j in range(cap):
            ref = w.at[w_base + j]
            remote(ref, ref, w_send.at[0], w_sib.at[0], sib).start()

        n_pieces = cap * nq
        LAG_Z, LAG_Y = 2, 4
        n_steps = n_pieces + LAG_Y

        def pass_on(ref, sem, to):
            remote(ref, ref, w_send.at[0], sem, to).start()

        def weights_step(i):
            if i < n_pieces:
                ref = piece(ox * cap + i // nq, alpha, i % nq)
                remote(ref, ref, w_xs.at[i], w_x.at[i], to_x).wait_recv()
                x_copy(i).wait_send()
                if i + WINDOW < n_pieces:
                    x_copy(i + WINDOW).start()
                pass_on(ref, w_z.at[i], to_z)

                @pl.when(is_end)
                def _():
                    pass_on(ref, w_y.at[i], to_y)

                pass_on(ref, w_sib.at[0], sib)
            k = i - LAG_Z
            if 0 <= k < n_pieces:
                ref_z = piece(ox * cap + k // nq, z_part, k % nq)
                remote(ref_z, ref_z, w_send.at[0], w_z.at[k], to_z).wait_recv()

                @pl.when(jnp.logical_not(is_end))
                def _():
                    pass_on(ref_z, w_y.at[k], to_y)

                pass_on(ref_z, w_sib.at[0], sib)
            k = i - LAG_Y
            if 0 <= k < n_pieces:
                ref_y = piece(ox * cap + k // nq, 1 - y, k % nq)
                remote(ref_y, ref_y, w_send.at[0], w_y.at[k], to_y).wait_recv()
                pass_on(ref_y, w_sib.at[0], sib)

        def weights_end():
            wait_bytes(w.at[pl.ds(0, 2 * cap)], w_sib.at[0])
            wait_bytes(w.at[pl.ds(0, 2 * cap)], w_send.at[0])
            wait_bytes(w.at[0, pl.ds(0, 2 * third)], w_send.at[0])
            wait_bytes(w.at[0, pl.ds(0, 2 * third)], w_send.at[0])

    else:

        def send_w(i, carry):
            p = lax.rem(o_ix + 1 + i, own_n)
            ref = w.at[pl.ds(w_base, cap)]
            remote(ref, ref, w_send.at[0], w_sib.at[0], (s_ix, p)).start()
            return carry

        lax.fori_loop(0, own_n - 1, send_w, 0)

        n_steps = 0

        def weights_step(i):
            pass

        def weights_end():
            wait_bytes(w.at[pl.ds(0, (own_n - 1) * cap)], w_sib.at[0])
            wait_bytes(w.at[pl.ds(0, (own_n - 1) * cap)], w_send.at[0])

    chip = s_ix * NX + x

    def ar_begin(i):
        remote(ar_val.at[i], ar_core.at[i], ar_s.at[i], ar_r.at[i], sib).start()

    def ar_chip_copy(i, k):
        p = lax.rem(chip + 1 + k, chips)
        ref = ar_chip.at[i % ar_chip.shape[0], chip]
        return remote(
            ref, ref, ar_s2.at[i], ar_r2.at[i], (p // NX, lax.rem(p, NX) * 2 + c)
        )

    def ar_mid(i):
        remote(ar_val.at[i], ar_core.at[i], ar_s.at[i], ar_r.at[i], sib).wait()
        ar_chip[i % ar_chip.shape[0], chip] = ar_val[i] + ar_core[i]

        def body(k, carry):
            ar_chip_copy(i, k).start()
            return carry

        lax.fori_loop(0, chips - 1, body, 0)

    def ar_end(i):
        at = i % ar_chip.shape[0]
        wait_bytes(ar_chip.at[at, pl.ds(0, chips - 1)], ar_r2.at[i])
        wait_bytes(ar_chip.at[at, pl.ds(0, chips - 1)], ar_s2.at[i])
        return jnp.sum(ar_chip[at], axis=0)

    pltpu.make_async_copy(x_hbm, dz, ld_sem.at[cap]).wait()
    ts = hp // 3
    total = jnp.zeros((1, ch), F32)
    square = jnp.zeros((1, ch), F32)
    for i in range(3):
        for j in range(ch // 128):
            il[j] = dz[2 * ts * i : 2 * ts * (i + 1), j * 128 : (j + 1) * 128].astype(F32)
        for k in range(2):
            v = jnp.concatenate([il[j, pl.ds(k, ts, stride=2), :] for j in range(ch // 128)], axis=1)
            xf[k * hp + i * ts : k * hp + (i + 1) * ts] = v
            total += colsum(v)
            square += colsum(v * v)
    zero_row = jnp.zeros((1, ch), F32)
    ar_val[0] = jnp.concatenate([total, square, zero_row, zero_row], axis=0)
    ar_begin(0)
    before, after = lax.rem(me + n_dev - 1, n_dev), lax.rem(me + 1, n_dev)
    to_before = (before // own_n, lax.rem(before, own_n))
    to_after = (after // own_n, lax.rem(after, own_n))
    has_before = jnp.where(me > 0, 1.0, 0.0).astype(F32)
    has_after = jnp.where(me < n_dev - 1, 1.0, 0.0).astype(F32)
    hx_s[0] = jnp.concatenate([xf[0:1], xf[hp : hp + 1]], axis=0)
    hx_s[1] = jnp.concatenate([xf[hp - 1 : hp], xf[pos - 1 : pos]], axis=0)
    hx = [
        remote(hx_s.at[0], hx_r.at[1], h_s.at[0], h_r.at[0], to_before),
        remote(hx_s.at[1], hx_r.at[0], h_s.at[1], h_r.at[1], to_after),
    ]
    for cp in hx:
        cp.start()
    ar_mid(0)
    for i in range(min(2, n_steps)):
        weights_step(i)
    sums = ar_end(0)
    for cp in hx:
        cp.wait()

    mu1 = sums[0:1] * inv_n
    rstd1 = lax.rsqrt(sums[1:2] * inv_n - mu1 * mu1 + NORM_EPS)
    g1, b1, c1 = sp_ref[0:1], sp_ref[1:2], sp_ref[2:3]
    g2, b2, c2 = sp_ref[3:4], sp_ref[4:5], sp_ref[5:6]
    PAD = 8

    def windows():
        for k in range(2):
            for i in range(3):
                b[k * hp + i * ts : k * hp + (i + 1) * ts] = sh[
                    k, PAD - 1 + i * ts : PAD - 1 + (i + 1) * ts
                ].astype(BF16)
                lo = (4 + k) * hp + i * ts
                b[lo : lo + ts] = sh[k, PAD + 1 + i * ts : PAD + 1 + (i + 1) * ts].astype(BF16)

    for k in range(2):
        for i in range(3):
            lo = k * hp + i * ts
            act, slope = gelu_both((xf[lo : lo + ts] - mu1) * rstd1 * g1 + b1)
            d1[lo : lo + ts] = slope
            b[2 * hp + lo : 2 * hp + lo + ts] = act.astype(BF16)
            sh[k, PAD + i * ts : PAD + (i + 1) * ts] = act
            if 2 + 3 * k + i < n_steps:
                weights_step(2 + 3 * k + i)
    lead, _ = gelu_both((hx_r[0] - mu1) * rstd1 * g1 + b1)
    trail, _ = gelu_both((hx_r[1] - mu1) * rstd1 * g1 + b1)
    lead, trail = lead * has_before, trail * has_after
    for k in range(2):
        sh[k, PAD - 1 : PAD] = lead[k : k + 1]
        sh[k, PAD + hp : PAD + hp + 1] = trail[k : k + 1]
    windows()
    for i in range(8, n_steps):
        weights_step(i)
    weights_end()

    slots = [slot_ref[k] for k in range(NMAT)]

    def cols(n):
        return pl.ds(pl.multiple_of(n * TILE, TILE), TILE)

    def over_tiles(fn):
        def body(n, carry):
            fn(cols(n))
            return carry

        lax.fori_loop(0, nt, body, 0)

    def conv_tile(n):
        acc = mm(b[0:pos, :], w[slots[0], :, n])
        for t in range(1, 5):
            acc += mm(b[t * hp : t * hp + pos, :], w[slots[t], :, n])
        acc += sp_ref[2:3, n]
        h[:, n] = acc
        ar_val[1, 0:1, n] = colsum(acc)
        ar_val[1, 1:2, n] = colsum(acc * acc)

    ar_val[1] = jnp.zeros_like(ar_val[1])
    over_tiles(conv_tile)
    ar_begin(1)
    for i in range(nt):
        a1t[i * TILE : (i + 1) * TILE, :] = b[2 * hp : 4 * hp, i * TILE : (i + 1) * TILE].T
    ar_mid(1)
    sums = ar_end(1)
    mu2 = sums[0:1] * inv_n
    rstd2 = lax.rsqrt(sums[1:2] * inv_n - mu2 * mu2 + NORM_EPS)
    for k in range(2):
        for i in range(3):
            lo = k * hp + i * ts
            act, slope = gelu_both((h[lo : lo + ts] - mu2) * rstd2 * g2 + b2)
            d2[lo : lo + ts] = slope
            a2[lo : lo + ts] = act.astype(BF16)

    half = ch // 2
    halves = own.shape[1]
    rh = rb // halves

    def put_gradient(p, lhs, rhs):
        def tile(n):
            v = mm(lhs[...], rhs(n))
            keep = jnp.where(c == 0, v[:half], v[half:]).astype(BF16)
            give = jnp.where(c == 0, v[half:], v[:half]).astype(BF16)
            for i in range(NX * NY):
                for k in range(halves):
                    at = (i * halves + k) * rh
                    own[p, k, i // NY, i % NY, :, n] = keep[at : at + rh]
                    snd[p, k, i // NY, i % NY, :, n] = give[at : at + rh]

        over_tiles(tile)
        core_copy(p).start()

    def core_copy(p):
        return remote(snd.at[p], rcv.at[p], c_s.at[p], c_r.at[p], sib)

    def first_copies(p):
        made = []
        for k in range(NX - 1):
            to = lax.rem(x + 1 + k, NX)
            at = NX - 2 - k
            made.append(remote(own.at[p, 0, to], fst.at[p, 0, at], f_s.at[p, 0, k], f_r.at[p, 0, at], dev(z, y, to, c)))
        for k in range(NY - 1 if halves > 1 else 0):
            to = lax.rem(y + 1 + k, NY)
            at = NY - 2 - k
            made.append(remote(own.at[p, 1, :, to], fst.at[p, 1, at], f_s.at[p, 1, k], f_r.at[p, 1, at], dev(z, to, x, c)))
        return made

    def second_copies(p):
        made = []
        for k in range(NY - 1):
            to = lax.rem(y + 1 + k, NY)
            at = NY - 2 - k
            made.append(remote(own.at[p, 0, x, to], sec.at[p, 0, at], s_s.at[p, 0, k], s_r.at[p, 0, at], dev(z, to, x, c)))
        for k in range(NX - 1 if halves > 1 else 0):
            to = lax.rem(x + 1 + k, NX)
            at = NX - 2 - k
            made.append(remote(own.at[p, 1, to, y], sec.at[p, 1, at], s_s.at[p, 1, k], s_r.at[p, 1, at], dev(z, y, to, c)))
        return made

    def wait_all(copies):
        for cp in copies:
            cp.wait_send()
        for cp in copies:
            cp.wait_recv()

    def step_first(p):
        core_copy(p).wait()
        for k in range(halves):
            for i in range(NX):
                for j in range(NY):
                    own[p, k, i, j] = (own[p, k, i, j].astype(F32) + rcv[p, k, i, j].astype(F32)).astype(BF16)
        for cp in first_copies(p):
            cp.start()

    def step_second(p):
        wait_all(first_copies(p))
        for k in range(halves):
            n, m = (NX, NY) if k == 0 else (NY, NX)
            for j in range(m):
                at = (p, 0, x, j) if k == 0 else (p, 1, j, y)
                v = own[at].astype(F32)
                for i in range(n - 1):
                    v += fst[p, k, i, j].astype(F32)
                own[at] = v.astype(BF16)
        for cp in second_copies(p):
            cp.start()

    chain = NZ == 4 and halves == 2
    is_outer = jnp.logical_or(z == 0, z == NZ - 1)
    is_inner = jnp.logical_not(is_outer)
    inner = jnp.where(z < 2, 1, 2)
    my_half = jnp.clip(z - 1, 0, 1)

    def end_copy(p):
        return remote(zs.at[p], zr.at[p, 0], z_s.at[p, 0], z_r.at[p, 0], dev(inner, y, x, c))

    def swap_copy(p, k):
        return remote(zs.at[p, k], zr.at[p, 1, k], z_s.at[p, 1], z_r.at[p, 1], dev(lax.rem(3 - z + NZ, NZ), y, x, c))

    def spread_copy(p, k, i):
        return remote(res.at[p, k], res.at[p, k], zb_s.at[p, i], zb_r.at[p, k], dev(lax.rem(z + 1 + i, NZ), y, x, c))

    def gather_copy(p, at):
        return remote(zs.at[p], zr.at[p, at], z_s.at[p, 0], z_r.at[p, at], dev(0, y, x, c))

    def whole_copy(p, i):
        return remote(res.at[p], res.at[p], zb_s.at[p, i], zb_r.at[p, 0], dev(lax.rem(z + 1 + i, NZ), y, x, c))

    def step_sum(p):
        wait_all(second_copies(p))
        for k in range(halves):
            v = own[p, k, x, y].astype(F32)
            for i in range((NY if k == 0 else NX) - 1):
                v += sec[p, k, i].astype(F32)
            zs[p, k] = v.astype(BF16)
        if chain:

            @pl.when(is_outer)
            def _():
                end_copy(p).start()

        else:

            @pl.when(z > 0)
            def _():
                gather_copy(p, z - 1).start()

    def step_pass(p):
        if chain:

            @pl.when(is_inner)
            def _():
                end_copy(p).wait_recv()
                zs[p] = (zs[p].astype(F32) + zr[p, 0].astype(F32)).astype(BF16)
                swap_copy(p, 1 - my_half).start()

    def step_root(p):
        if chain:

            @pl.when(is_inner)
            def _():
                swap_copy(p, my_half).wait_recv()
                res[p, my_half] = (zs[p, my_half].astype(F32) + zr[p, 1, my_half].astype(F32)).astype(BF16)
                for i in range(NZ - 1):
                    spread_copy(p, my_half, i).start()

        else:

            @pl.when(z == 0)
            def _():
                v = zs[p].astype(F32)
                for i in range(NZ - 1):
                    gather_copy(p, i).wait_recv()
                    v += zr[p, i].astype(F32)
                res[p] = v.astype(BF16)
                for i in range(NZ - 1):
                    whole_copy(p, i).start()

    def step_spread(p):
        if chain:

            @pl.when(is_outer)
            def _():
                for k in range(2):
                    spread_copy(p, k, 0).wait_recv()

            @pl.when(is_inner)
            def _():
                spread_copy(p, 1 - my_half, 0).wait_recv()

        else:

            @pl.when(z > 0)
            def _():
                whole_copy(p, 0).wait_recv()

    def step_done(p):
        if chain:

            @pl.when(is_outer)
            def _():
                end_copy(p).wait_send()

            @pl.when(is_inner)
            def _():
                swap_copy(p, 1 - my_half).wait_send()
                for i in range(NZ - 1):
                    spread_copy(p, my_half, i).wait_send()

        else:

            @pl.when(z > 0)
            def _():
                gather_copy(p, z - 1).wait_send()

            @pl.when(z == 0)
            def _():
                for i in range(NZ - 1):
                    whole_copy(p, i).wait_send()

    ar_val[2] = jnp.zeros_like(ar_val[2])
    par[...] = jnp.concatenate([mu2, rstd2, zero_row, zero_row], axis=0)

    def mix_tile(n):
        v = h[:, n] + mm(a2[...], w[slots[5], :, n]) + sp_ref[5:6, n]
        r[:, n] = v
        rd[:, n] = (v[:hp] - v[hp:]).astype(BF16)

    over_tiles(mix_tile)
    for i in range(nt):
        rdt[i * TILE : (i + 1) * TILE, :] = rd[:, i * TILE : (i + 1) * TILE].T

    def pool_tile(n):
        diff = mm(rd[...], w[slots[6], :, n])
        t = 0.5 * jnp.tanh(0.5 * diff)
        p0, p1 = 0.5 + t, 0.5 - t
        r0, r1 = r[0:hp, n], r[hp:pos, n]
        dy = dy_ref[:, n].astype(F32)
        pooled_ref[:, n] = (p0 * r0 + p1 * r1).astype(BF16)
        dl[:, n] = (p0 * p1 * dy * (r0 - r1)).astype(BF16)
        mst[0, 0:hp, n] = p0 * dy
        mst[0, hp:pos, n] = p1 * dy

    over_tiles(pool_tile)
    put_gradient(0, rdt, lambda n: dl[:, n])

    def resid_tile(n):
        v = mm_t(dl[...], w[slots[6], n, :])
        v0 = mst[0, 0:hp, n] + v
        v1 = mst[0, hp:pos, n] - v
        mst[0, 0:hp, n] = v0
        mst[0, hp:pos, n] = v1
        dz[0:hp, n] = v0.astype(BF16)
        dz[hp:pos, n] = v1.astype(BF16)
        ar_val[2, 2:3, n] = colsum(v0) + colsum(v1)

    over_tiles(resid_tile)
    step_first(0)

    def branch_tile(n):
        v = mm_t(dz[...], w[slots[5], n, :]) * d2[:, n]
        mst[1, :, n] = v
        xhat = (h[:, n] - par[0:1, n]) * par[1:2, n]
        ar_val[2, 0:1, n] = colsum(v)
        ar_val[2, 1:2, n] = colsum(v * xhat)

    over_tiles(branch_tile)
    ar_begin(2)
    hd_s[0] = jnp.concatenate(
        [v for ref in (mst.at[0], mst.at[1], h) for v in (ref[0:1], ref[hp : hp + 1])]
        + [zero_row, zero_row],
        axis=0,
    )
    hd_s[1] = jnp.concatenate(
        [v for ref in (mst.at[0], mst.at[1], h) for v in (ref[hp - 1 : hp], ref[pos - 1 : pos])]
        + [zero_row, zero_row],
        axis=0,
    )
    hd = [
        remote(hd_s.at[0], hd_r.at[1], h_s.at[2], h_r.at[2], to_before),
        remote(hd_s.at[1], hd_r.at[0], h_s.at[3], h_r.at[3], to_after),
    ]
    for cp in hd:
        cp.start()

    for i in range(nt):
        b[i * TILE : (i + 1) * TILE, :] = a2[:, i * TILE : (i + 1) * TILE].T
    ar_mid(2)
    put_gradient(1, b.at[pl.ds(0, ch)], lambda n: dz[:, n])
    step_second(0)
    sums = ar_end(2)
    s2, q2, e2 = sums[0:1], sums[1:2], sums[2:3]
    step_first(1)

    scale2 = rstd2 * g2

    def dh_of(dr, dn, hid):
        xhat = (hid - mu2) * rstd2
        return dr + scale2 * (dn - s2 * inv_n - xhat * (q2 * inv_n))

    e1_local = jnp.zeros((1, ch), F32)
    for k in range(2):
        for i in range(3):
            lo = k * hp + i * ts
            v = dh_of(mst[0, lo : lo + ts], mst[1, lo : lo + ts], h[lo : lo + ts])
            e1_local += colsum(v)
            sh[k, PAD + i * ts : PAD + (i + 1) * ts] = v
            b[2 * hp + lo : 2 * hp + lo + ts] = v.astype(BF16)
    for cp in hd:
        cp.wait()
    lead = dh_of(hd_r[0, 0:2], hd_r[0, 2:4], hd_r[0, 4:6]) * has_before
    trail = dh_of(hd_r[1, 0:2], hd_r[1, 2:4], hd_r[1, 4:6]) * has_after
    for k in range(2):
        sh[k, PAD - 1 : PAD] = lead[k : k + 1]
        sh[k, PAD + hp : PAD + hp + 1] = trail[k : k + 1]
    windows()

    def tap(t):
        lo = (4 - t) * hp
        put_gradient(2 + t, a1t, lambda n: b[lo : lo + pos, n])

    tap(0)
    step_second(1)
    tap(1)
    step_first(2)
    step_sum(0)
    tap(2)
    step_first(3)
    tap(3)
    tap(4)
    step_pass(0)
    step_sum(1)
    step_second(2)
    step_first(4)

    ar_val[3] = jnp.zeros_like(ar_val[3])
    ar_val[3, 2:3] = e1_local
    par[...] = jnp.concatenate([mu1, rstd1, zero_row, zero_row], axis=0)

    def input_tile(n):
        acc = mm_t(b[4 * hp : 4 * hp + pos, :], w[slots[0], n, :])
        for t in range(1, 5):
            lo = (4 - t) * hp
            acc += mm_t(b[lo : lo + pos, :], w[slots[t], n, :])
        v = acc * d1[:, n]
        mst[1, :, n] = v
        xhat = (xf[:, n] - par[0:1, n]) * par[1:2, n]
        ar_val[3, 0:1, n] = colsum(v)
        ar_val[3, 1:2, n] = colsum(v * xhat)

    input_tile(cols(0))
    step_second(3)
    step_first(5)
    step_root(0)
    step_pass(1)
    for i in range(1, nt - 1):
        input_tile(cols(i))
    step_second(4)
    step_first(6)
    step_sum(2)
    input_tile(cols(nt - 1))
    ar_begin(3)
    step_root(1)
    step_spread(0)
    ar_mid(3)
    step_second(5)
    step_sum(3)
    step_pass(2)
    sums = ar_end(3)
    s1, q1, e1 = sums[0:1], sums[1:2], sums[2:3]
    gs_ref[...] = jnp.concatenate([q1, s1, e1, q2, s2, e2], axis=0)
    scale1 = rstd1 * g1
    for i in range(3):
        for k in range(2):
            lo = k * hp + i * ts
            xhat = (xf[lo : lo + ts] - mu1) * rstd1
            v = scale1 * (mst[1, lo : lo + ts] - s1 * inv_n - xhat * (q1 * inv_n))
            for j in range(ch // 128):
                il[j, pl.ds(k, ts, stride=2), :] = v[:, j * 128 : (j + 1) * 128]
        for j in range(ch // 128):
            ig_ref[2 * i * ts : 2 * (i + 1) * ts, j * 128 : (j + 1) * 128] = il[j].astype(BF16)

    step_second(6)
    step_sum(4)
    step_pass(3)
    step_root(2)
    step_spread(1)
    step_sum(5)
    step_pass(4)
    step_root(3)
    step_spread(2)
    step_sum(6)
    step_pass(5)
    step_root(4)
    step_spread(3)
    step_pass(6)
    step_root(5)
    step_spread(4)
    step_root(6)
    step_spread(5)
    step_spread(6)

    plane = NX * NY * 2
    mine = (x * NY + y) * 2 + c
    for s in range(own_n * cap):
        at = jnp.int32(0)
        for p in range(NMAT):
            at = jnp.maximum(at, jnp.where(slots[ORDER[p]] == s, p, 0))
        stage[s] = res[at]

    def plane_of(k):
        p = lax.rem(mine + 1 + k, plane)
        return p, p // (2 * NY), lax.rem(p // 2, NY), lax.rem(p, 2)

    def gather_send(k):
        _, px, py, pc = plane_of(k)
        src = stage.at[pl.ds((px * 2 + pc) * cap, cap)]
        return remote(src, g_ref.at[:, c, x, y], g_s.at[k], g_r.at[plane - 2 - k], dev(z, py, px, pc))

    def gather_recv(k):
        _, px, py, pc = plane_of(k)
        src = stage.at[pl.ds((px * 2 + pc) * cap, cap)]
        return remote(src, g_ref.at[:, pc, px, py], g_s.at[k], g_r.at[k], dev(z, py, px, pc))

    def square_copy(k):
        _, px, py, pc = plane_of(k)
        ref = sq_all.at[mine]
        return remote(ref, ref, q_s.at[0], q_r.at[0], dev(z, py, px, pc))

    for k in range(plane - 1):
        gather_send(k).start()
    keep = pltpu.make_async_copy(
        stage.at[pl.ds(o_ix * cap, cap)], g_ref.at[:, c, x, y], g_l.at[0]
    )
    keep.start()
    sq = jnp.zeros((8, ch), F32)
    for p in range(NMAT):
        for k in range(halves):
            v = res[p, k].astype(F32)
            v = v * v
            for i in range(rh // 8):
                sq += v[i * 8 : (i + 1) * 8]
    sq_all[mine] = sq
    for k in range(plane - 1):
        square_copy(k).start()
    for p in range(NMAT):
        step_done(p)
    wait_bytes(sq_all.at[pl.ds(0, plane - 1)], q_r.at[0])
    wait_bytes(sq_all.at[pl.ds(0, plane - 1)], q_s.at[0])
    ssq_ref[...] = jnp.sum(sq_all[...], axis=0)
    for k in range(plane - 1):
        gather_send(k).wait_send()
    for k in range(plane - 1):
        gather_recv(k).wait_recv()
    keep.wait()


def adam(grads, first_old, second_old):
    first_new = BETA_ONE * first_old + (1.0 - BETA_ONE) * grads
    second_new = BETA_TWO * second_old + (1.0 - BETA_TWO) * grads * grads
    direction = (first_new * (1.0 / (1.0 - BETA_ONE**STEP))) / (
        jnp.sqrt(second_new * (1.0 / (1.0 - BETA_TWO**STEP))) + ADAM_EPS
    )
    return first_new, second_new, direction


def optimizer_kernel(
    used_ref,
    ssq_ref,
    gs_ref,
    sp_ref,
    sf_ref,
    ss_ref,
    g_hbm,
    left_hbm,
    right_hbm,
    first_hbm,
    second_hbm,
    master_hbm,
    norm_ref,
    nsp_ref,
    nsf_ref,
    nss_ref,
    nmaster_hbm,
    nfirst_hbm,
    nsecond_hbm,
    g,
    left,
    right,
    first,
    second,
    master,
    left_low,
    left_t,
    right_low,
    mid,
    turn,
    in_sem,
    out_sem,
):
    cap, ch, _ = g.shape
    nt = ch // TILE
    sources = (g_hbm, right_hbm, left_hbm, first_hbm, second_hbm, master_hbm)
    places = (g, right, left, first, second, master)

    def load(i, j):
        return pltpu.make_async_copy(sources[i].at[j], places[i].at[j], in_sem.at[i, j])

    def save(i, j):
        src = (first, second, master)[i]
        dst = (nfirst_hbm, nsecond_hbm, nmaster_hbm)[i]
        return pltpu.make_async_copy(src.at[j], dst.at[j], out_sem.at[i, j])

    for j in range(cap):
        for i in range(6):
            load(i, j).start()

    gs = gs_ref[...]
    norm = jnp.sqrt(
        jnp.sum(jnp.sum(ssq_ref[...], axis=0, keepdims=True), axis=1, keepdims=True)
        + jnp.sum(jnp.sum(gs * gs, axis=0, keepdims=True), axis=1, keepdims=True)
    )
    norm_ref[...] = norm
    factor = jnp.minimum(1.0, CLIP_RATIO * ch * math.sqrt(NMAT) / (norm + 1e-06))
    small_first, small_second, small_dir = adam(gs * factor, sf_ref[...], ss_ref[...])
    nsf_ref[...] = small_first
    nss_ref[...] = small_second
    nsp_ref[...] = sp_ref[...] - SMALL_RATE * (small_dir + DECAY_RATE * sp_ref[...])

    def over_tiles(fn):
        def body(n, carry):
            fn(pl.ds(pl.multiple_of(n * TILE, TILE), TILE))
            return carry

        lax.fori_loop(0, nt, body, 0)

    for j in range(cap):
        used = used_ref[j] > 0
        load(0, j).wait()
        load(1, j).wait()
        right_low[...] = right[j].astype(BF16)

        def mid_tile(n):
            mid[:, n] = mm(g[j], right_low[:, n]).astype(BF16)

        over_tiles(mid_tile)
        load(2, j).wait()
        left_low[...] = left[j].astype(BF16)
        for i in range(nt):
            left_t[i * TILE : (i + 1) * TILE, :] = left_low[:, i * TILE : (i + 1) * TILE].T
        load(3, j).wait()
        load(4, j).wait()

        def moment_tile(n):
            grads = factor * mm(left_t[...], mid[:, n])
            f_old, s_old = first[j, :, n], second[j, :, n]
            f_new, s_new, direction = adam(grads, f_old, s_old)
            first[j, :, n] = jnp.where(used, f_new, f_old)
            second[j, :, n] = jnp.where(used, s_new, s_old)
            turn[:, n] = direction.astype(BF16)

        over_tiles(moment_tile)
        save(0, j).start()
        save(1, j).start()

        def back_tile(n):
            mid[:, n] = mm(left_low[...], turn[:, n]).astype(BF16)

        over_tiles(back_tile)
        load(5, j).wait()

        def master_tile(n):
            old = master[j, :, n]
            step = mm_t(mid[...], right_low[n, :]) + DECAY_RATE * old
            master[j, :, n] = jnp.where(used, old - LEARN_RATE * step, old)

        over_tiles(master_tile)
        save(2, j).start()
    for j in range(cap):
        for i in range(3):
            save(i, j).wait()


def optimizer(used, squares, small_grad, small_params, small_first, small_second, owned, left, right, first, second, master):
    cap, ch, _ = master.shape
    vm, dma = pltpu.VMEM, pltpu.SemaphoreType.DMA
    in_vmem = pl.BlockSpec(memory_space=pltpu.VMEM)
    anywhere = pl.BlockSpec(memory_space=pl.ANY)
    big = jax.ShapeDtypeStruct((cap, ch, ch), F32)
    small = jax.ShapeDtypeStruct((6, ch), F32)
    return pl.pallas_call(
        optimizer_kernel,
        out_shape=(jax.ShapeDtypeStruct((1, 1), F32), small, small, small, big, big, big),
        in_specs=[pl.BlockSpec(memory_space=pltpu.SMEM)] + [in_vmem] * 5 + [anywhere] * 6,
        out_specs=(in_vmem,) * 4 + (anywhere,) * 3,
        scratch_shapes=[vm((cap, ch, ch), BF16)]
        + [vm((cap, ch, ch), F32)] * 5
        + [vm((ch, ch), BF16)] * 5
        + [dma((6, cap)), dma((3, cap))],
        compiler_params=pltpu.CompilerParams(vmem_limit_bytes=60 * 2**20),
    )(used, squares, small_grad, small_params, small_first, small_second, owned, left, right, first, second, master)


def block_and_grads(inputs, cotangent, small_params, slot_of_matrix, master):
    pos, ch = inputs.shape
    seq_n, own_n = lax.axis_size("seq"), lax.axis_size("own")
    nx = own_n // 2
    ny = nx
    nz = seq_n // ny
    cap = master.shape[0]
    hp = pos // 2
    slots = cap * own_n
    chips = seq_n * nx
    rb = ch // 2 // (nx * ny)
    plane = nx * ny * 2
    nn = max(nx, ny)
    halves = 2 if rb % 32 == 0 else 1
    rh = rb // halves
    dma = pltpu.SemaphoreType.DMA
    vm = pltpu.VMEM
    scratch = [
        vm((slots, ch, ch), BF16),
        vm((max(cap, 2), ch, ch), F32),
        vm((pos, ch), F32),
        vm((2, hp + 16, ch), F32),
        vm((pos, ch), F32),
        vm((pos, ch), F32),
        vm((pos, ch), BF16),
        vm((pos, ch), F32),
        vm((pos, ch), F32),
        vm((hp, ch), BF16),
        vm((hp, ch), BF16),
        vm((pos, ch), BF16),
        vm((6 * hp, ch), BF16),
        vm((ch, pos), BF16),
        vm((ch, hp), BF16),
        vm((NMAT, halves, nx, ny, rh, ch), BF16),
        vm((NMAT, halves, nx, ny, rh, ch), BF16),
        vm((NMAT, halves, nx, ny, rh, ch), BF16),
        vm((NMAT, halves, nn - 1, nn, rh, ch), BF16),
        vm((NMAT, halves, nn - 1, rh, ch), BF16),
        vm((NMAT, 2 if nz == 4 else nz - 1, halves, rh, ch), BF16),
        vm((NMAT, halves, rh, ch), BF16),
        vm((NMAT, halves, rh, ch), BF16),
        vm((slots, halves, rh, ch), BF16),
        vm((4, ch), F32),
        vm((4, 4, ch), F32),
        vm((4, 4, ch), F32),
        vm((4 if chips <= 16 else 2, chips, 4, ch), F32),
        vm((2, 2, ch), F32),
        vm((2, 2, ch), F32),
        vm((2, 8, ch), F32),
        vm((2, 8, ch), F32),
        vm((ch // 128, hp // 3 * 2, 128), F32),
        vm((plane, 8, ch), F32),
        dma((cap + 1,)),
        dma((1,)),
        dma((1,)),
        dma((cap * 4,)),
        dma((cap * 4,)),
        dma((cap * 4,)),
        dma((cap * 4,)),
        dma((4,)),
        dma((4,)),
        dma((4,)),
        dma((4,)),
        dma((4,)),
        dma((4,)),
        dma((NMAT,)),
        dma((NMAT,)),
        dma((NMAT, halves, nn - 1)),
        dma((NMAT, halves, nn - 1)),
        dma((NMAT, halves, nn - 1)),
        dma((NMAT, halves, nn - 1)),
        dma((NMAT, 2)),
        dma((NMAT, max(2, nz - 1))),
        dma((NMAT, nz - 1)),
        dma((NMAT, 2)),
        dma((plane - 1,)),
        dma((plane - 1,)),
        dma((1,)),
        dma((1,)),
        dma((1,)),
    ]
    in_vmem = pl.BlockSpec(memory_space=pltpu.VMEM)
    anywhere = pl.BlockSpec(memory_space=pl.ANY)
    return pl.pallas_call(
        functools.partial(kernel, (nx, ny, nz, cap, pos * seq_n * own_n)),
        out_shape=(
            jax.ShapeDtypeStruct((hp, ch), BF16),
            jax.ShapeDtypeStruct((pos, ch), BF16),
            jax.ShapeDtypeStruct((cap, 2, nx, ny, halves, rh, ch), BF16),
            jax.ShapeDtypeStruct((6, ch), F32),
            jax.ShapeDtypeStruct((8, ch), F32),
        ),
        in_specs=[pl.BlockSpec(memory_space=pltpu.SMEM), in_vmem, in_vmem, anywhere, anywhere],
        out_specs=(in_vmem, in_vmem, anywhere, in_vmem, in_vmem),
        scratch_shapes=scratch,
        compiler_params=pltpu.CompilerParams(
            collective_id=0, has_side_effects=True, vmem_limit_bytes=63 * 2**20
        ),
    )(slot_of_matrix, small_params, cotangent, inputs, master)


def per_device(
    inputs,
    cotangent,
    small_params,
    small_first,
    small_second,
    slot_of_matrix,
    master,
    first_moment,
    second_moment,
    left_basis,
    right_basis,
):
    cap, ch = master.shape[0], master.shape[2]
    own_n = lax.axis_size("own")
    pooled, input_grad, owned, small_grad, squares = block_and_grads(
        inputs, cotangent, small_params, slot_of_matrix, master
    )
    slot_ids = lax.axis_index("own") * cap + jnp.arange(cap, dtype=jnp.int32)
    used = jnp.any(slot_ids[:, None] == slot_of_matrix[None, :], axis=1).astype(jnp.int32)
    grad_norm, new_small, small_first_new, small_second_new, new_master, new_first, new_second = optimizer(
        used,
        squares,
        small_grad,
        small_params,
        small_first,
        small_second,
        owned.reshape(cap, ch, ch),
        left_basis,
        right_basis,
        first_moment,
        second_moment,
        master,
    )
    return (
        pooled,
        input_grad,
        grad_norm.reshape(()),
        new_master,
        new_first,
        new_second,
        new_small,
        small_first_new,
        small_second_new,
    )


def solution(mesh):
    rows, owned, same = P(("seq", "own"), None), P("own", None, None), P()
    return jax.shard_map(
        per_device,
        mesh=mesh,
        in_specs=(rows, rows, same, same, same, same, owned, owned, owned, owned, owned),
        out_specs=(rows, rows, same, owned, owned, owned, same, same, same),
        check_vma=False,
    )
```

```python
import functools
import math

import jax
import jax.numpy as jnp
from jax import lax
from jax.experimental import pallas as pl
from jax.experimental.pallas import tpu as pltpu
from jax.sharding import PartitionSpec as P

NMAT = 7
STEP = 10
NORM_EPS = 1e-05
BETA_ONE = 0.9
BETA_TWO = 0.999
ADAM_EPS = 1e-08
DECAY_RATE = 0.01
LEARN_RATE = 0.02
SMALL_RATE = 0.1
CLIP_RATIO = 0.5
MESH = pl.DeviceIdType.MESH
F32 = jnp.float32
BF16 = jnp.bfloat16

ORDER = (6, 5, 0, 1, 2, 3, 4)
TILE = 256


def mm(a, b):
    return lax.dot_general(a, b, (((1,), (0,)), ((), ())), preferred_element_type=F32)


def mm_t(a, b):
    return lax.dot_general(a, b, (((1,), (1,)), ((), ())), preferred_element_type=F32)


def gelu_both(v):
    k = math.sqrt(2.0 / math.pi)
    sq = v * v
    t = jnp.tanh(v * (k + (k * 0.044715) * sq))
    half = 0.5 + 0.5 * t
    slope = half + (0.5 * v) * (1.0 - t * t) * (k + (3.0 * k * 0.044715) * sq)
    return v * half, slope


def colsum(v):
    return jnp.sum(v, axis=0, keepdims=True)


def kernel(
    dims,
    slot_ref,
    sp_hbm,
    dy_hbm,
    x_hbm,
    master_hbm,
    pooled_hbm,
    ig_hbm,
    g_ref,
    gs_hbm,
    ssq_hbm,
    sp_ref,
    dy_ref,
    pooled_ref,
    ig_ref,
    gs_ref,
    ssq_ref,
    w,
    mst,
    xf,
    sh,
    d1,
    h,
    a2,
    d2,
    r,
    rd,
    dl,
    dz,
    b,
    a1t,
    rdt,
    snd,
    own,
    rcv,
    fst,
    sec,
    zr,
    zs,
    res,
    stage,
    par,
    ar_val,
    ar_core,
    ar_chip,
    last_val,
    last_core,
    last_chip,
    hx_s,
    hx_r,
    hd_s,
    hd_r,
    il,
    sq_all,
    ld_sem,
    st_sem,
    w_send,
    w_sib,
    w_xs,
    w_x,
    w_y,
    w_z,
    ar_s,
    ar_r,
    ar_s2,
    ar_r2,
    h_s,
    h_r,
    c_s,
    c_r,
    f_s,
    f_r,
    s_s,
    s_r,
    z_s,
    z_r,
    zb_s,
    zb_r,
    g_s,
    g_r,
    q_s,
    q_r,
    g_l,
):
    NX, NY, NZ, cap, rows_total = dims
    pos, ch = dz.shape
    hp = pos // 2
    seq_n, own_n = NZ * NY, NX * 2
    n_dev = seq_n * own_n
    chips = n_dev // 2
    rb = ch // 2 // (NX * NY)
    nt = ch // TILE
    s_ix, o_ix = lax.axis_index("seq"), lax.axis_index("own")
    z, y = s_ix // NY, lax.rem(s_ix, NY)
    x, c = o_ix // 2, lax.rem(o_ix, 2)
    me = s_ix * own_n + o_ix
    inv_n = 1.0 / rows_total

    def dev(z_, y_, x_, c_):
        return (z_ * NY + y_, x_ * 2 + c_)

    def wrap(v, n):
        return jnp.where(v >= n, v - n, v)

    def remote(src, dst, ss, rs, to):
        return pltpu.make_async_remote_copy(
            src_ref=src, dst_ref=dst, send_sem=ss, recv_sem=rs, device_id=to, device_id_type=MESH
        )

    def wait_bytes(ref, sem):
        pltpu.make_async_copy(ref, ref, sem).wait()

    sib = dev(z, y, x, 1 - c)

    for j in range(cap):
        pltpu.make_async_copy(master_hbm.at[j], mst.at[j], ld_sem.at[j]).start()
    pltpu.make_async_copy(x_hbm, dz, ld_sem.at[cap]).start()
    loads = [
        pltpu.make_async_copy(sp_hbm, sp_ref, ld_sem.at[cap + 1]),
        pltpu.make_async_copy(dy_hbm, dy_ref, ld_sem.at[cap + 2]),
    ]
    for cp in loads:
        cp.start()
    saves = [
        pltpu.make_async_copy(src, dst, st_sem.at[i])
        for i, (src, dst) in enumerate(
            ((pooled_ref, pooled_hbm), (ig_ref, ig_hbm), (gs_ref, gs_hbm), (ssq_ref, ssq_hbm))
        )
    ]

    at_end, at_start = o_ix == own_n - 1, o_ix == 0
    to_after = (wrap(s_ix + at_end.astype(jnp.int32), seq_n), wrap(o_ix + 1, own_n))
    to_before = (
        wrap(s_ix + seq_n - at_start.astype(jnp.int32), seq_n),
        wrap(o_ix + own_n - 1, own_n),
    )
    chip_peers = [(ds, dx) for ds in range(seq_n) for dx in range(NX) if ds or dx]
    plane_peers = [
        (dy_, dx, dc) for dy_ in range(NY) for dx in range(NX) for dc in range(2) if dy_ or dx or dc
    ]

    def chip_peer(ds, dx):
        return (wrap(s_ix + ds, seq_n), wrap(x + dx, NX) * 2 + c)

    def plane_peer(dy_, dx, dc):
        return wrap(y + dy_, NY), wrap(x + dx, NX), c + dc - 2 * c * dc

    barrier = pltpu.get_barrier_semaphore()
    crossed = [k for k in plane_peers if k[2]]

    def greet(to):
        pl.semaphore_signal(barrier, inc=1, device_id=to, device_id_type=MESH)

    for k in chip_peers:
        greet(chip_peer(*k))
    for k in crossed:
        py, px, pc = plane_peer(*k)
        greet(dev(z, py, px, pc))
    greet(to_before)
    greet(to_after)
    n_greet = len(chip_peers) + len(crossed) + 2

    for j in range(cap):
        pltpu.make_async_copy(master_hbm.at[j], mst.at[j], ld_sem.at[j]).wait()
        w[o_ix * cap + j] = mst[j].astype(BF16)
    pl.semaphore_wait(barrier, n_greet)

    thirds = (NX, NY, NZ) == (2, 2, 4)
    QR = 64
    third = ch // 3
    nq = third // QR
    w_base = o_ix * cap
    if thirds:
        is_end = jnp.logical_or(z == 0, z == NZ - 1)
        zp = z + 1 - 2 * lax.rem(z, 2)
        ox = (1 - x) * 2 + c
        to_x, to_y, to_z = dev(z, y, 1 - x, c), dev(z, 1 - y, x, c), dev(zp, y, x, c)
        alpha = jnp.where(is_end, y, 2)
        z_part = jnp.where(is_end, 2, y)

        def piece(slot, part, q):
            return w.at[slot, pl.ds(pl.multiple_of(part * third + q * QR, QR), QR)]

        WINDOW = 2

        def x_copy(i):
            ref = piece(w_base + i // nq, alpha, i % nq)
            return remote(ref, ref, w_xs.at[i], w_x.at[i], to_x)

        for i in range(WINDOW):
            x_copy(i).start()
        for j in range(cap):
            ref = w.at[w_base + j]
            remote(ref, ref, w_send.at[0], w_sib.at[0], sib).start()

        n_pieces = cap * nq
        LAG_Z, LAG_Y = 2, 4
        n_steps = n_pieces + LAG_Y

        def pass_on(ref, sem, to):
            remote(ref, ref, w_send.at[0], sem, to).start()

        def weights_step(i):
            if i < n_pieces:
                ref = piece(ox * cap + i // nq, alpha, i % nq)
                remote(ref, ref, w_xs.at[i], w_x.at[i], to_x).wait_recv()
                x_copy(i).wait_send()
                if i + WINDOW < n_pieces:
                    x_copy(i + WINDOW).start()
                pass_on(ref, w_z.at[i], to_z)

                @pl.when(is_end)
                def _():
                    pass_on(ref, w_y.at[i], to_y)

                pass_on(ref, w_sib.at[0], sib)
            k = i - LAG_Z
            if 0 <= k < n_pieces:
                ref_z = piece(ox * cap + k // nq, z_part, k % nq)
                remote(ref_z, ref_z, w_send.at[0], w_z.at[k], to_z).wait_recv()

                @pl.when(jnp.logical_not(is_end))
                def _():
                    pass_on(ref_z, w_y.at[k], to_y)

                pass_on(ref_z, w_sib.at[0], sib)
            k = i - LAG_Y
            if 0 <= k < n_pieces:
                ref_y = piece(ox * cap + k // nq, 1 - y, k % nq)
                remote(ref_y, ref_y, w_send.at[0], w_y.at[k], to_y).wait_recv()
                pass_on(ref_y, w_sib.at[0], sib)

        def weights_end():
            wait_bytes(w.at[pl.ds(0, 2 * cap)], w_sib.at[0])
            wait_bytes(w.at[pl.ds(0, 2 * cap)], w_send.at[0])
            wait_bytes(w.at[0, pl.ds(0, 2 * third)], w_send.at[0])
            wait_bytes(w.at[0, pl.ds(0, 2 * third)], w_send.at[0])

    else:

        def send_w(i, carry):
            p = lax.rem(o_ix + 1 + i, own_n)
            ref = w.at[pl.ds(w_base, cap)]
            remote(ref, ref, w_send.at[0], w_sib.at[0], (s_ix, p)).start()
            return carry

        lax.fori_loop(0, own_n - 1, send_w, 0)

        n_steps = 0

        def weights_step(i):
            pass

        def weights_end():
            wait_bytes(w.at[pl.ds(0, (own_n - 1) * cap)], w_sib.at[0])
            wait_bytes(w.at[pl.ds(0, (own_n - 1) * cap)], w_send.at[0])

    chip = s_ix * NX + x

    def ar_refs(i):
        if i == 3:
            return last_val, last_core, last_chip
        return ar_val.at[i], ar_core.at[i], ar_chip.at[i % ar_chip.shape[0]]

    def ar_pair_copy(i):
        val, core, _ = ar_refs(i)
        return remote(val, core, ar_s.at[i], ar_r.at[i], sib)

    def ar_begin(i):
        ar_pair_copy(i).start()

    def ar_mid(i):
        ar_pair_copy(i).wait()
        val, core, every = ar_refs(i)
        every[chip] = val[...] + core[...]
        for k in chip_peers:
            ref = every.at[chip]
            remote(ref, ref, ar_s2.at[i], ar_r2.at[i], chip_peer(*k)).start()

    def ar_end(i):
        _, _, every = ar_refs(i)
        wait_bytes(every.at[pl.ds(0, chips - 1)], ar_r2.at[i])
        wait_bytes(every.at[pl.ds(0, chips - 1)], ar_s2.at[i])
        return jnp.sum(every[...], axis=0)

    pltpu.make_async_copy(x_hbm, dz, ld_sem.at[cap]).wait()
    for cp in loads:
        cp.wait()
    ts = hp // 3
    total = jnp.zeros((1, ch), F32)
    square = jnp.zeros((1, ch), F32)
    for i in range(3):
        for j in range(ch // 128):
            il[j] = dz[2 * ts * i : 2 * ts * (i + 1), j * 128 : (j + 1) * 128].astype(F32)
        for k in range(2):
            v = jnp.concatenate([il[j, pl.ds(k, ts, stride=2), :] for j in range(ch // 128)], axis=1)
            xf[k * hp + i * ts : k * hp + (i + 1) * ts] = v
            total += colsum(v)
            square += colsum(v * v)
    zero_row = jnp.zeros((1, ch), F32)
    ar_val[0] = jnp.concatenate([total, square], axis=0)
    ar_begin(0)
    has_before = jnp.where(me > 0, 1.0, 0.0).astype(F32)
    has_after = jnp.where(me < n_dev - 1, 1.0, 0.0).astype(F32)
    hx_s[0] = jnp.concatenate([xf[0:1], xf[hp : hp + 1]], axis=0)
    hx_s[1] = jnp.concatenate([xf[hp - 1 : hp], xf[pos - 1 : pos]], axis=0)
    hx = [
        remote(hx_s.at[0], hx_r.at[1], h_s.at[0], h_r.at[0], to_before),
        remote(hx_s.at[1], hx_r.at[0], h_s.at[1], h_r.at[1], to_after),
    ]
    for cp in hx:
        cp.start()
    ar_mid(0)
    for i in range(min(2, n_steps)):
        weights_step(i)
    sums = ar_end(0)
    for cp in hx:
        cp.wait()

    mu1 = sums[0:1] * inv_n
    rstd1 = lax.rsqrt(sums[1:2] * inv_n - mu1 * mu1 + NORM_EPS)
    g1, b1, c1 = sp_ref[0:1], sp_ref[1:2], sp_ref[2:3]
    g2, b2, c2 = sp_ref[3:4], sp_ref[4:5], sp_ref[5:6]
    PAD = 8

    def windows():
        for k in range(2):
            for i in range(3):
                b[k * hp + i * ts : k * hp + (i + 1) * ts] = sh[
                    k, PAD - 1 + i * ts : PAD - 1 + (i + 1) * ts
                ].astype(BF16)
                lo = (4 + k) * hp + i * ts
                b[lo : lo + ts] = sh[k, PAD + 1 + i * ts : PAD + 1 + (i + 1) * ts].astype(BF16)

    for k in range(2):
        for i in range(3):
            lo = k * hp + i * ts
            act, slope = gelu_both((xf[lo : lo + ts] - mu1) * rstd1 * g1 + b1)
            d1[lo : lo + ts] = slope
            b[2 * hp + lo : 2 * hp + lo + ts] = act.astype(BF16)
            sh[k, PAD + i * ts : PAD + (i + 1) * ts] = act
            if 2 + 3 * k + i < n_steps:
                weights_step(2 + 3 * k + i)
    lead, _ = gelu_both((hx_r[0] - mu1) * rstd1 * g1 + b1)
    trail, _ = gelu_both((hx_r[1] - mu1) * rstd1 * g1 + b1)
    lead, trail = lead * has_before, trail * has_after
    for k in range(2):
        sh[k, PAD - 1 : PAD] = lead[k : k + 1]
        sh[k, PAD + hp : PAD + hp + 1] = trail[k : k + 1]
    windows()
    for i in range(8, n_steps):
        weights_step(i)
    weights_end()

    slots = [slot_ref[k] for k in range(NMAT)]

    def cols(n):
        return pl.ds(pl.multiple_of(n * TILE, TILE), TILE)

    def over_tiles(fn):
        def body(n, carry):
            fn(cols(n))
            return carry

        lax.fori_loop(0, nt, body, 0)

    def conv_tile(n):
        acc = mm(b[0:pos, :], w[slots[0], :, n])
        for t in range(1, 5):
            acc += mm(b[t * hp : t * hp + pos, :], w[slots[t], :, n])
        acc += sp_ref[2:3, n]
        h[:, n] = acc
        ar_val[1, 0:1, n] = colsum(acc)
        ar_val[1, 1:2, n] = colsum(acc * acc)

    over_tiles(conv_tile)
    ar_begin(1)
    for i in range(nt):
        a1t[i * TILE : (i + 1) * TILE, :] = b[2 * hp : 4 * hp, i * TILE : (i + 1) * TILE].T
    ar_mid(1)
    sums = ar_end(1)
    mu2 = sums[0:1] * inv_n
    rstd2 = lax.rsqrt(sums[1:2] * inv_n - mu2 * mu2 + NORM_EPS)
    for k in range(2):
        for i in range(3):
            lo = k * hp + i * ts
            act, slope = gelu_both((h[lo : lo + ts] - mu2) * rstd2 * g2 + b2)
            d2[lo : lo + ts] = slope
            a2[lo : lo + ts] = act.astype(BF16)

    half = ch // 2
    halves = own.shape[1]
    rh = rb // halves

    def put_gradient(p, lhs, rhs):
        def tile(n):
            v = mm(lhs[...], rhs(n))
            keep = jnp.where(c == 0, v[:half], v[half:]).astype(BF16)
            give = jnp.where(c == 0, v[half:], v[:half]).astype(BF16)
            for i in range(NX * NY):
                for k in range(halves):
                    at = (i * halves + k) * rh
                    own[p, k, i // NY, i % NY, :, n] = keep[at : at + rh]
                    snd[p, k, i // NY, i % NY, :, n] = give[at : at + rh]

        over_tiles(tile)
        core_copy(p).start()

    def core_copy(p):
        return remote(snd.at[p], rcv.at[p], c_s.at[p], c_r.at[p], sib)

    def first_copies(p):
        made = []
        for k in range(NX - 1):
            to = lax.rem(x + 1 + k, NX)
            at = NX - 2 - k
            made.append(remote(own.at[p, 0, to], fst.at[p, 0, at], f_s.at[p, 0, k], f_r.at[p, 0, at], dev(z, y, to, c)))
        for k in range(NY - 1 if halves > 1 else 0):
            to = lax.rem(y + 1 + k, NY)
            at = NY - 2 - k
            made.append(remote(own.at[p, 1, :, to], fst.at[p, 1, at], f_s.at[p, 1, k], f_r.at[p, 1, at], dev(z, to, x, c)))
        return made

    def second_copies(p):
        made = []
        for k in range(NY - 1):
            to = lax.rem(y + 1 + k, NY)
            at = NY - 2 - k
            made.append(remote(own.at[p, 0, x, to], sec.at[p, 0, at], s_s.at[p, 0, k], s_r.at[p, 0, at], dev(z, to, x, c)))
        for k in range(NX - 1 if halves > 1 else 0):
            to = lax.rem(x + 1 + k, NX)
            at = NX - 2 - k
            made.append(remote(own.at[p, 1, to, y], sec.at[p, 1, at], s_s.at[p, 1, k], s_r.at[p, 1, at], dev(z, y, to, c)))
        return made

    def wait_all(copies):
        for cp in copies:
            cp.wait_send()
        for cp in copies:
            cp.wait_recv()

    def step_first(p):
        core_copy(p).wait()
        for k in range(halves):
            for i in range(NX):
                for j in range(NY):
                    own[p, k, i, j] = (own[p, k, i, j].astype(F32) + rcv[p, k, i, j].astype(F32)).astype(BF16)
        for cp in first_copies(p):
            cp.start()

    def step_second(p):
        wait_all(first_copies(p))
        for k in range(halves):
            n, m = (NX, NY) if k == 0 else (NY, NX)
            for j in range(m):
                at = (p, 0, x, j) if k == 0 else (p, 1, j, y)
                v = own[at].astype(F32)
                for i in range(n - 1):
                    v += fst[p, k, i, j].astype(F32)
                own[at] = v.astype(BF16)
        for cp in second_copies(p):
            cp.start()

    chain = NZ == 4 and halves == 2
    is_outer = jnp.logical_or(z == 0, z == NZ - 1)
    is_inner = jnp.logical_not(is_outer)
    inner = jnp.where(z < 2, 1, 2)
    my_half = jnp.clip(z - 1, 0, 1)

    def end_copy(p):
        return remote(zs.at[p], zr.at[p, 0], z_s.at[p, 0], z_r.at[p, 0], dev(inner, y, x, c))

    def direct(p):
        return chain and p >= NMAT - 2

    def direct_copy(p, k, i):
        return remote(
            zs.at[p, k], zr.at[p, i, k], z_s.at[p, k], z_r.at[p, 2 * i + k], dev(k + 1, y, x, c)
        )

    def swap_copy(p, k):
        return remote(zs.at[p, k], zr.at[p, 1, k], z_s.at[p, 1], z_r.at[p, 1], dev(lax.rem(3 - z + NZ, NZ), y, x, c))

    def spread_copy(p, k, i):
        if direct(p):
            to = wrap(z + 1 + i, NZ)
        else:
            to = jnp.clip(3 - z, 0, NZ - 1) if i == 1 else jnp.where(z < 2, 0, NZ - 1)
        return remote(res.at[p, k], res.at[p, k], zb_s.at[p, i], zb_r.at[p, k], dev(to, y, x, c))

    def gather_copy(p, at):
        return remote(zs.at[p], zr.at[p, at], z_s.at[p, 0], z_r.at[p, at], dev(0, y, x, c))

    def whole_copy(p, i):
        return remote(res.at[p], res.at[p], zb_s.at[p, i], zb_r.at[p, 0], dev(lax.rem(z + 1 + i, NZ), y, x, c))

    def step_sum(p):
        wait_all(second_copies(p))
        for k in range(halves):
            v = own[p, k, x, y].astype(F32)
            for i in range((NY if k == 0 else NX) - 1):
                v += sec[p, k, i].astype(F32)
            zs[p, k] = v.astype(BF16)
        if direct(p):

            @pl.when(is_outer)
            def _():
                for k in range(2):
                    direct_copy(p, k, z // 3).start()

            @pl.when(is_inner)
            def _():
                direct_copy(p, 1 - my_half, 2).start()

        elif chain:

            @pl.when(is_outer)
            def _():
                end_copy(p).start()

        else:

            @pl.when(z > 0)
            def _():
                gather_copy(p, z - 1).start()

    def step_pass(p):
        if chain and not direct(p):

            @pl.when(is_inner)
            def _():
                end_copy(p).wait_recv()
                zs[p] = (zs[p].astype(F32) + zr[p, 0].astype(F32)).astype(BF16)
                swap_copy(p, 1 - my_half).start()

    def step_root(p):
        if chain:

            @pl.when(is_inner)
            def _():
                v = zs[p, my_half].astype(F32)
                if direct(p):
                    for i in range(3):
                        direct_copy(p, my_half, i).wait_recv()
                        v += zr[p, i, my_half].astype(F32)
                else:
                    swap_copy(p, my_half).wait_recv()
                    v += zr[p, 1, my_half].astype(F32)
                res[p, my_half] = v.astype(BF16)
                for i in range(NZ - 1 if direct(p) else 2):
                    spread_copy(p, my_half, i).start()

        else:

            @pl.when(z == 0)
            def _():
                v = zs[p].astype(F32)
                for i in range(NZ - 1):
                    gather_copy(p, i).wait_recv()
                    v += zr[p, i].astype(F32)
                res[p] = v.astype(BF16)
                for i in range(NZ - 1):
                    whole_copy(p, i).start()

    def step_relay(p):
        if chain and not direct(p):

            @pl.when(is_inner)
            def _():
                spread_copy(p, 1 - my_half, 2).wait_recv()
                spread_copy(p, 1 - my_half, 2).start()

    def step_spread(p):
        if chain:

            @pl.when(is_outer)
            def _():
                for k in range(2):
                    spread_copy(p, k, 0).wait_recv()

            if direct(p):

                @pl.when(is_inner)
                def _():
                    spread_copy(p, 1 - my_half, 0).wait_recv()

        else:

            @pl.when(z > 0)
            def _():
                whole_copy(p, 0).wait_recv()

    def step_done(p):
        if chain:

            @pl.when(is_outer)
            def _():
                if direct(p):
                    for k in range(2):
                        direct_copy(p, k, 0).wait_send()
                else:
                    end_copy(p).wait_send()

            @pl.when(is_inner)
            def _():
                if direct(p):
                    direct_copy(p, 1 - my_half, 2).wait_send()
                else:
                    swap_copy(p, 1 - my_half).wait_send()
                for i in range(NZ - 1):
                    half_sent = my_half if direct(p) or i < 2 else 1 - my_half
                    spread_copy(p, half_sent, i).wait_send()

        else:

            @pl.when(z > 0)
            def _():
                gather_copy(p, z - 1).wait_send()

            @pl.when(z == 0)
            def _():
                for i in range(NZ - 1):
                    whole_copy(p, i).wait_send()

    par[...] = jnp.concatenate([mu2, rstd2, zero_row, zero_row], axis=0)

    def mix_tile(n):
        v = h[:, n] + mm(a2[...], w[slots[5], :, n]) + sp_ref[5:6, n]
        r[:, n] = v
        rd[:, n] = (v[:hp] - v[hp:]).astype(BF16)

    over_tiles(mix_tile)
    for i in range(nt):
        rdt[i * TILE : (i + 1) * TILE, :] = rd[:, i * TILE : (i + 1) * TILE].T

    def pool_tile(n):
        diff = mm(rd[...], w[slots[6], :, n])
        t = 0.5 * jnp.tanh(0.5 * diff)
        p0, p1 = 0.5 + t, 0.5 - t
        r0, r1 = r[0:hp, n], r[hp:pos, n]
        dy = dy_ref[:, n].astype(F32)
        pooled_ref[:, n] = (p0 * r0 + p1 * r1).astype(BF16)
        dl[:, n] = (p0 * p1 * dy * (r0 - r1)).astype(BF16)
        mst[0, 0:hp, n] = p0 * dy
        mst[0, hp:pos, n] = p1 * dy

    over_tiles(pool_tile)
    saves[0].start()
    put_gradient(0, rdt, lambda n: dl[:, n])

    def resid_tile(n):
        v = mm_t(dl[...], w[slots[6], n, :])
        v0 = mst[0, 0:hp, n] + v
        v1 = mst[0, hp:pos, n] - v
        mst[0, 0:hp, n] = v0
        mst[0, hp:pos, n] = v1
        dz[0:hp, n] = v0.astype(BF16)
        dz[hp:pos, n] = v1.astype(BF16)
        last_val[3:4, n] = colsum(v0) + colsum(v1)

    over_tiles(resid_tile)
    step_first(0)

    def branch_tile(n):
        v = mm_t(dz[...], w[slots[5], n, :]) * d2[:, n]
        mst[1, :, n] = v
        xhat = (h[:, n] - par[0:1, n]) * par[1:2, n]
        ar_val[2, 0:1, n] = colsum(v)
        ar_val[2, 1:2, n] = colsum(v * xhat)

    over_tiles(branch_tile)
    ar_begin(2)
    hd_s[0] = jnp.concatenate(
        [v for ref in (mst.at[0], mst.at[1], h) for v in (ref[0:1], ref[hp : hp + 1])]
        + [zero_row, zero_row],
        axis=0,
    )
    hd_s[1] = jnp.concatenate(
        [v for ref in (mst.at[0], mst.at[1], h) for v in (ref[hp - 1 : hp], ref[pos - 1 : pos])]
        + [zero_row, zero_row],
        axis=0,
    )
    hd = [
        remote(hd_s.at[0], hd_r.at[1], h_s.at[2], h_r.at[2], to_before),
        remote(hd_s.at[1], hd_r.at[0], h_s.at[3], h_r.at[3], to_after),
    ]
    for cp in hd:
        cp.start()

    for i in range(nt):
        b[i * TILE : (i + 1) * TILE, :] = a2[:, i * TILE : (i + 1) * TILE].T
    ar_mid(2)
    put_gradient(1, b.at[pl.ds(0, ch)], lambda n: dz[:, n])
    step_second(0)
    step_first(1)
    sums = ar_end(2)
    s2, q2 = sums[0:1], sums[1:2]

    scale2 = rstd2 * g2

    def dh_of(dr, dn, hid):
        xhat = (hid - mu2) * rstd2
        return dr + scale2 * (dn - s2 * inv_n - xhat * (q2 * inv_n))

    e1_local = jnp.zeros((1, ch), F32)
    for k in range(2):
        for i in range(3):
            lo = k * hp + i * ts
            v = dh_of(mst[0, lo : lo + ts], mst[1, lo : lo + ts], h[lo : lo + ts])
            e1_local += colsum(v)
            sh[k, PAD + i * ts : PAD + (i + 1) * ts] = v
            b[2 * hp + lo : 2 * hp + lo + ts] = v.astype(BF16)
    for cp in hd:
        cp.wait()
    lead = dh_of(hd_r[0, 0:2], hd_r[0, 2:4], hd_r[0, 4:6]) * has_before
    trail = dh_of(hd_r[1, 0:2], hd_r[1, 2:4], hd_r[1, 4:6]) * has_after
    for k in range(2):
        sh[k, PAD - 1 : PAD] = lead[k : k + 1]
        sh[k, PAD + hp : PAD + hp + 1] = trail[k : k + 1]
    windows()

    def tap(t):
        lo = (4 - t) * hp
        put_gradient(2 + t, a1t, lambda n: b[lo : lo + pos, n])

    tap(0)
    tap(1)
    step_first(2)
    step_second(1)
    tap(2)
    step_first(3)
    step_sum(0)
    tap(3)
    tap(4)
    step_second(2)
    step_first(4)
    step_pass(0)
    step_sum(1)

    last_val[2:3] = e1_local
    par[...] = jnp.concatenate([mu1, rstd1, zero_row, zero_row], axis=0)

    def input_tile(n):
        acc = mm_t(b[4 * hp : 4 * hp + pos, :], w[slots[0], n, :])
        for t in range(1, 5):
            lo = (4 - t) * hp
            acc += mm_t(b[lo : lo + pos, :], w[slots[t], n, :])
        v = acc * d1[:, n]
        mst[1, :, n] = v
        xhat = (xf[:, n] - par[0:1, n]) * par[1:2, n]
        last_val[0:1, n] = colsum(v)
        last_val[1:2, n] = colsum(v * xhat)

    input_tile(cols(0))
    step_second(3)
    step_first(5)
    step_root(0)
    step_pass(1)
    step_sum(2)
    for i in range(1, nt - 1):
        input_tile(cols(i))
    step_second(4)
    step_first(6)
    step_relay(0)
    step_root(1)
    step_pass(2)
    step_sum(3)
    input_tile(cols(nt - 1))
    ar_begin(3)
    step_second(5)
    step_relay(1)
    step_root(2)
    step_pass(3)
    step_sum(4)
    ar_mid(3)
    step_second(6)
    step_relay(2)
    step_root(3)
    step_pass(4)
    step_sum(5)
    sums = ar_end(3)
    s1, q1, e1, e2 = sums[0:1], sums[1:2], sums[2:3], sums[3:4]
    gs_ref[...] = jnp.concatenate([q1, s1, e1, q2, s2, e2], axis=0)
    saves[2].start()
    scale1 = rstd1 * g1
    def input_rows(i):
        for k in range(2):
            lo = k * hp + i * ts
            xhat = (xf[lo : lo + ts] - mu1) * rstd1
            v = scale1 * (mst[1, lo : lo + ts] - s1 * inv_n - xhat * (q1 * inv_n))
            for j in range(ch // 128):
                il[j, pl.ds(k, ts, stride=2), :] = v[:, j * 128 : (j + 1) * 128]
        for j in range(ch // 128):
            ig_ref[2 * i * ts : 2 * (i + 1) * ts, j * 128 : (j + 1) * 128] = il[j].astype(BF16)

    input_rows(0)
    step_relay(3)
    step_root(4)
    step_sum(6)
    input_rows(1)
    step_relay(4)
    step_root(5)
    input_rows(2)
    saves[1].start()
    step_root(6)
    for p in range(NMAT):
        step_spread(p)

    plane = NX * NY * 2

    def plane_id(py, px, pc):
        return (px * NY + py) * 2 + pc

    mine = plane_id(y, x, c)
    for s in range(own_n * cap):
        at = jnp.int32(0)
        for p in range(NMAT):
            at = jnp.maximum(at, jnp.where(slots[ORDER[p]] == s, p, 0))
        stage[s] = res[at]

    def gather_send(k):
        py, px, pc = plane_peer(*plane_peers[k])
        src = stage.at[pl.ds((px * 2 + pc) * cap, cap)]
        return remote(src, g_ref.at[:, c, x, y], g_s.at[k], g_r.at[mine], dev(z, py, px, pc))

    def gather_recv(k):
        py, px, pc = plane_peer(*plane_peers[k])
        src = stage.at[pl.ds((px * 2 + pc) * cap, cap)]
        return remote(src, g_ref.at[:, pc, px, py], g_s.at[k], g_r.at[plane_id(py, px, pc)], dev(z, py, px, pc))

    def square_copy(k):
        py, px, pc = plane_peer(*plane_peers[k])
        ref = sq_all.at[mine]
        return remote(ref, ref, q_s.at[0], q_r.at[0], dev(z, py, px, pc))

    for k in range(plane - 1):
        gather_send(k).start()
    keep = pltpu.make_async_copy(
        stage.at[pl.ds(o_ix * cap, cap)], g_ref.at[:, c, x, y], g_l.at[0]
    )
    keep.start()
    sq = jnp.zeros((8, ch), F32)
    for p in range(NMAT):
        for k in range(halves):
            v = res[p, k].astype(F32)
            v = v * v
            for i in range(rh // 8):
                sq += v[i * 8 : (i + 1) * 8]
    sq_all[mine] = sq
    for k in range(plane - 1):
        square_copy(k).start()
    for p in range(NMAT):
        step_done(p)
    wait_bytes(sq_all.at[pl.ds(0, plane - 1)], q_r.at[0])
    wait_bytes(sq_all.at[pl.ds(0, plane - 1)], q_s.at[0])
    ssq_ref[...] = jnp.sum(sq_all[...], axis=0)
    saves[3].start()
    for k in range(plane - 1):
        gather_send(k).wait_send()
    for k in range(plane - 1):
        gather_recv(k).wait_recv()
    keep.wait()
    for cp in saves:
        cp.wait()


def adam(grads, first_old, second_old):
    first_new = BETA_ONE * first_old + (1.0 - BETA_ONE) * grads
    second_new = BETA_TWO * second_old + (1.0 - BETA_TWO) * grads * grads
    direction = (first_new * (1.0 / (1.0 - BETA_ONE**STEP))) / (
        jnp.sqrt(second_new * (1.0 / (1.0 - BETA_TWO**STEP))) + ADAM_EPS
    )
    return first_new, second_new, direction


def optimizer_kernel(
    slot_ref,
    ssq_hbm,
    gs_hbm,
    sp_hbm,
    sf_hbm,
    ss_hbm,
    g_hbm,
    left_hbm,
    right_hbm,
    first_hbm,
    second_hbm,
    master_hbm,
    norm_ref,
    nsp_hbm,
    nsf_hbm,
    nss_hbm,
    nmaster_hbm,
    nfirst_hbm,
    nsecond_hbm,
    g,
    left,
    right,
    first,
    second,
    master,
    left_low,
    left_t,
    right_low,
    mid,
    turn,
    ssq,
    gs_all,
    sp,
    sf,
    ss,
    in_sem,
    out_sem,
    small_sem,
):
    cap, ch, _ = g.shape
    nt = ch // TILE
    sources = (g_hbm, right_hbm, left_hbm, first_hbm, second_hbm, master_hbm)
    places = (g, right, left, first, second, master)

    def load(i, j):
        return pltpu.make_async_copy(sources[i].at[j], places[i].at[j], in_sem.at[i, j])

    def save(i, j):
        src = (first, second)[i]
        dst = (nfirst_hbm, nsecond_hbm)[i]
        return pltpu.make_async_copy(src.at[j], dst.at[j], out_sem.at[i, j])

    def save_rows(j, i):
        at = pl.ds(i * TILE, TILE)
        return pltpu.make_async_copy(master.at[j, at], nmaster_hbm.at[j, at], out_sem.at[2 + i, j])

    for i in range(3):
        load(i, 0).start()

    smalls = (ssq, gs_all, sp, sf, ss)

    def small_load(i):
        return pltpu.make_async_copy((ssq_hbm, gs_hbm, sp_hbm, sf_hbm, ss_hbm)[i], smalls[i], small_sem.at[i])

    def small_save(i):
        return pltpu.make_async_copy(smalls[2 + i], (nsp_hbm, nsf_hbm, nss_hbm)[i], small_sem.at[i])

    for i in range(5):
        small_load(i).start()

    def small_update():
        for i in range(5):
            small_load(i).wait()
        gs = gs_all[...]
        norm = jnp.sqrt(
            jnp.sum(jnp.sum(ssq[...], axis=0, keepdims=True), axis=1, keepdims=True)
            + jnp.sum(jnp.sum(gs * gs, axis=0, keepdims=True), axis=1, keepdims=True)
        )
        norm_ref[...] = norm
        factor = jnp.minimum(1.0, CLIP_RATIO * ch * math.sqrt(NMAT) / (norm + 1e-06))
        small_first, small_second, small_dir = adam(gs * factor, sf[...], ss[...])
        sp[...] = sp[...] - SMALL_RATE * (small_dir + DECAY_RATE * sp[...])
        sf[...] = small_first
        ss[...] = small_second
        for i in range(3):
            small_save(i).start()
        return factor

    def over_tiles(fn):
        def body(n, carry):
            fn(pl.ds(pl.multiple_of(n * TILE, TILE), TILE))
            return carry

        lax.fori_loop(0, nt, body, 0)

    for j in range(cap):
        slot = lax.axis_index("own") * cap + j
        used = slot_ref[0] == slot
        for k in range(1, NMAT):
            used = jnp.logical_or(used, slot_ref[k] == slot)
        load(0, j).wait()
        load(1, j).wait()
        for i in range(3, 6):
            load(i, j).start()
        right_low[...] = right[j].astype(BF16)

        def mid_tile(n):
            mid[:, n] = mm(g[j], right_low[:, n]).astype(BF16)

        over_tiles(mid_tile)
        if j == 0:
            factor = small_update()
        load(2, j).wait()
        if j + 1 < cap:
            load(0, j + 1).start()
            load(1, j + 1).start()
        left_low[...] = left[j].astype(BF16)
        for i in range(nt):
            left_t[i * TILE : (i + 1) * TILE, :] = left_low[:, i * TILE : (i + 1) * TILE].T
        load(3, j).wait()
        load(4, j).wait()
        if j + 1 < cap:
            load(2, j + 1).start()

        def moment_tile(n):
            grads = factor * mm(left_t[...], mid[:, n])
            f_old, s_old = first[j, :, n], second[j, :, n]
            f_new, s_new, direction = adam(grads, f_old, s_old)
            first[j, :, n] = jnp.where(used, f_new, f_old)
            second[j, :, n] = jnp.where(used, s_new, s_old)
            turn[:, n] = direction.astype(BF16)

        over_tiles(moment_tile)
        save(0, j).start()
        save(1, j).start()

        def back_tile(n):
            mid[:, n] = mm(left_low[...], turn[:, n]).astype(BF16)

        over_tiles(back_tile)
        load(5, j).wait()

        for i in range(nt):
            at = pl.ds(i * TILE, TILE)
            old = master[j, at, :]
            step = mm_t(mid[at, :], right_low[...]) + DECAY_RATE * old
            master[j, at, :] = jnp.where(used, old - LEARN_RATE * step, old)
            save_rows(j, i).start()
    for i in range(3):
        small_save(i).wait()
    for j in range(cap):
        for i in range(2):
            save(i, j).wait()
        for i in range(nt):
            save_rows(j, i).wait()


def optimizer(slots, squares, small_grad, small_params, small_first, small_second, *large):
    cap, ch, _ = large[5].shape
    vm, dma = pltpu.VMEM, pltpu.SemaphoreType.DMA
    in_vmem = pl.BlockSpec(memory_space=pltpu.VMEM)
    anywhere = pl.BlockSpec(memory_space=pl.ANY)
    big = jax.ShapeDtypeStruct((cap, ch, ch), F32)
    small = jax.ShapeDtypeStruct((6, ch), F32)
    return pl.pallas_call(
        optimizer_kernel,
        out_shape=(
            jax.ShapeDtypeStruct((1, 1), F32),
            small,
            small,
            small,
            big,
            big,
            big,
        ),
        in_specs=[pl.BlockSpec(memory_space=pltpu.SMEM)] + [anywhere] * 11,
        out_specs=(in_vmem,) + (anywhere,) * 6,
        scratch_shapes=[vm((cap, ch, ch), BF16)]
        + [vm((cap, ch, ch), F32)] * 5
        + [vm((ch, ch), BF16)] * 5
        + [vm((8, ch), F32)]
        + [vm((6, ch), F32)] * 4
        + [dma((6, cap)), dma((2 + ch // TILE, cap)), dma((5,))],
        compiler_params=pltpu.CompilerParams(vmem_limit_bytes=60 * 2**20),
    )(slots, squares, small_grad, small_params, small_first, small_second, *large)


def block_and_grads(inputs, cotangent, small_params, slot_of_matrix, master):
    pos, ch = inputs.shape
    seq_n, own_n = lax.axis_size("seq"), lax.axis_size("own")
    nx = own_n // 2
    ny = nx
    nz = seq_n // ny
    cap = master.shape[0]
    hp = pos // 2
    slots = cap * own_n
    chips = seq_n * nx
    rb = ch // 2 // (nx * ny)
    plane = nx * ny * 2
    nn = max(nx, ny)
    halves = 2 if rb % 32 == 0 else 1
    rh = rb // halves
    dma = pltpu.SemaphoreType.DMA
    vm = pltpu.VMEM
    scratch = [
        vm((6, ch), F32),
        vm((hp, ch), BF16),
        vm((hp, ch), BF16),
        vm((pos, ch), BF16),
        vm((6, ch), F32),
        vm((8, ch), F32),
        vm((slots, ch, ch), BF16),
        vm((max(cap, 2), ch, ch), F32),
        vm((pos, ch), F32),
        vm((2, hp + 16, ch), F32),
        vm((pos, ch), F32),
        vm((pos, ch), F32),
        vm((pos, ch), BF16),
        vm((pos, ch), F32),
        vm((pos, ch), F32),
        vm((hp, ch), BF16),
        vm((hp, ch), BF16),
        vm((pos, ch), BF16),
        vm((6 * hp, ch), BF16),
        vm((ch, pos), BF16),
        vm((ch, hp), BF16),
        vm((NMAT, halves, nx, ny, rh, ch), BF16),
        vm((NMAT, halves, nx, ny, rh, ch), BF16),
        vm((NMAT, halves, nx, ny, rh, ch), BF16),
        vm((NMAT, halves, nn - 1, nn, rh, ch), BF16),
        vm((NMAT, halves, nn - 1, rh, ch), BF16),
        vm((NMAT, nz - 1, halves, rh, ch), BF16),
        vm((NMAT, halves, rh, ch), BF16),
        vm((NMAT, halves, rh, ch), BF16),
        vm((slots, halves, rh, ch), BF16),
        vm((4, ch), F32),
        vm((3, 2, ch), F32),
        vm((3, 2, ch), F32),
        vm((3 if chips <= 16 else 2, chips, 2, ch), F32),
        vm((4, ch), F32),
        vm((4, ch), F32),
        vm((chips, 4, ch), F32),
        vm((2, 2, ch), F32),
        vm((2, 2, ch), F32),
        vm((2, 8, ch), F32),
        vm((2, 8, ch), F32),
        vm((ch // 128, hp // 3 * 2, 128), F32),
        vm((plane, 8, ch), F32),
        dma((cap + 3,)),
        dma((4,)),
        dma((1,)),
        dma((1,)),
        dma((cap * 4,)),
        dma((cap * 4,)),
        dma((cap * 4,)),
        dma((cap * 4,)),
        dma((4,)),
        dma((4,)),
        dma((4,)),
        dma((4,)),
        dma((4,)),
        dma((4,)),
        dma((NMAT,)),
        dma((NMAT,)),
        dma((NMAT, halves, nn - 1)),
        dma((NMAT, halves, nn - 1)),
        dma((NMAT, halves, nn - 1)),
        dma((NMAT, halves, nn - 1)),
        dma((NMAT, 2)),
        dma((NMAT, 2 * nz - 2)),
        dma((NMAT, nz - 1)),
        dma((NMAT, 2)),
        dma((plane - 1,)),
        dma((plane,)),
        dma((1,)),
        dma((1,)),
        dma((1,)),
    ]
    anywhere = pl.BlockSpec(memory_space=pl.ANY)
    return pl.pallas_call(
        functools.partial(kernel, (nx, ny, nz, cap, pos * seq_n * own_n)),
        out_shape=(
            jax.ShapeDtypeStruct((hp, ch), BF16),
            jax.ShapeDtypeStruct((pos, ch), BF16),
            jax.ShapeDtypeStruct((cap, 2, nx, ny, halves, rh, ch), BF16),
            jax.ShapeDtypeStruct((6, ch), F32),
            jax.ShapeDtypeStruct((8, ch), F32),
        ),
        in_specs=[pl.BlockSpec(memory_space=pltpu.SMEM)] + [anywhere] * 4,
        out_specs=(anywhere,) * 5,
        scratch_shapes=scratch,
        compiler_params=pltpu.CompilerParams(
            collective_id=0, has_side_effects=True, vmem_limit_bytes=63 * 2**20
        ),
    )(slot_of_matrix, small_params, cotangent, inputs, master)


def per_device(
    inputs,
    cotangent,
    small_params,
    small_first,
    small_second,
    slot_of_matrix,
    master,
    first_moment,
    second_moment,
    left_basis,
    right_basis,
):
    cap, ch = master.shape[0], master.shape[2]
    pooled, input_grad, owned, small_grad, squares = block_and_grads(
        inputs, cotangent, small_params, slot_of_matrix, master
    )
    (
        grad_norm,
        new_small,
        small_first_new,
        small_second_new,
        new_master,
        new_first,
        new_second,
    ) = optimizer(
        slot_of_matrix,
        squares,
        small_grad,
        small_params,
        small_first,
        small_second,
        owned.reshape(cap, ch, ch),
        left_basis,
        right_basis,
        first_moment,
        second_moment,
        master,
    )
    return (
        pooled,
        input_grad,
        grad_norm.reshape(()),
        new_master,
        new_first,
        new_second,
        new_small,
        small_first_new,
        small_second_new,
    )


def solution(mesh):
    rows, owned, same = P(("seq", "own"), None), P("own", None, None), P()
    return jax.shard_map(
        per_device,
        mesh=mesh,
        in_specs=(rows, rows, same, same, same, same, owned, owned, owned, owned, owned),
        out_specs=(rows, rows, same, owned, owned, owned, same, same, same),
        check_vma=False,
    )
```

```python
import functools
import math

import jax
import jax.numpy as jnp
from jax import lax
from jax.experimental import pallas as pl
from jax.experimental.pallas import tpu as pltpu
from jax.sharding import PartitionSpec as P

NMAT = 7
STEP = 10
NORM_EPS = 1e-05
BETA_ONE = 0.9
BETA_TWO = 0.999
ADAM_EPS = 1e-08
DECAY_RATE = 0.01
LEARN_RATE = 0.02
SMALL_RATE = 0.1
CLIP_RATIO = 0.5
MESH = pl.DeviceIdType.MESH
F32 = jnp.float32
BF16 = jnp.bfloat16

ORDER = (6, 5, 0, 1, 2, 3, 4)
TILE = 256


def mm(a, b):
    return lax.dot_general(a, b, (((1,), (0,)), ((), ())), preferred_element_type=F32)


def mm_t(a, b):
    return lax.dot_general(a, b, (((1,), (1,)), ((), ())), preferred_element_type=F32)


def gelu_both(v):
    k = math.sqrt(2.0 / math.pi)
    sq = v * v
    t = jnp.tanh(v * (k + (k * 0.044715) * sq))
    half = 0.5 + 0.5 * t
    slope = half + (0.5 * v) * (1.0 - t * t) * (k + (3.0 * k * 0.044715) * sq)
    return v * half, slope


def colsum(v):
    return jnp.sum(v, axis=0, keepdims=True)


def kernel(
    dims,
    slot_ref,
    sp_hbm,
    dy_hbm,
    x_hbm,
    master_hbm,
    pooled_hbm,
    ig_hbm,
    g_ref,
    gs_hbm,
    ssq_hbm,
    sp_ref,
    dy_ref,
    pooled_ref,
    ig_ref,
    gs_ref,
    ssq_ref,
    w,
    mst,
    xf,
    sh,
    d1,
    h,
    a2,
    d2,
    r,
    rd,
    dl,
    dz,
    b,
    a1t,
    rdt,
    snd,
    own,
    rcv,
    fst,
    sec,
    zr,
    zs,
    res,
    stage,
    par,
    ar_val,
    ar_core,
    ar_chip,
    last_val,
    last_core,
    last_chip,
    hx_s,
    hx_r,
    hd_s,
    hd_r,
    il,
    sq_all,
    ld_sem,
    st_sem,
    w_send,
    w_sib,
    w_xs,
    w_x,
    w_y,
    w_z,
    ar_s,
    ar_r,
    ar_s2,
    ar_r2,
    h_s,
    h_r,
    c_s,
    c_r,
    f_s,
    f_r,
    s_s,
    s_r,
    z_s,
    z_r,
    zb_s,
    zb_r,
    g_s,
    g_r,
    p_s,
    p_r,
    q_s,
    q_r,
    g_l,
):
    NX, NY, NZ, cap, rows_total = dims
    pos, ch = dz.shape
    hp = pos // 2
    seq_n, own_n = NZ * NY, NX * 2
    n_dev = seq_n * own_n
    chips = n_dev // 2
    rb = ch // 2 // (NX * NY)
    nt = ch // TILE
    s_ix, o_ix = lax.axis_index("seq"), lax.axis_index("own")
    z, y = s_ix // NY, lax.rem(s_ix, NY)
    x, c = o_ix // 2, lax.rem(o_ix, 2)
    me = s_ix * own_n + o_ix
    inv_n = 1.0 / rows_total

    def dev(z_, y_, x_, c_):
        return (z_ * NY + y_, x_ * 2 + c_)

    def wrap(v, n):
        return jnp.where(v >= n, v - n, v)

    def remote(src, dst, ss, rs, to):
        return pltpu.make_async_remote_copy(
            src_ref=src, dst_ref=dst, send_sem=ss, recv_sem=rs, device_id=to, device_id_type=MESH
        )

    def wait_bytes(ref, sem):
        pltpu.make_async_copy(ref, ref, sem).wait()

    sib = dev(z, y, x, 1 - c)

    for j in range(cap):
        pltpu.make_async_copy(master_hbm.at[j], mst.at[j], ld_sem.at[j]).start()
    pltpu.make_async_copy(x_hbm, dz, ld_sem.at[cap]).start()
    loads = [
        pltpu.make_async_copy(sp_hbm, sp_ref, ld_sem.at[cap + 1]),
        pltpu.make_async_copy(dy_hbm, dy_ref, ld_sem.at[cap + 2]),
    ]
    for cp in loads:
        cp.start()
    saves = [
        pltpu.make_async_copy(src, dst, st_sem.at[i])
        for i, (src, dst) in enumerate(
            ((pooled_ref, pooled_hbm), (ig_ref, ig_hbm), (gs_ref, gs_hbm), (ssq_ref, ssq_hbm))
        )
    ]

    at_end, at_start = o_ix == own_n - 1, o_ix == 0
    to_after = (wrap(s_ix + at_end.astype(jnp.int32), seq_n), wrap(o_ix + 1, own_n))
    to_before = (
        wrap(s_ix + seq_n - at_start.astype(jnp.int32), seq_n),
        wrap(o_ix + own_n - 1, own_n),
    )
    chip_peers = [(ds, dx) for ds in range(seq_n) for dx in range(NX) if ds or dx]
    plane_peers = [
        (dy_, dx, dc) for dy_ in range(NY) for dx in range(NX) for dc in range(2) if dy_ or dx or dc
    ]

    def chip_peer(ds, dx):
        return (wrap(s_ix + ds, seq_n), wrap(x + dx, NX) * 2 + c)

    def plane_peer(dy_, dx, dc):
        return wrap(y + dy_, NY), wrap(x + dx, NX), c + dc - 2 * c * dc

    barrier = pltpu.get_barrier_semaphore()
    crossed = [k for k in plane_peers if k[2]]

    def greet(to):
        pl.semaphore_signal(barrier, inc=1, device_id=to, device_id_type=MESH)

    for k in chip_peers:
        greet(chip_peer(*k))
    for k in crossed:
        py, px, pc = plane_peer(*k)
        greet(dev(z, py, px, pc))
    greet(to_before)
    greet(to_after)
    n_greet = len(chip_peers) + len(crossed) + 2

    for j in range(cap):
        pltpu.make_async_copy(master_hbm.at[j], mst.at[j], ld_sem.at[j]).wait()
        w[o_ix * cap + j] = mst[j].astype(BF16)
    pl.semaphore_wait(barrier, n_greet)

    thirds = (NX, NY, NZ) == (2, 2, 4)
    QR = 64
    third = ch // 3
    nq = third // QR
    w_base = o_ix * cap
    if thirds:
        is_end = jnp.logical_or(z == 0, z == NZ - 1)
        zp = z + 1 - 2 * lax.rem(z, 2)
        ox = (1 - x) * 2 + c
        to_x, to_y, to_z = dev(z, y, 1 - x, c), dev(z, 1 - y, x, c), dev(zp, y, x, c)
        alpha = jnp.where(is_end, y, 2)
        z_part = jnp.where(is_end, 2, y)

        def piece(slot, part, q):
            return w.at[slot, pl.ds(pl.multiple_of(part * third + q * QR, QR), QR)]

        WINDOW = 2

        def x_copy(i):
            ref = piece(w_base + i // nq, alpha, i % nq)
            return remote(ref, ref, w_xs.at[i], w_x.at[i], to_x)

        for i in range(WINDOW):
            x_copy(i).start()
        for j in range(cap):
            ref = w.at[w_base + j]
            remote(ref, ref, w_send.at[0], w_sib.at[0], sib).start()

        n_pieces = cap * nq
        LAG_Z, LAG_Y = 2, 4
        n_steps = n_pieces + LAG_Y

        def pass_on(ref, sem, to):
            remote(ref, ref, w_send.at[0], sem, to).start()

        def weights_step(i):
            if i < n_pieces:
                ref = piece(ox * cap + i // nq, alpha, i % nq)
                remote(ref, ref, w_xs.at[i], w_x.at[i], to_x).wait_recv()
                x_copy(i).wait_send()
                if i + WINDOW < n_pieces:
                    x_copy(i + WINDOW).start()
                pass_on(ref, w_z.at[i], to_z)

                @pl.when(is_end)
                def _():
                    pass_on(ref, w_y.at[i], to_y)

                pass_on(ref, w_sib.at[0], sib)
            k = i - LAG_Z
            if 0 <= k < n_pieces:
                ref_z = piece(ox * cap + k // nq, z_part, k % nq)
                remote(ref_z, ref_z, w_send.at[0], w_z.at[k], to_z).wait_recv()

                @pl.when(jnp.logical_not(is_end))
                def _():
                    pass_on(ref_z, w_y.at[k], to_y)

                pass_on(ref_z, w_sib.at[0], sib)
            k = i - LAG_Y
            if 0 <= k < n_pieces:
                ref_y = piece(ox * cap + k // nq, 1 - y, k % nq)
                remote(ref_y, ref_y, w_send.at[0], w_y.at[k], to_y).wait_recv()
                pass_on(ref_y, w_sib.at[0], sib)

        def weights_end():
            wait_bytes(w.at[pl.ds(0, 2 * cap)], w_sib.at[0])
            wait_bytes(w.at[pl.ds(0, 2 * cap)], w_send.at[0])
            wait_bytes(w.at[0, pl.ds(0, 2 * third)], w_send.at[0])
            wait_bytes(w.at[0, pl.ds(0, 2 * third)], w_send.at[0])

    else:

        def send_w(i, carry):
            p = lax.rem(o_ix + 1 + i, own_n)
            ref = w.at[pl.ds(w_base, cap)]
            remote(ref, ref, w_send.at[0], w_sib.at[0], (s_ix, p)).start()
            return carry

        lax.fori_loop(0, own_n - 1, send_w, 0)

        n_steps = 0

        def weights_step(i):
            pass

        def weights_end():
            wait_bytes(w.at[pl.ds(0, (own_n - 1) * cap)], w_sib.at[0])
            wait_bytes(w.at[pl.ds(0, (own_n - 1) * cap)], w_send.at[0])

    chip = s_ix * NX + x

    def ar_refs(i):
        if i == 3:
            return last_val, last_core, last_chip
        return ar_val.at[i], ar_core.at[i], ar_chip.at[i % ar_chip.shape[0]]

    def ar_pair_copy(i):
        val, core, _ = ar_refs(i)
        return remote(val, core, ar_s.at[i], ar_r.at[i], sib)

    def ar_begin(i):
        ar_pair_copy(i).start()

    def ar_mid(i):
        ar_pair_copy(i).wait()
        val, core, every = ar_refs(i)
        every[chip] = val[...] + core[...]
        for k in chip_peers:
            ref = every.at[chip]
            remote(ref, ref, ar_s2.at[i], ar_r2.at[i], chip_peer(*k)).start()

    def ar_end(i):
        _, _, every = ar_refs(i)
        wait_bytes(every.at[pl.ds(0, chips - 1)], ar_r2.at[i])
        wait_bytes(every.at[pl.ds(0, chips - 1)], ar_s2.at[i])
        return jnp.sum(every[...], axis=0)

    pltpu.make_async_copy(x_hbm, dz, ld_sem.at[cap]).wait()
    for cp in loads:
        cp.wait()
    ts = hp // 3
    total = jnp.zeros((1, ch), F32)
    square = jnp.zeros((1, ch), F32)
    for i in range(3):
        for j in range(ch // 128):
            il[j] = dz[2 * ts * i : 2 * ts * (i + 1), j * 128 : (j + 1) * 128].astype(F32)
        for k in range(2):
            v = jnp.concatenate([il[j, pl.ds(k, ts, stride=2), :] for j in range(ch // 128)], axis=1)
            xf[k * hp + i * ts : k * hp + (i + 1) * ts] = v
            total += colsum(v)
            square += colsum(v * v)
    zero_row = jnp.zeros((1, ch), F32)
    ar_val[0] = jnp.concatenate([total, square], axis=0)
    ar_begin(0)
    has_before = jnp.where(me > 0, 1.0, 0.0).astype(F32)
    has_after = jnp.where(me < n_dev - 1, 1.0, 0.0).astype(F32)
    hx_s[0] = jnp.concatenate([xf[0:1], xf[hp : hp + 1]], axis=0)
    hx_s[1] = jnp.concatenate([xf[hp - 1 : hp], xf[pos - 1 : pos]], axis=0)
    hx = [
        remote(hx_s.at[0], hx_r.at[1], h_s.at[0], h_r.at[0], to_before),
        remote(hx_s.at[1], hx_r.at[0], h_s.at[1], h_r.at[1], to_after),
    ]
    for cp in hx:
        cp.start()
    ar_mid(0)
    for i in range(min(2, n_steps)):
        weights_step(i)
    sums = ar_end(0)
    for cp in hx:
        cp.wait()

    mu1 = sums[0:1] * inv_n
    rstd1 = lax.rsqrt(sums[1:2] * inv_n - mu1 * mu1 + NORM_EPS)
    g1, b1, c1 = sp_ref[0:1], sp_ref[1:2], sp_ref[2:3]
    g2, b2, c2 = sp_ref[3:4], sp_ref[4:5], sp_ref[5:6]
    PAD = 8

    def windows():
        for k in range(2):
            for i in range(3):
                b[k * hp + i * ts : k * hp + (i + 1) * ts] = sh[
                    k, PAD - 1 + i * ts : PAD - 1 + (i + 1) * ts
                ].astype(BF16)
                lo = (4 + k) * hp + i * ts
                b[lo : lo + ts] = sh[k, PAD + 1 + i * ts : PAD + 1 + (i + 1) * ts].astype(BF16)

    for k in range(2):
        for i in range(3):
            lo = k * hp + i * ts
            act, slope = gelu_both((xf[lo : lo + ts] - mu1) * rstd1 * g1 + b1)
            d1[lo : lo + ts] = slope
            b[2 * hp + lo : 2 * hp + lo + ts] = act.astype(BF16)
            sh[k, PAD + i * ts : PAD + (i + 1) * ts] = act
            if 2 + 3 * k + i < n_steps:
                weights_step(2 + 3 * k + i)
    lead, _ = gelu_both((hx_r[0] - mu1) * rstd1 * g1 + b1)
    trail, _ = gelu_both((hx_r[1] - mu1) * rstd1 * g1 + b1)
    lead, trail = lead * has_before, trail * has_after
    for k in range(2):
        sh[k, PAD - 1 : PAD] = lead[k : k + 1]
        sh[k, PAD + hp : PAD + hp + 1] = trail[k : k + 1]
    windows()
    for i in range(8, n_steps):
        weights_step(i)
    weights_end()

    slots = [slot_ref[k] for k in range(NMAT)]

    def cols(n):
        return slice(n * TILE, (n + 1) * TILE)

    def over_tiles(fn):
        for n in range(nt):
            fn(cols(n))

    def conv_tile(n):
        acc = mm(b[0:pos, :], w[slots[0], :, n])
        for t in range(1, 5):
            acc += mm(b[t * hp : t * hp + pos, :], w[slots[t], :, n])
        acc += sp_ref[2:3, n]
        h[:, n] = acc
        ar_val[1, 0:1, n] = colsum(acc)
        ar_val[1, 1:2, n] = colsum(acc * acc)

    over_tiles(conv_tile)
    ar_begin(1)
    for i in range(nt):
        a1t[i * TILE : (i + 1) * TILE, :] = b[2 * hp : 4 * hp, i * TILE : (i + 1) * TILE].T
    ar_mid(1)
    sums = ar_end(1)
    mu2 = sums[0:1] * inv_n
    rstd2 = lax.rsqrt(sums[1:2] * inv_n - mu2 * mu2 + NORM_EPS)
    for k in range(2):
        for i in range(3):
            lo = k * hp + i * ts
            act, slope = gelu_both((h[lo : lo + ts] - mu2) * rstd2 * g2 + b2)
            d2[lo : lo + ts] = slope
            a2[lo : lo + ts] = act.astype(BF16)

    half = ch // 2
    halves = own.shape[1]
    rh = rb // halves

    def put_gradient(p, lhs, rhs):
        def tile(n):
            v = mm(lhs[...], rhs(n))
            keep = jnp.where(c == 0, v[:half], v[half:]).astype(BF16)
            give = jnp.where(c == 0, v[half:], v[:half]).astype(BF16)
            for i in range(NX * NY):
                for k in range(halves):
                    at = (i * halves + k) * rh
                    own[p, k, i // NY, i % NY, :, n] = keep[at : at + rh]
                    snd[p, k, i // NY, i % NY, :, n] = give[at : at + rh]

        over_tiles(tile)
        core_copy(p).start()

    def core_copy(p):
        return remote(snd.at[p], rcv.at[p], c_s.at[p], c_r.at[p], sib)

    def first_copies(p):
        made = []
        for k in range(NX - 1):
            to = lax.rem(x + 1 + k, NX)
            at = NX - 2 - k
            made.append(remote(own.at[p, 0, to], fst.at[p, 0, at], f_s.at[p, 0, k], f_r.at[p, 0, at], dev(z, y, to, c)))
        for k in range(NY - 1 if halves > 1 else 0):
            to = lax.rem(y + 1 + k, NY)
            at = NY - 2 - k
            made.append(remote(own.at[p, 1, :, to], fst.at[p, 1, at], f_s.at[p, 1, k], f_r.at[p, 1, at], dev(z, to, x, c)))
        return made

    def second_copies(p):
        made = []
        for k in range(NY - 1):
            to = lax.rem(y + 1 + k, NY)
            at = NY - 2 - k
            made.append(remote(own.at[p, 0, x, to], sec.at[p, 0, at], s_s.at[p, 0, k], s_r.at[p, 0, at], dev(z, to, x, c)))
        for k in range(NX - 1 if halves > 1 else 0):
            to = lax.rem(x + 1 + k, NX)
            at = NX - 2 - k
            made.append(remote(own.at[p, 1, to, y], sec.at[p, 1, at], s_s.at[p, 1, k], s_r.at[p, 1, at], dev(z, y, to, c)))
        return made

    def wait_all(copies):
        for cp in copies:
            cp.wait_send()
        for cp in copies:
            cp.wait_recv()

    def step_first(p):
        core_copy(p).wait()
        for k in range(halves):
            for i in range(NX):
                for j in range(NY):
                    own[p, k, i, j] = (own[p, k, i, j].astype(F32) + rcv[p, k, i, j].astype(F32)).astype(BF16)
        for cp in first_copies(p):
            cp.start()

    def step_second(p):
        wait_all(first_copies(p))
        for k in range(halves):
            n, m = (NX, NY) if k == 0 else (NY, NX)
            for j in range(m):
                at = (p, 0, x, j) if k == 0 else (p, 1, j, y)
                v = own[at].astype(F32)
                for i in range(n - 1):
                    v += fst[p, k, i, j].astype(F32)
                own[at] = v.astype(BF16)
        for cp in second_copies(p):
            cp.start()

    chain = NZ == 4 and halves == 2
    is_outer = jnp.logical_or(z == 0, z == NZ - 1)
    is_inner = jnp.logical_not(is_outer)
    inner = jnp.where(z < 2, 1, 2)
    my_half = jnp.clip(z - 1, 0, 1)

    def end_copy(p):
        return remote(zs.at[p], zr.at[p, 0], z_s.at[p, 0], z_r.at[p, 0], dev(inner, y, x, c))

    def direct(p):
        return chain and p >= NMAT - 2

    def direct_copy(p, k, i):
        return remote(
            zs.at[p, k], zr.at[p, i, k], z_s.at[p, k], z_r.at[p, 2 * i + k], dev(k + 1, y, x, c)
        )

    def swap_copy(p, k):
        return remote(zs.at[p, k], zr.at[p, 1, k], z_s.at[p, 1], z_r.at[p, 1], dev(lax.rem(3 - z + NZ, NZ), y, x, c))

    def spread_copy(p, k, i):
        if direct(p):
            to = wrap(z + 1 + i, NZ)
        else:
            to = jnp.clip(3 - z, 0, NZ - 1) if i == 1 else jnp.where(z < 2, 0, NZ - 1)
        return remote(res.at[p, k], res.at[p, k], zb_s.at[p, i], zb_r.at[p, k], dev(to, y, x, c))

    def gather_copy(p, at):
        return remote(zs.at[p], zr.at[p, at], z_s.at[p, 0], z_r.at[p, at], dev(0, y, x, c))

    def whole_copy(p, i):
        return remote(res.at[p], res.at[p], zb_s.at[p, i], zb_r.at[p, 0], dev(lax.rem(z + 1 + i, NZ), y, x, c))

    def step_sum(p):
        wait_all(second_copies(p))
        for k in range(halves):
            v = own[p, k, x, y].astype(F32)
            for i in range((NY if k == 0 else NX) - 1):
                v += sec[p, k, i].astype(F32)
            zs[p, k] = v.astype(BF16)
        if direct(p):

            @pl.when(is_outer)
            def _():
                for k in range(2):
                    direct_copy(p, k, z // 3).start()

            @pl.when(is_inner)
            def _():
                direct_copy(p, 1 - my_half, 2).start()

        elif chain:

            @pl.when(is_outer)
            def _():
                end_copy(p).start()

        else:

            @pl.when(z > 0)
            def _():
                gather_copy(p, z - 1).start()

    def step_pass(p):
        if chain and not direct(p):

            @pl.when(is_inner)
            def _():
                end_copy(p).wait_recv()
                zs[p] = (zs[p].astype(F32) + zr[p, 0].astype(F32)).astype(BF16)
                swap_copy(p, 1 - my_half).start()

    def step_root(p):
        if chain:

            @pl.when(is_inner)
            def _():
                v = zs[p, my_half].astype(F32)
                if direct(p):
                    for i in range(3):
                        direct_copy(p, my_half, i).wait_recv()
                        v += zr[p, i, my_half].astype(F32)
                else:
                    swap_copy(p, my_half).wait_recv()
                    v += zr[p, 1, my_half].astype(F32)
                res[p, my_half] = v.astype(BF16)
                for i in range(NZ - 1 if direct(p) else 2):
                    spread_copy(p, my_half, i).start()

        else:

            @pl.when(z == 0)
            def _():
                v = zs[p].astype(F32)
                for i in range(NZ - 1):
                    gather_copy(p, i).wait_recv()
                    v += zr[p, i].astype(F32)
                res[p] = v.astype(BF16)
                for i in range(NZ - 1):
                    whole_copy(p, i).start()

    def step_relay(p):
        if chain and not direct(p):

            @pl.when(is_inner)
            def _():
                spread_copy(p, 1 - my_half, 2).wait_recv()
                spread_copy(p, 1 - my_half, 2).start()

    def step_spread(p):
        if chain:

            @pl.when(is_outer)
            def _():
                for k in range(2):
                    spread_copy(p, k, 0).wait_recv()

            if direct(p):

                @pl.when(is_inner)
                def _():
                    spread_copy(p, 1 - my_half, 0).wait_recv()

        else:

            @pl.when(z > 0)
            def _():
                whole_copy(p, 0).wait_recv()

    def step_done(p):
        if chain:

            @pl.when(is_outer)
            def _():
                if direct(p):
                    for k in range(2):
                        direct_copy(p, k, 0).wait_send()
                else:
                    end_copy(p).wait_send()

            @pl.when(is_inner)
            def _():
                if direct(p):
                    direct_copy(p, 1 - my_half, 2).wait_send()
                else:
                    swap_copy(p, 1 - my_half).wait_send()
                for i in range(NZ - 1):
                    half_sent = my_half if direct(p) or i < 2 else 1 - my_half
                    spread_copy(p, half_sent, i).wait_send()

        else:

            @pl.when(z > 0)
            def _():
                gather_copy(p, z - 1).wait_send()

            @pl.when(z == 0)
            def _():
                for i in range(NZ - 1):
                    whole_copy(p, i).wait_send()

    par[...] = jnp.concatenate([mu2, rstd2, zero_row, zero_row], axis=0)

    def mix_tile(n):
        v = h[:, n] + mm(a2[...], w[slots[5], :, n]) + sp_ref[5:6, n]
        r[:, n] = v
        rd[:, n] = (v[:hp] - v[hp:]).astype(BF16)

    over_tiles(mix_tile)
    for i in range(nt):
        rdt[i * TILE : (i + 1) * TILE, :] = rd[:, i * TILE : (i + 1) * TILE].T

    def pool_tile(n):
        diff = mm(rd[...], w[slots[6], :, n])
        t = 0.5 * jnp.tanh(0.5 * diff)
        p0, p1 = 0.5 + t, 0.5 - t
        r0, r1 = r[0:hp, n], r[hp:pos, n]
        dy = dy_ref[:, n].astype(F32)
        pooled_ref[:, n] = (p0 * r0 + p1 * r1).astype(BF16)
        dl[:, n] = (p0 * p1 * dy * (r0 - r1)).astype(BF16)
        mst[0, 0:hp, n] = p0 * dy
        mst[0, hp:pos, n] = p1 * dy

    over_tiles(pool_tile)
    saves[0].start()
    put_gradient(0, rdt, lambda n: dl[:, n])

    def resid_tile(n):
        v = mm_t(dl[...], w[slots[6], n, :])
        v0 = mst[0, 0:hp, n] + v
        v1 = mst[0, hp:pos, n] - v
        mst[0, 0:hp, n] = v0
        mst[0, hp:pos, n] = v1
        dz[0:hp, n] = v0.astype(BF16)
        dz[hp:pos, n] = v1.astype(BF16)
        last_val[3:4, n] = colsum(v0) + colsum(v1)

    over_tiles(resid_tile)
    step_first(0)

    def branch_tile(n):
        v = mm_t(dz[...], w[slots[5], n, :]) * d2[:, n]
        mst[1, :, n] = v
        xhat = (h[:, n] - par[0:1, n]) * par[1:2, n]
        ar_val[2, 0:1, n] = colsum(v)
        ar_val[2, 1:2, n] = colsum(v * xhat)

    over_tiles(branch_tile)
    ar_begin(2)
    hd_s[0] = jnp.concatenate(
        [v for ref in (mst.at[0], mst.at[1], h) for v in (ref[0:1], ref[hp : hp + 1])]
        + [zero_row, zero_row],
        axis=0,
    )
    hd_s[1] = jnp.concatenate(
        [v for ref in (mst.at[0], mst.at[1], h) for v in (ref[hp - 1 : hp], ref[pos - 1 : pos])]
        + [zero_row, zero_row],
        axis=0,
    )
    hd = [
        remote(hd_s.at[0], hd_r.at[1], h_s.at[2], h_r.at[2], to_before),
        remote(hd_s.at[1], hd_r.at[0], h_s.at[3], h_r.at[3], to_after),
    ]
    for cp in hd:
        cp.start()

    for i in range(nt):
        b[i * TILE : (i + 1) * TILE, :] = a2[:, i * TILE : (i + 1) * TILE].T
    ar_mid(2)
    put_gradient(1, b.at[pl.ds(0, ch)], lambda n: dz[:, n])
    step_second(0)
    step_first(1)
    sums = ar_end(2)
    s2, q2 = sums[0:1], sums[1:2]

    scale2 = rstd2 * g2

    def dh_of(dr, dn, hid):
        xhat = (hid - mu2) * rstd2
        return dr + scale2 * (dn - s2 * inv_n - xhat * (q2 * inv_n))

    e1_local = jnp.zeros((1, ch), F32)
    for k in range(2):
        for i in range(3):
            lo = k * hp + i * ts
            v = dh_of(mst[0, lo : lo + ts], mst[1, lo : lo + ts], h[lo : lo + ts])
            e1_local += colsum(v)
            sh[k, PAD + i * ts : PAD + (i + 1) * ts] = v
            b[2 * hp + lo : 2 * hp + lo + ts] = v.astype(BF16)
    for cp in hd:
        cp.wait()
    lead = dh_of(hd_r[0, 0:2], hd_r[0, 2:4], hd_r[0, 4:6]) * has_before
    trail = dh_of(hd_r[1, 0:2], hd_r[1, 2:4], hd_r[1, 4:6]) * has_after
    for k in range(2):
        sh[k, PAD - 1 : PAD] = lead[k : k + 1]
        sh[k, PAD + hp : PAD + hp + 1] = trail[k : k + 1]
    windows()

    def tap(t):
        lo = (4 - t) * hp
        put_gradient(2 + t, a1t, lambda n: b[lo : lo + pos, n])

    tap(0)
    tap(1)
    step_first(2)
    step_second(1)
    tap(2)
    step_first(3)
    step_sum(0)
    tap(3)
    tap(4)
    step_second(2)
    step_first(4)
    step_pass(0)
    step_sum(1)

    last_val[2:3] = e1_local
    par[...] = jnp.concatenate([mu1, rstd1, zero_row, zero_row], axis=0)

    def input_tile(n):
        acc = mm_t(b[4 * hp : 4 * hp + pos, :], w[slots[0], n, :])
        for t in range(1, 5):
            lo = (4 - t) * hp
            acc += mm_t(b[lo : lo + pos, :], w[slots[t], n, :])
        v = acc * d1[:, n]
        mst[1, :, n] = v
        xhat = (xf[:, n] - par[0:1, n]) * par[1:2, n]
        last_val[0:1, n] = colsum(v)
        last_val[1:2, n] = colsum(v * xhat)

    input_tile(cols(0))
    step_second(3)
    step_first(5)
    step_root(0)
    step_pass(1)
    step_sum(2)
    for i in range(1, nt - 1):
        input_tile(cols(i))
    step_second(4)
    step_first(6)
    step_relay(0)
    step_root(1)
    step_pass(2)
    step_sum(3)
    input_tile(cols(nt - 1))
    ar_begin(3)
    step_second(5)
    step_relay(1)
    step_root(2)
    step_pass(3)
    step_sum(4)
    ar_mid(3)
    step_second(6)
    step_relay(2)
    step_root(3)
    step_pass(4)
    step_sum(5)
    sums = ar_end(3)
    s1, q1, e1, e2 = sums[0:1], sums[1:2], sums[2:3], sums[3:4]
    gs_ref[...] = jnp.concatenate([q1, s1, e1, q2, s2, e2], axis=0)
    saves[2].start()
    scale1 = rstd1 * g1
    def input_rows(i):
        for k in range(2):
            lo = k * hp + i * ts
            xhat = (xf[lo : lo + ts] - mu1) * rstd1
            v = scale1 * (mst[1, lo : lo + ts] - s1 * inv_n - xhat * (q1 * inv_n))
            for j in range(ch // 128):
                il[j, pl.ds(k, ts, stride=2), :] = v[:, j * 128 : (j + 1) * 128]
        for j in range(ch // 128):
            ig_ref[2 * i * ts : 2 * (i + 1) * ts, j * 128 : (j + 1) * 128] = il[j].astype(BF16)

    input_rows(0)
    step_relay(3)
    step_root(4)
    step_sum(6)
    input_rows(1)
    step_relay(4)
    step_root(5)
    input_rows(2)
    saves[1].start()
    step_root(6)
    for p in range(NMAT):
        step_spread(p)

    plane = NX * NY * 2

    def plane_id(py, px, pc):
        return (px * NY + py) * 2 + pc

    mine = plane_id(y, x, c)
    for s in range(own_n * cap):
        at = jnp.int32(0)
        for p in range(NMAT):
            at = jnp.maximum(at, jnp.where(slots[ORDER[p]] == s, p, 0))
        stage[s] = res[at]

    def gather_send(k):
        py, px, pc = plane_peer(*plane_peers[k])
        src = stage.at[pl.ds((px * 2 + pc) * cap, cap)]
        return remote(src, g_ref.at[:, c, x, y], g_s.at[k], g_r.at[mine], dev(z, py, px, pc))

    def gather_recv(k):
        py, px, pc = plane_peer(*plane_peers[k])
        src = stage.at[pl.ds((px * 2 + pc) * cap, cap)]
        return remote(src, g_ref.at[:, pc, px, py], g_s.at[k], g_r.at[plane_id(py, px, pc)], dev(z, py, px, pc))

    def square_copy(k):
        py, px, pc = plane_peer(*plane_peers[k])
        ref = sq_all.at[mine]
        return remote(ref, ref, q_s.at[0], q_r.at[0], dev(z, py, px, pc))

    paired = (NX, NY) == (2, 2) and NZ % 2 == 0 and halves == 2
    diagonal = [k for k, (dy_, dx, _) in enumerate(plane_peers) if paired and dy_ and dx]
    later = [k for k, (dy_, dx, _) in enumerate(plane_peers) if paired and dx and not dy_]
    direct_now = [k for k in range(plane - 1) if k not in diagonal and k not in later]
    odd = lax.rem(z, 2)

    def half_send(k):
        py, px, pc = plane_peer(*plane_peers[k])
        src = stage.at[pl.ds((px * 2 + pc) * cap, cap), odd]
        return remote(src, g_ref.at[:, c, x, y, odd], g_s.at[k], g_r.at[mine], dev(z, py, px, pc))

    def half_recv(k):
        py, px, pc = plane_peer(*plane_peers[k])
        src = stage.at[pl.ds((px * 2 + pc) * cap, cap), odd]
        at = plane_id(py, px, pc)
        return remote(src, g_ref.at[:, pc, px, py, odd], g_s.at[k], g_r.at[at], dev(z, py, px, pc))

    def hand_over(k, part):
        py, px, pc = plane_peer(*plane_peers[k])
        ref = g_ref.at[:, pc, px, py, part]
        return remote(ref, ref, p_s.at[pc], p_r.at[pc], dev(z + 1 - 2 * odd, y, x, c))

    for k in diagonal:
        half_send(k).start()
    for k in direct_now:
        gather_send(k).start()
    keep = pltpu.make_async_copy(
        stage.at[pl.ds(o_ix * cap, cap)], g_ref.at[:, c, x, y], g_l.at[0]
    )
    keep.start()
    sq = jnp.zeros((8, ch), F32)
    for p in range(NMAT):
        for k in range(halves):
            v = res[p, k].astype(F32)
            v = v * v
            for i in range(rh // 8):
                sq += v[i * 8 : (i + 1) * 8]
    sq_all[mine] = sq
    for k in range(plane - 1):
        square_copy(k).start()
    for k in diagonal:
        half_send(k).wait_send()
    for k in later:
        gather_send(k).start()
    for p in range(NMAT):
        step_done(p)
    for k in diagonal:
        half_recv(k).wait_recv()
        hand_over(k, odd).start()
    wait_bytes(sq_all.at[pl.ds(0, plane - 1)], q_r.at[0])
    wait_bytes(sq_all.at[pl.ds(0, plane - 1)], q_s.at[0])
    ssq_ref[...] = jnp.sum(sq_all[...], axis=0)
    saves[3].start()
    for k in direct_now + later:
        gather_send(k).wait_send()
    for k in direct_now + later:
        gather_recv(k).wait_recv()
    for k in diagonal:
        hand_over(k, odd).wait_send()
        hand_over(k, 1 - odd).wait_recv()
    keep.wait()
    for cp in saves:
        cp.wait()


def adam(grads, first_old, second_old):
    first_new = BETA_ONE * first_old + (1.0 - BETA_ONE) * grads
    second_new = BETA_TWO * second_old + (1.0 - BETA_TWO) * grads * grads
    direction = (first_new * (1.0 / (1.0 - BETA_ONE**STEP))) / (
        jnp.sqrt(second_new * (1.0 / (1.0 - BETA_TWO**STEP))) + ADAM_EPS
    )
    return first_new, second_new, direction


def optimizer_kernel(
    slot_ref,
    ssq_hbm,
    gs_hbm,
    sp_hbm,
    sf_hbm,
    ss_hbm,
    g_hbm,
    left_hbm,
    right_hbm,
    first_hbm,
    second_hbm,
    master_hbm,
    norm_ref,
    nsp_hbm,
    nsf_hbm,
    nss_hbm,
    nmaster_hbm,
    nfirst_hbm,
    nsecond_hbm,
    g,
    left,
    right,
    first,
    second,
    master,
    left_low,
    left_t,
    right_low,
    mid,
    turn,
    ssq,
    gs_all,
    sp,
    sf,
    ss,
    in_sem,
    out_sem,
    small_sem,
):
    cap, ch, _ = g.shape
    nt = ch // TILE
    sources = (g_hbm, right_hbm, left_hbm, first_hbm, second_hbm, master_hbm)
    places = (g, right, left, first, second, master)

    def load(i, j):
        return pltpu.make_async_copy(sources[i].at[j], places[i].at[j], in_sem.at[i, j])

    def save(i, j):
        src = (first, second)[i]
        dst = (nfirst_hbm, nsecond_hbm)[i]
        return pltpu.make_async_copy(src.at[j], dst.at[j], out_sem.at[i, j])

    def save_rows(j, i):
        at = pl.ds(i * TILE, TILE)
        return pltpu.make_async_copy(master.at[j, at], nmaster_hbm.at[j, at], out_sem.at[2 + i, j])

    for i in range(3):
        load(i, 0).start()

    smalls = (ssq, gs_all, sp, sf, ss)

    def small_load(i):
        return pltpu.make_async_copy((ssq_hbm, gs_hbm, sp_hbm, sf_hbm, ss_hbm)[i], smalls[i], small_sem.at[i])

    def small_save(i):
        return pltpu.make_async_copy(smalls[2 + i], (nsp_hbm, nsf_hbm, nss_hbm)[i], small_sem.at[i])

    for i in range(5):
        small_load(i).start()

    def small_update():
        for i in range(5):
            small_load(i).wait()
        gs = gs_all[...]
        norm = jnp.sqrt(
            jnp.sum(jnp.sum(ssq[...], axis=0, keepdims=True), axis=1, keepdims=True)
            + jnp.sum(jnp.sum(gs * gs, axis=0, keepdims=True), axis=1, keepdims=True)
        )
        norm_ref[...] = norm
        factor = jnp.minimum(1.0, CLIP_RATIO * ch * math.sqrt(NMAT) / (norm + 1e-06))
        small_first, small_second, small_dir = adam(gs * factor, sf[...], ss[...])
        sp[...] = sp[...] - SMALL_RATE * (small_dir + DECAY_RATE * sp[...])
        sf[...] = small_first
        ss[...] = small_second
        for i in range(3):
            small_save(i).start()
        return factor

    def over_tiles(fn):
        def body(n, carry):
            fn(pl.ds(pl.multiple_of(n * TILE, TILE), TILE))
            return carry

        lax.fori_loop(0, nt, body, 0)

    for j in range(cap):
        slot = lax.axis_index("own") * cap + j
        used = slot_ref[0] == slot
        for k in range(1, NMAT):
            used = jnp.logical_or(used, slot_ref[k] == slot)
        load(0, j).wait()
        load(1, j).wait()
        for i in range(3, 6):
            load(i, j).start()
        right_low[...] = right[j].astype(BF16)

        def mid_tile(n):
            mid[:, n] = mm(g[j], right_low[:, n]).astype(BF16)

        over_tiles(mid_tile)
        if j == 0:
            factor = small_update()
        load(2, j).wait()
        if j + 1 < cap:
            load(0, j + 1).start()
            load(1, j + 1).start()
        left_low[...] = left[j].astype(BF16)
        for i in range(nt):
            left_t[i * TILE : (i + 1) * TILE, :] = left_low[:, i * TILE : (i + 1) * TILE].T
        load(3, j).wait()
        load(4, j).wait()
        if j + 1 < cap:
            load(2, j + 1).start()

        def moment_tile(n):
            grads = factor * mm(left_t[...], mid[:, n])
            f_old, s_old = first[j, :, n], second[j, :, n]
            f_new, s_new, direction = adam(grads, f_old, s_old)
            first[j, :, n] = jnp.where(used, f_new, f_old)
            second[j, :, n] = jnp.where(used, s_new, s_old)
            turn[:, n] = direction.astype(BF16)

        over_tiles(moment_tile)
        save(0, j).start()
        save(1, j).start()

        def back_tile(n):
            mid[:, n] = mm(left_low[...], turn[:, n]).astype(BF16)

        over_tiles(back_tile)
        load(5, j).wait()

        for i in range(nt):
            at = pl.ds(i * TILE, TILE)
            old = master[j, at, :]
            step = mm_t(mid[at, :], right_low[...]) + DECAY_RATE * old
            master[j, at, :] = jnp.where(used, old - LEARN_RATE * step, old)
            save_rows(j, i).start()
    for i in range(3):
        small_save(i).wait()
    for j in range(cap):
        for i in range(2):
            save(i, j).wait()
        for i in range(nt):
            save_rows(j, i).wait()


def optimizer(slots, squares, small_grad, small_params, small_first, small_second, *large):
    cap, ch, _ = large[5].shape
    vm, dma = pltpu.VMEM, pltpu.SemaphoreType.DMA
    in_vmem = pl.BlockSpec(memory_space=pltpu.VMEM)
    anywhere = pl.BlockSpec(memory_space=pl.ANY)
    big = jax.ShapeDtypeStruct((cap, ch, ch), F32)
    small = jax.ShapeDtypeStruct((6, ch), F32)
    return pl.pallas_call(
        optimizer_kernel,
        out_shape=(
            jax.ShapeDtypeStruct((1, 1), F32),
            small,
            small,
            small,
            big,
            big,
            big,
        ),
        in_specs=[pl.BlockSpec(memory_space=pltpu.SMEM)] + [anywhere] * 11,
        out_specs=(in_vmem,) + (anywhere,) * 6,
        scratch_shapes=[vm((cap, ch, ch), BF16)]
        + [vm((cap, ch, ch), F32)] * 5
        + [vm((ch, ch), BF16)] * 5
        + [vm((8, ch), F32)]
        + [vm((6, ch), F32)] * 4
        + [dma((6, cap)), dma((2 + ch // TILE, cap)), dma((5,))],
        compiler_params=pltpu.CompilerParams(vmem_limit_bytes=60 * 2**20),
    )(slots, squares, small_grad, small_params, small_first, small_second, *large)


def block_and_grads(inputs, cotangent, small_params, slot_of_matrix, master):
    pos, ch = inputs.shape
    seq_n, own_n = lax.axis_size("seq"), lax.axis_size("own")
    nx = own_n // 2
    ny = nx
    nz = seq_n // ny
    cap = master.shape[0]
    hp = pos // 2
    slots = cap * own_n
    chips = seq_n * nx
    rb = ch // 2 // (nx * ny)
    plane = nx * ny * 2
    nn = max(nx, ny)
    halves = 2 if rb % 32 == 0 else 1
    rh = rb // halves
    dma = pltpu.SemaphoreType.DMA
    vm = pltpu.VMEM
    scratch = [
        vm((6, ch), F32),
        vm((hp, ch), BF16),
        vm((hp, ch), BF16),
        vm((pos, ch), BF16),
        vm((6, ch), F32),
        vm((8, ch), F32),
        vm((slots, ch, ch), BF16),
        vm((max(cap, 2), ch, ch), F32),
        vm((pos, ch), F32),
        vm((2, hp + 16, ch), F32),
        vm((pos, ch), F32),
        vm((pos, ch), F32),
        vm((pos, ch), BF16),
        vm((pos, ch), F32),
        vm((pos, ch), F32),
        vm((hp, ch), BF16),
        vm((hp, ch), BF16),
        vm((pos, ch), BF16),
        vm((6 * hp, ch), BF16),
        vm((ch, pos), BF16),
        vm((ch, hp), BF16),
        vm((NMAT, halves, nx, ny, rh, ch), BF16),
        vm((NMAT, halves, nx, ny, rh, ch), BF16),
        vm((NMAT, halves, nx, ny, rh, ch), BF16),
        vm((NMAT, halves, nn - 1, nn, rh, ch), BF16),
        vm((NMAT, halves, nn - 1, rh, ch), BF16),
        vm((NMAT, nz - 1, halves, rh, ch), BF16),
        vm((NMAT, halves, rh, ch), BF16),
        vm((NMAT, halves, rh, ch), BF16),
        vm((slots, halves, rh, ch), BF16),
        vm((4, ch), F32),
        vm((3, 2, ch), F32),
        vm((3, 2, ch), F32),
        vm((3 if chips <= 16 else 2, chips, 2, ch), F32),
        vm((4, ch), F32),
        vm((4, ch), F32),
        vm((chips, 4, ch), F32),
        vm((2, 2, ch), F32),
        vm((2, 2, ch), F32),
        vm((2, 8, ch), F32),
        vm((2, 8, ch), F32),
        vm((ch // 128, hp // 3 * 2, 128), F32),
        vm((plane, 8, ch), F32),
        dma((cap + 3,)),
        dma((4,)),
        dma((1,)),
        dma((1,)),
        dma((cap * 4,)),
        dma((cap * 4,)),
        dma((cap * 4,)),
        dma((cap * 4,)),
        dma((4,)),
        dma((4,)),
        dma((4,)),
        dma((4,)),
        dma((4,)),
        dma((4,)),
        dma((NMAT,)),
        dma((NMAT,)),
        dma((NMAT, halves, nn - 1)),
        dma((NMAT, halves, nn - 1)),
        dma((NMAT, halves, nn - 1)),
        dma((NMAT, halves, nn - 1)),
        dma((NMAT, 2)),
        dma((NMAT, 2 * nz - 2)),
        dma((NMAT, nz - 1)),
        dma((NMAT, 2)),
        dma((plane - 1,)),
        dma((plane,)),
        dma((2,)),
        dma((2,)),
        dma((1,)),
        dma((1,)),
        dma((1,)),
    ]
    anywhere = pl.BlockSpec(memory_space=pl.ANY)
    return pl.pallas_call(
        functools.partial(kernel, (nx, ny, nz, cap, pos * seq_n * own_n)),
        out_shape=(
            jax.ShapeDtypeStruct((hp, ch), BF16),
            jax.ShapeDtypeStruct((pos, ch), BF16),
            jax.ShapeDtypeStruct((cap, 2, nx, ny, halves, rh, ch), BF16),
            jax.ShapeDtypeStruct((6, ch), F32),
            jax.ShapeDtypeStruct((8, ch), F32),
        ),
        in_specs=[pl.BlockSpec(memory_space=pltpu.SMEM)] + [anywhere] * 4,
        out_specs=(anywhere,) * 5,
        scratch_shapes=scratch,
        compiler_params=pltpu.CompilerParams(
            collective_id=0, has_side_effects=True, vmem_limit_bytes=63 * 2**20
        ),
    )(slot_of_matrix, small_params, cotangent, inputs, master)


def per_device(
    inputs,
    cotangent,
    small_params,
    small_first,
    small_second,
    slot_of_matrix,
    master,
    first_moment,
    second_moment,
    left_basis,
    right_basis,
):
    cap, ch = master.shape[0], master.shape[2]
    pooled, input_grad, owned, small_grad, squares = block_and_grads(
        inputs, cotangent, small_params, slot_of_matrix, master
    )
    (
        grad_norm,
        new_small,
        small_first_new,
        small_second_new,
        new_master,
        new_first,
        new_second,
    ) = optimizer(
        slot_of_matrix,
        squares,
        small_grad,
        small_params,
        small_first,
        small_second,
        owned.reshape(cap, ch, ch),
        left_basis,
        right_basis,
        first_moment,
        second_moment,
        master,
    )
    return (
        pooled,
        input_grad,
        grad_norm.reshape(()),
        new_master,
        new_first,
        new_second,
        new_small,
        small_first_new,
        small_second_new,
    )


def solution(mesh):
    rows, owned, same = P(("seq", "own"), None), P("own", None, None), P()
    return jax.shard_map(
        per_device,
        mesh=mesh,
        in_specs=(rows, rows, same, same, same, same, owned, owned, owned, owned, owned),
        out_specs=(rows, rows, same, owned, owned, owned, same, same, same),
        check_vma=False,
    )
```

```python
import functools
import math

import jax
import jax.numpy as jnp
from jax import lax
from jax.experimental import pallas as pl
from jax.experimental.pallas import tpu as pltpu
from jax.sharding import PartitionSpec as P

NMAT = 7
STEP = 10
NORM_EPS = 1e-05
BETA_ONE = 0.9
BETA_TWO = 0.999
ADAM_EPS = 1e-08
DECAY_RATE = 0.01
LEARN_RATE = 0.02
SMALL_RATE = 0.1
CLIP_RATIO = 0.5
MESH = pl.DeviceIdType.MESH
F32 = jnp.float32
BF16 = jnp.bfloat16

ORDER = (6, 5, 0, 1, 2, 3, 4)
TILE = 256


def mm(a, b):
    return lax.dot_general(a, b, (((1,), (0,)), ((), ())), preferred_element_type=F32)


def mm_t(a, b):
    return lax.dot_general(a, b, (((1,), (1,)), ((), ())), preferred_element_type=F32)


def gelu_both(v):
    k = math.sqrt(2.0 / math.pi)
    sq = v * v
    t = jnp.tanh(v * (k + (k * 0.044715) * sq))
    half = 0.5 + 0.5 * t
    slope = half + (0.5 * v) * (1.0 - t * t) * (k + (3.0 * k * 0.044715) * sq)
    return v * half, slope


def colsum(v):
    return jnp.sum(v, axis=0, keepdims=True)


def kernel(
    dims,
    slot_ref,
    sp_hbm,
    dy_hbm,
    x_hbm,
    master_hbm,
    pooled_hbm,
    ig_hbm,
    g_ref,
    gs_hbm,
    ssq_hbm,
    sp_ref,
    dy_ref,
    pooled_ref,
    ig_ref,
    gs_ref,
    ssq_ref,
    w,
    mst,
    xf,
    sh,
    d1,
    h,
    a2,
    d2,
    r,
    rd,
    dl,
    dz,
    b,
    a1t,
    rdt,
    snd,
    own,
    rcv,
    fst,
    sec,
    zr,
    zs,
    res,
    stage,
    par,
    ar_val,
    ar_core,
    ar_chip,
    last_val,
    last_core,
    last_chip,
    hx_s,
    hx_r,
    hd_s,
    hd_r,
    il,
    sq_all,
    ld_sem,
    st_sem,
    w_send,
    w_sib,
    w_xs,
    w_x,
    w_y,
    w_z,
    ar_s,
    ar_r,
    ar_s2,
    ar_r2,
    h_s,
    h_r,
    c_s,
    c_r,
    f_s,
    f_r,
    s_s,
    s_r,
    z_s,
    z_r,
    zb_s,
    zb_r,
    g_s,
    g_r,
    p_s,
    p_r,
    q_s,
    q_r,
    g_l,
):
    NX, NY, NZ, cap, rows_total = dims
    pos, ch = dz.shape
    hp = pos // 2
    seq_n, own_n = NZ * NY, NX * 2
    n_dev = seq_n * own_n
    chips = n_dev // 2
    rb = ch // 2 // (NX * NY)
    nt = ch // TILE
    s_ix, o_ix = lax.axis_index("seq"), lax.axis_index("own")
    z, y = s_ix // NY, lax.rem(s_ix, NY)
    x, c = o_ix // 2, lax.rem(o_ix, 2)
    me = s_ix * own_n + o_ix
    inv_n = 1.0 / rows_total

    def dev(z_, y_, x_, c_):
        return (z_ * NY + y_, x_ * 2 + c_)

    def wrap(v, n):
        return jnp.where(v >= n, v - n, v)

    def remote(src, dst, ss, rs, to):
        return pltpu.make_async_remote_copy(
            src_ref=src, dst_ref=dst, send_sem=ss, recv_sem=rs, device_id=to, device_id_type=MESH
        )

    def wait_bytes(ref, sem):
        pltpu.make_async_copy(ref, ref, sem).wait()

    sib = dev(z, y, x, 1 - c)

    for j in range(cap):
        pltpu.make_async_copy(master_hbm.at[j], mst.at[j], ld_sem.at[j]).start()
    pltpu.make_async_copy(x_hbm, dz, ld_sem.at[cap]).start()
    loads = [
        pltpu.make_async_copy(sp_hbm, sp_ref, ld_sem.at[cap + 1]),
        pltpu.make_async_copy(dy_hbm, dy_ref, ld_sem.at[cap + 2]),
    ]
    for cp in loads:
        cp.start()
    saves = [
        pltpu.make_async_copy(src, dst, st_sem.at[i])
        for i, (src, dst) in enumerate(
            ((pooled_ref, pooled_hbm), (ig_ref, ig_hbm), (gs_ref, gs_hbm), (ssq_ref, ssq_hbm))
        )
    ]

    at_end, at_start = o_ix == own_n - 1, o_ix == 0
    to_after = (wrap(s_ix + at_end.astype(jnp.int32), seq_n), wrap(o_ix + 1, own_n))
    to_before = (
        wrap(s_ix + seq_n - at_start.astype(jnp.int32), seq_n),
        wrap(o_ix + own_n - 1, own_n),
    )
    chip_peers = [(ds, dx) for ds in range(seq_n) for dx in range(NX) if ds or dx]
    plane_peers = [
        (dy_, dx, dc) for dy_ in range(NY) for dx in range(NX) for dc in range(2) if dy_ or dx or dc
    ]

    def chip_peer(ds, dx):
        return (wrap(s_ix + ds, seq_n), wrap(x + dx, NX) * 2 + c)

    def plane_peer(dy_, dx, dc):
        return wrap(y + dy_, NY), wrap(x + dx, NX), c + dc - 2 * c * dc

    barrier = pltpu.get_barrier_semaphore()
    crossed = [k for k in plane_peers if k[2]]

    def greet(to):
        pl.semaphore_signal(barrier, inc=1, device_id=to, device_id_type=MESH)

    for k in chip_peers:
        greet(chip_peer(*k))
    for k in crossed:
        py, px, pc = plane_peer(*k)
        greet(dev(z, py, px, pc))
    greet(to_before)
    greet(to_after)
    n_greet = len(chip_peers) + len(crossed) + 2

    for j in range(cap):
        pltpu.make_async_copy(master_hbm.at[j], mst.at[j], ld_sem.at[j]).wait()
        w[o_ix * cap + j] = mst[j].astype(BF16)
    pl.semaphore_wait(barrier, n_greet)

    thirds = (NX, NY, NZ) == (2, 2, 4)
    QR = 64
    third = ch // 3
    nq = third // QR
    w_base = o_ix * cap
    if thirds:
        is_end = jnp.logical_or(z == 0, z == NZ - 1)
        zp = z + 1 - 2 * lax.rem(z, 2)
        ox = (1 - x) * 2 + c
        to_x, to_y, to_z = dev(z, y, 1 - x, c), dev(z, 1 - y, x, c), dev(zp, y, x, c)
        alpha = jnp.where(is_end, y, 2)
        z_part = jnp.where(is_end, 2, y)

        def piece(slot, part, q):
            return w.at[slot, pl.ds(pl.multiple_of(part * third + q * QR, QR), QR)]

        WINDOW = 2

        def x_copy(i):
            ref = piece(w_base + i // nq, alpha, i % nq)
            return remote(ref, ref, w_xs.at[i], w_x.at[i], to_x)

        for i in range(WINDOW):
            x_copy(i).start()
        for j in range(cap):
            ref = w.at[w_base + j]
            remote(ref, ref, w_send.at[0], w_sib.at[0], sib).start()

        n_pieces = cap * nq
        LAG_Z, LAG_Y = 2, 4
        n_steps = n_pieces + LAG_Y

        def pass_on(ref, sem, to):
            remote(ref, ref, w_send.at[0], sem, to).start()

        def weights_step(i):
            if i < n_pieces:
                ref = piece(ox * cap + i // nq, alpha, i % nq)
                remote(ref, ref, w_xs.at[i], w_x.at[i], to_x).wait_recv()
                x_copy(i).wait_send()
                if i + WINDOW < n_pieces:
                    x_copy(i + WINDOW).start()
                pass_on(ref, w_z.at[i], to_z)

                @pl.when(is_end)
                def _():
                    pass_on(ref, w_y.at[i], to_y)

                pass_on(ref, w_sib.at[0], sib)
            k = i - LAG_Z
            if 0 <= k < n_pieces:
                ref_z = piece(ox * cap + k // nq, z_part, k % nq)
                remote(ref_z, ref_z, w_send.at[0], w_z.at[k], to_z).wait_recv()

                @pl.when(jnp.logical_not(is_end))
                def _():
                    pass_on(ref_z, w_y.at[k], to_y)

                pass_on(ref_z, w_sib.at[0], sib)
            k = i - LAG_Y
            if 0 <= k < n_pieces:
                ref_y = piece(ox * cap + k // nq, 1 - y, k % nq)
                remote(ref_y, ref_y, w_send.at[0], w_y.at[k], to_y).wait_recv()
                pass_on(ref_y, w_sib.at[0], sib)

        def weights_end():
            wait_bytes(w.at[pl.ds(0, 2 * cap)], w_sib.at[0])
            wait_bytes(w.at[pl.ds(0, 2 * cap)], w_send.at[0])
            wait_bytes(w.at[0, pl.ds(0, 2 * third)], w_send.at[0])
            wait_bytes(w.at[0, pl.ds(0, 2 * third)], w_send.at[0])

    else:

        def send_w(i, carry):
            p = lax.rem(o_ix + 1 + i, own_n)
            ref = w.at[pl.ds(w_base, cap)]
            remote(ref, ref, w_send.at[0], w_sib.at[0], (s_ix, p)).start()
            return carry

        lax.fori_loop(0, own_n - 1, send_w, 0)

        n_steps = 0

        def weights_step(i):
            pass

        def weights_end():
            wait_bytes(w.at[pl.ds(0, (own_n - 1) * cap)], w_sib.at[0])
            wait_bytes(w.at[pl.ds(0, (own_n - 1) * cap)], w_send.at[0])

    chip = s_ix * NX + x

    def ar_refs(i):
        if i == 3:
            return last_val, last_core, last_chip
        return ar_val.at[i], ar_core.at[i], ar_chip.at[i % ar_chip.shape[0]]

    def ar_pair_copy(i):
        val, core, _ = ar_refs(i)
        return remote(val, core, ar_s.at[i], ar_r.at[i], sib)

    def ar_begin(i):
        ar_pair_copy(i).start()

    def ar_mid(i):
        ar_pair_copy(i).wait()
        val, core, every = ar_refs(i)
        every[chip] = val[...] + core[...]
        for k in chip_peers:
            ref = every.at[chip]
            remote(ref, ref, ar_s2.at[i], ar_r2.at[i], chip_peer(*k)).start()

    def ar_end(i):
        _, _, every = ar_refs(i)
        wait_bytes(every.at[pl.ds(0, chips - 1)], ar_r2.at[i])
        wait_bytes(every.at[pl.ds(0, chips - 1)], ar_s2.at[i])
        return jnp.sum(every[...], axis=0)

    pltpu.make_async_copy(x_hbm, dz, ld_sem.at[cap]).wait()
    for cp in loads:
        cp.wait()
    ts = hp // 3
    total = jnp.zeros((1, ch), F32)
    square = jnp.zeros((1, ch), F32)
    for i in range(3):
        for j in range(ch // 128):
            il[j] = dz[2 * ts * i : 2 * ts * (i + 1), j * 128 : (j + 1) * 128].astype(F32)
        for k in range(2):
            v = jnp.concatenate([il[j, pl.ds(k, ts, stride=2), :] for j in range(ch // 128)], axis=1)
            xf[k * hp + i * ts : k * hp + (i + 1) * ts] = v
            total += colsum(v)
            square += colsum(v * v)
    zero_row = jnp.zeros((1, ch), F32)
    ar_val[0] = jnp.concatenate([total, square], axis=0)
    ar_begin(0)
    has_before = jnp.where(me > 0, 1.0, 0.0).astype(F32)
    has_after = jnp.where(me < n_dev - 1, 1.0, 0.0).astype(F32)
    hx_s[0] = jnp.concatenate([xf[0:1], xf[hp : hp + 1]], axis=0)
    hx_s[1] = jnp.concatenate([xf[hp - 1 : hp], xf[pos - 1 : pos]], axis=0)
    hx = [
        remote(hx_s.at[0], hx_r.at[1], h_s.at[0], h_r.at[0], to_before),
        remote(hx_s.at[1], hx_r.at[0], h_s.at[1], h_r.at[1], to_after),
    ]
    for cp in hx:
        cp.start()
    ar_mid(0)
    for i in range(min(2, n_steps)):
        weights_step(i)
    sums = ar_end(0)
    for cp in hx:
        cp.wait()

    mu1 = sums[0:1] * inv_n
    rstd1 = lax.rsqrt(sums[1:2] * inv_n - mu1 * mu1 + NORM_EPS)
    g1, b1, c1 = sp_ref[0:1], sp_ref[1:2], sp_ref[2:3]
    g2, b2, c2 = sp_ref[3:4], sp_ref[4:5], sp_ref[5:6]
    PAD = 8

    def windows():
        for k in range(2):
            for i in range(3):
                b[k * hp + i * ts : k * hp + (i + 1) * ts] = sh[
                    k, PAD - 1 + i * ts : PAD - 1 + (i + 1) * ts
                ].astype(BF16)
                lo = (4 + k) * hp + i * ts
                b[lo : lo + ts] = sh[k, PAD + 1 + i * ts : PAD + 1 + (i + 1) * ts].astype(BF16)

    for k in range(2):
        for i in range(3):
            lo = k * hp + i * ts
            act, slope = gelu_both((xf[lo : lo + ts] - mu1) * rstd1 * g1 + b1)
            d1[lo : lo + ts] = slope
            b[2 * hp + lo : 2 * hp + lo + ts] = act.astype(BF16)
            sh[k, PAD + i * ts : PAD + (i + 1) * ts] = act
            if 2 + 3 * k + i < n_steps:
                weights_step(2 + 3 * k + i)
    lead, _ = gelu_both((hx_r[0] - mu1) * rstd1 * g1 + b1)
    trail, _ = gelu_both((hx_r[1] - mu1) * rstd1 * g1 + b1)
    lead, trail = lead * has_before, trail * has_after
    for k in range(2):
        sh[k, PAD - 1 : PAD] = lead[k : k + 1]
        sh[k, PAD + hp : PAD + hp + 1] = trail[k : k + 1]
    windows()
    for i in range(8, n_steps):
        weights_step(i)
    weights_end()

    slots = [slot_ref[k] for k in range(NMAT)]

    def cols(n):
        return slice(n * TILE, (n + 1) * TILE)

    def over_tiles(fn):
        for n in range(nt):
            fn(cols(n))

    def conv_tile(n):
        acc = mm(b[0:pos, :], w[slots[0], :, n])
        for t in range(1, 5):
            acc += mm(b[t * hp : t * hp + pos, :], w[slots[t], :, n])
        acc += sp_ref[2:3, n]
        h[:, n] = acc
        ar_val[1, 0:1, n] = colsum(acc)
        ar_val[1, 1:2, n] = colsum(acc * acc)

    over_tiles(conv_tile)
    ar_begin(1)
    for i in range(nt):
        a1t[i * TILE : (i + 1) * TILE, :] = b[2 * hp : 4 * hp, i * TILE : (i + 1) * TILE].T
    ar_mid(1)
    sums = ar_end(1)
    mu2 = sums[0:1] * inv_n
    rstd2 = lax.rsqrt(sums[1:2] * inv_n - mu2 * mu2 + NORM_EPS)
    for k in range(2):
        for i in range(3):
            lo = k * hp + i * ts
            act, slope = gelu_both((h[lo : lo + ts] - mu2) * rstd2 * g2 + b2)
            d2[lo : lo + ts] = slope
            a2[lo : lo + ts] = act.astype(BF16)

    half = ch // 2
    halves = own.shape[1]
    rh = rb // halves

    def put_gradient(p, lhs, rhs):
        def tile(n):
            v = mm(lhs[...], rhs(n))
            keep = jnp.where(c == 0, v[:half], v[half:]).astype(BF16)
            give = jnp.where(c == 0, v[half:], v[:half]).astype(BF16)
            for i in range(NX * NY):
                for k in range(halves):
                    at = (i * halves + k) * rh
                    own[p, k, i // NY, i % NY, :, n] = keep[at : at + rh]
                    snd[p, k, i // NY, i % NY, :, n] = give[at : at + rh]

        over_tiles(tile)
        core_copy(p).start()

    def core_copy(p):
        return remote(snd.at[p], rcv.at[p], c_s.at[p], c_r.at[p], sib)

    def first_copies(p):
        made = []
        for k in range(NX - 1):
            to = lax.rem(x + 1 + k, NX)
            at = NX - 2 - k
            made.append(remote(own.at[p, 0, to], fst.at[p, 0, at], f_s.at[p, 0, k], f_r.at[p, 0, at], dev(z, y, to, c)))
        for k in range(NY - 1 if halves > 1 else 0):
            to = lax.rem(y + 1 + k, NY)
            at = NY - 2 - k
            made.append(remote(own.at[p, 1, :, to], fst.at[p, 1, at], f_s.at[p, 1, k], f_r.at[p, 1, at], dev(z, to, x, c)))
        return made

    def second_copies(p):
        made = []
        for k in range(NY - 1):
            to = lax.rem(y + 1 + k, NY)
            at = NY - 2 - k
            made.append(remote(own.at[p, 0, x, to], sec.at[p, 0, at], s_s.at[p, 0, k], s_r.at[p, 0, at], dev(z, to, x, c)))
        for k in range(NX - 1 if halves > 1 else 0):
            to = lax.rem(x + 1 + k, NX)
            at = NX - 2 - k
            made.append(remote(own.at[p, 1, to, y], sec.at[p, 1, at], s_s.at[p, 1, k], s_r.at[p, 1, at], dev(z, y, to, c)))
        return made

    def wait_all(copies):
        for cp in copies:
            cp.wait_send()
        for cp in copies:
            cp.wait_recv()

    def step_first(p):
        core_copy(p).wait()
        for k in range(halves):
            for i in range(NX):
                for j in range(NY):
                    own[p, k, i, j] = (own[p, k, i, j].astype(F32) + rcv[p, k, i, j].astype(F32)).astype(BF16)
        for cp in first_copies(p):
            cp.start()

    def step_second(p):
        wait_all(first_copies(p))
        for k in range(halves):
            n, m = (NX, NY) if k == 0 else (NY, NX)
            for j in range(m):
                at = (p, 0, x, j) if k == 0 else (p, 1, j, y)
                v = own[at].astype(F32)
                for i in range(n - 1):
                    v += fst[p, k, i, j].astype(F32)
                own[at] = v.astype(BF16)
        for cp in second_copies(p):
            cp.start()

    chain = NZ == 4 and halves == 2
    is_outer = jnp.logical_or(z == 0, z == NZ - 1)
    is_inner = jnp.logical_not(is_outer)
    inner = jnp.where(z < 2, 1, 2)
    my_half = jnp.clip(z - 1, 0, 1)

    def end_copy(p):
        return remote(zs.at[p], zr.at[p, 0], z_s.at[p, 0], z_r.at[p, 0], dev(inner, y, x, c))

    def direct(p):
        return chain and p >= NMAT - 2

    def direct_copy(p, k, i):
        return remote(
            zs.at[p, k], zr.at[p, i, k], z_s.at[p, k], z_r.at[p, 2 * i + k], dev(k + 1, y, x, c)
        )

    def swap_copy(p, k):
        return remote(zs.at[p, k], zr.at[p, 1, k], z_s.at[p, 1], z_r.at[p, 1], dev(lax.rem(3 - z + NZ, NZ), y, x, c))

    def spread_copy(p, k, i):
        if direct(p):
            to = wrap(z + 1 + i, NZ)
        else:
            to = jnp.clip(3 - z, 0, NZ - 1) if i == 1 else jnp.where(z < 2, 0, NZ - 1)
        return remote(res.at[p, k], res.at[p, k], zb_s.at[p, i], zb_r.at[p, k], dev(to, y, x, c))

    def gather_copy(p, at):
        return remote(zs.at[p], zr.at[p, at], z_s.at[p, 0], z_r.at[p, at], dev(0, y, x, c))

    def whole_copy(p, i):
        return remote(res.at[p], res.at[p], zb_s.at[p, i], zb_r.at[p, 0], dev(lax.rem(z + 1 + i, NZ), y, x, c))

    def step_sum(p):
        wait_all(second_copies(p))
        for k in range(halves):
            v = own[p, k, x, y].astype(F32)
            for i in range((NY if k == 0 else NX) - 1):
                v += sec[p, k, i].astype(F32)
            zs[p, k] = v.astype(BF16)
        if direct(p):

            @pl.when(is_outer)
            def _():
                for k in range(2):
                    direct_copy(p, k, z // 3).start()

            @pl.when(is_inner)
            def _():
                direct_copy(p, 1 - my_half, 2).start()

        elif chain:

            @pl.when(is_outer)
            def _():
                end_copy(p).start()

        else:

            @pl.when(z > 0)
            def _():
                gather_copy(p, z - 1).start()

    def step_pass(p):
        if chain and not direct(p):

            @pl.when(is_inner)
            def _():
                end_copy(p).wait_recv()
                zs[p] = (zs[p].astype(F32) + zr[p, 0].astype(F32)).astype(BF16)
                swap_copy(p, 1 - my_half).start()

    def step_root(p):
        if chain:

            @pl.when(is_inner)
            def _():
                v = zs[p, my_half].astype(F32)
                if direct(p):
                    for i in range(3):
                        direct_copy(p, my_half, i).wait_recv()
                        v += zr[p, i, my_half].astype(F32)
                else:
                    swap_copy(p, my_half).wait_recv()
                    v += zr[p, 1, my_half].astype(F32)
                res[p, my_half] = v.astype(BF16)
                for i in range(NZ - 1 if direct(p) else 2):
                    spread_copy(p, my_half, i).start()

        else:

            @pl.when(z == 0)
            def _():
                v = zs[p].astype(F32)
                for i in range(NZ - 1):
                    gather_copy(p, i).wait_recv()
                    v += zr[p, i].astype(F32)
                res[p] = v.astype(BF16)
                for i in range(NZ - 1):
                    whole_copy(p, i).start()

    def step_relay(p):
        if chain and not direct(p):

            @pl.when(is_inner)
            def _():
                spread_copy(p, 1 - my_half, 2).wait_recv()
                spread_copy(p, 1 - my_half, 2).start()

    def step_spread(p):
        if chain:

            @pl.when(is_outer)
            def _():
                for k in range(2):
                    spread_copy(p, k, 0).wait_recv()

            if direct(p):

                @pl.when(is_inner)
                def _():
                    spread_copy(p, 1 - my_half, 0).wait_recv()

        else:

            @pl.when(z > 0)
            def _():
                whole_copy(p, 0).wait_recv()

    def step_done(p):
        if chain:

            @pl.when(is_outer)
            def _():
                if direct(p):
                    for k in range(2):
                        direct_copy(p, k, 0).wait_send()
                else:
                    end_copy(p).wait_send()

            @pl.when(is_inner)
            def _():
                if direct(p):
                    direct_copy(p, 1 - my_half, 2).wait_send()
                else:
                    swap_copy(p, 1 - my_half).wait_send()
                for i in range(NZ - 1):
                    half_sent = my_half if direct(p) or i < 2 else 1 - my_half
                    spread_copy(p, half_sent, i).wait_send()

        else:

            @pl.when(z > 0)
            def _():
                gather_copy(p, z - 1).wait_send()

            @pl.when(z == 0)
            def _():
                for i in range(NZ - 1):
                    whole_copy(p, i).wait_send()

    par[...] = jnp.concatenate([mu2, rstd2, zero_row, zero_row], axis=0)

    def mix_tile(n):
        v = h[:, n] + mm(a2[...], w[slots[5], :, n]) + sp_ref[5:6, n]
        r[:, n] = v
        rd[:, n] = (v[:hp] - v[hp:]).astype(BF16)

    over_tiles(mix_tile)
    for i in range(nt):
        rdt[i * TILE : (i + 1) * TILE, :] = rd[:, i * TILE : (i + 1) * TILE].T

    def pool_tile(n):
        diff = mm(rd[...], w[slots[6], :, n])
        t = 0.5 * jnp.tanh(0.5 * diff)
        p0, p1 = 0.5 + t, 0.5 - t
        r0, r1 = r[0:hp, n], r[hp:pos, n]
        dy = dy_ref[:, n].astype(F32)
        pooled_ref[:, n] = (p0 * r0 + p1 * r1).astype(BF16)
        dl[:, n] = (p0 * p1 * dy * (r0 - r1)).astype(BF16)
        mst[0, 0:hp, n] = p0 * dy
        mst[0, hp:pos, n] = p1 * dy

    over_tiles(pool_tile)
    saves[0].start()
    put_gradient(0, rdt, lambda n: dl[:, n])

    def resid_tile(n):
        v = mm_t(dl[...], w[slots[6], n, :])
        v0 = mst[0, 0:hp, n] + v
        v1 = mst[0, hp:pos, n] - v
        mst[0, 0:hp, n] = v0
        mst[0, hp:pos, n] = v1
        dz[0:hp, n] = v0.astype(BF16)
        dz[hp:pos, n] = v1.astype(BF16)
        last_val[3:4, n] = colsum(v0) + colsum(v1)

    over_tiles(resid_tile)
    step_first(0)

    def branch_tile(n):
        v = mm_t(dz[...], w[slots[5], n, :]) * d2[:, n]
        mst[1, :, n] = v
        xhat = (h[:, n] - par[0:1, n]) * par[1:2, n]
        ar_val[2, 0:1, n] = colsum(v)
        ar_val[2, 1:2, n] = colsum(v * xhat)

    over_tiles(branch_tile)
    ar_begin(2)
    hd_s[0] = jnp.concatenate(
        [v for ref in (mst.at[0], mst.at[1], h) for v in (ref[0:1], ref[hp : hp + 1])]
        + [zero_row, zero_row],
        axis=0,
    )
    hd_s[1] = jnp.concatenate(
        [v for ref in (mst.at[0], mst.at[1], h) for v in (ref[hp - 1 : hp], ref[pos - 1 : pos])]
        + [zero_row, zero_row],
        axis=0,
    )
    hd = [
        remote(hd_s.at[0], hd_r.at[1], h_s.at[2], h_r.at[2], to_before),
        remote(hd_s.at[1], hd_r.at[0], h_s.at[3], h_r.at[3], to_after),
    ]
    for cp in hd:
        cp.start()

    for i in range(nt):
        b[i * TILE : (i + 1) * TILE, :] = a2[:, i * TILE : (i + 1) * TILE].T
    ar_mid(2)
    put_gradient(1, b.at[pl.ds(0, ch)], lambda n: dz[:, n])
    step_second(0)
    step_first(1)
    sums = ar_end(2)
    s2, q2 = sums[0:1], sums[1:2]

    scale2 = rstd2 * g2

    def dh_of(dr, dn, hid):
        xhat = (hid - mu2) * rstd2
        return dr + scale2 * (dn - s2 * inv_n - xhat * (q2 * inv_n))

    e1_local = jnp.zeros((1, ch), F32)
    for k in range(2):
        for i in range(3):
            lo = k * hp + i * ts
            v = dh_of(mst[0, lo : lo + ts], mst[1, lo : lo + ts], h[lo : lo + ts])
            e1_local += colsum(v)
            sh[k, PAD + i * ts : PAD + (i + 1) * ts] = v
            b[2 * hp + lo : 2 * hp + lo + ts] = v.astype(BF16)
    for cp in hd:
        cp.wait()
    lead = dh_of(hd_r[0, 0:2], hd_r[0, 2:4], hd_r[0, 4:6]) * has_before
    trail = dh_of(hd_r[1, 0:2], hd_r[1, 2:4], hd_r[1, 4:6]) * has_after
    for k in range(2):
        sh[k, PAD - 1 : PAD] = lead[k : k + 1]
        sh[k, PAD + hp : PAD + hp + 1] = trail[k : k + 1]
    windows()

    def tap(t):
        lo = (4 - t) * hp
        put_gradient(2 + t, a1t, lambda n: b[lo : lo + pos, n])

    tap(0)
    tap(1)
    step_first(2)
    step_second(1)
    tap(2)
    step_first(3)
    step_sum(0)
    tap(3)
    tap(4)
    step_second(2)
    step_first(4)
    step_pass(0)
    step_sum(1)

    last_val[2:3] = e1_local
    par[...] = jnp.concatenate([mu1, rstd1, zero_row, zero_row], axis=0)

    def input_tile(n):
        acc = mm_t(b[4 * hp : 4 * hp + pos, :], w[slots[0], n, :])
        for t in range(1, 5):
            lo = (4 - t) * hp
            acc += mm_t(b[lo : lo + pos, :], w[slots[t], n, :])
        v = acc * d1[:, n]
        mst[1, :, n] = v
        xhat = (xf[:, n] - par[0:1, n]) * par[1:2, n]
        last_val[0:1, n] = colsum(v)
        last_val[1:2, n] = colsum(v * xhat)

    input_tile(cols(0))
    step_second(3)
    step_first(5)
    step_root(0)
    step_pass(1)
    step_sum(2)
    for i in range(1, nt - 1):
        input_tile(cols(i))
    step_second(4)
    step_first(6)
    step_relay(0)
    step_root(1)
    step_pass(2)
    step_sum(3)
    input_tile(cols(nt - 1))
    ar_begin(3)
    step_second(5)
    step_relay(1)
    step_root(2)
    step_pass(3)
    step_sum(4)
    ar_mid(3)
    step_second(6)
    step_relay(2)
    step_root(3)
    step_pass(4)
    step_sum(5)
    sums = ar_end(3)
    s1, q1, e1, e2 = sums[0:1], sums[1:2], sums[2:3], sums[3:4]
    gs_ref[...] = jnp.concatenate([q1, s1, e1, q2, s2, e2], axis=0)
    saves[2].start()
    scale1 = rstd1 * g1
    def input_rows(i):
        for k in range(2):
            lo = k * hp + i * ts
            xhat = (xf[lo : lo + ts] - mu1) * rstd1
            v = scale1 * (mst[1, lo : lo + ts] - s1 * inv_n - xhat * (q1 * inv_n))
            for j in range(ch // 128):
                il[j, pl.ds(k, ts, stride=2), :] = v[:, j * 128 : (j + 1) * 128]
        for j in range(ch // 128):
            ig_ref[2 * i * ts : 2 * (i + 1) * ts, j * 128 : (j + 1) * 128] = il[j].astype(BF16)

    input_rows(0)
    step_relay(3)
    step_root(4)
    step_sum(6)
    input_rows(1)
    step_relay(4)
    step_root(5)
    input_rows(2)
    saves[1].start()
    step_root(6)
    for p in range(NMAT):
        step_spread(p)

    plane = NX * NY * 2

    def plane_id(py, px, pc):
        return (px * NY + py) * 2 + pc

    mine = plane_id(y, x, c)
    for s in range(own_n * cap):
        at = jnp.int32(0)
        for p in range(NMAT):
            at = jnp.maximum(at, jnp.where(slots[ORDER[p]] == s, p, 0))
        stage[s] = res[at]

    def gather_send(k):
        py, px, pc = plane_peer(*plane_peers[k])
        src = stage.at[pl.ds((px * 2 + pc) * cap, cap)]
        return remote(src, g_ref.at[:, c, x, y], g_s.at[k], g_r.at[mine], dev(z, py, px, pc))

    def gather_recv(k):
        py, px, pc = plane_peer(*plane_peers[k])
        src = stage.at[pl.ds((px * 2 + pc) * cap, cap)]
        return remote(src, g_ref.at[:, pc, px, py], g_s.at[k], g_r.at[plane_id(py, px, pc)], dev(z, py, px, pc))

    def square_copy(k):
        py, px, pc = plane_peer(*plane_peers[k])
        ref = sq_all.at[mine]
        return remote(ref, ref, q_s.at[0], q_r.at[0], dev(z, py, px, pc))

    paired = (NX, NY) == (2, 2) and NZ % 2 == 0 and halves == 2
    diagonal = [k for k, (dy_, dx, _) in enumerate(plane_peers) if paired and dy_ and dx]
    later = [k for k, (dy_, dx, _) in enumerate(plane_peers) if paired and dx and not dy_]
    direct_now = [k for k in range(plane - 1) if k not in diagonal and k not in later]
    odd = lax.rem(z, 2)

    def half_send(k):
        py, px, pc = plane_peer(*plane_peers[k])
        src = stage.at[pl.ds((px * 2 + pc) * cap, cap), odd]
        return remote(src, g_ref.at[:, c, x, y, odd], g_s.at[k], g_r.at[mine], dev(z, py, px, pc))

    def half_recv(k):
        py, px, pc = plane_peer(*plane_peers[k])
        src = stage.at[pl.ds((px * 2 + pc) * cap, cap), odd]
        at = plane_id(py, px, pc)
        return remote(src, g_ref.at[:, pc, px, py, odd], g_s.at[k], g_r.at[at], dev(z, py, px, pc))

    def hand_over(k, part):
        py, px, pc = plane_peer(*plane_peers[k])
        ref = g_ref.at[:, pc, px, py, part]
        return remote(ref, ref, p_s.at[pc], p_r.at[pc], dev(z + 1 - 2 * odd, y, x, c))

    for k in diagonal:
        half_send(k).start()
    for k in direct_now:
        gather_send(k).start()
    keep = pltpu.make_async_copy(
        stage.at[pl.ds(o_ix * cap, cap)], g_ref.at[:, c, x, y], g_l.at[0]
    )
    keep.start()
    sq = jnp.zeros((8, ch), F32)
    for p in range(NMAT):
        for k in range(halves):
            v = res[p, k].astype(F32)
            v = v * v
            for i in range(rh // 8):
                sq += v[i * 8 : (i + 1) * 8]
    sq_all[mine] = sq
    for k in range(plane - 1):
        square_copy(k).start()
    for k in diagonal:
        half_send(k).wait_send()
    for k in later:
        gather_send(k).start()
    for p in range(NMAT):
        step_done(p)
    for k in diagonal:
        half_recv(k).wait_recv()
        hand_over(k, odd).start()
    wait_bytes(sq_all.at[pl.ds(0, plane - 1)], q_r.at[0])
    wait_bytes(sq_all.at[pl.ds(0, plane - 1)], q_s.at[0])
    ssq_ref[...] = jnp.sum(sq_all[...], axis=0)
    saves[3].start()
    for k in direct_now + later:
        gather_send(k).wait_send()
    for k in direct_now + later:
        gather_recv(k).wait_recv()
    for k in diagonal:
        hand_over(k, odd).wait_send()
        hand_over(k, 1 - odd).wait_recv()
    keep.wait()
    for cp in saves:
        cp.wait()


def adam(grads, first_old, second_old):
    first_new = BETA_ONE * first_old + (1.0 - BETA_ONE) * grads
    second_new = BETA_TWO * second_old + (1.0 - BETA_TWO) * grads * grads
    direction = (first_new * (1.0 / (1.0 - BETA_ONE**STEP))) / (
        jnp.sqrt(second_new * (1.0 / (1.0 - BETA_TWO**STEP))) + ADAM_EPS
    )
    return first_new, second_new, direction


def optimizer_kernel(
    slot_ref,
    ssq_hbm,
    gs_hbm,
    sp_hbm,
    sf_hbm,
    ss_hbm,
    g_hbm,
    left_hbm,
    right_hbm,
    first_hbm,
    second_hbm,
    master_hbm,
    norm_ref,
    nsp_hbm,
    nsf_hbm,
    nss_hbm,
    nmaster_hbm,
    nfirst_hbm,
    nsecond_hbm,
    g,
    left,
    right,
    first,
    second,
    master,
    left_low,
    left_t,
    right_low,
    mid,
    turn,
    ssq,
    gs_all,
    sp,
    sf,
    ss,
    in_sem,
    out_sem,
    small_sem,
):
    cap, ch, _ = g.shape
    nt = ch // TILE
    sources = (g_hbm, right_hbm, left_hbm, first_hbm, second_hbm, master_hbm)
    places = (g, right, left, first, second, master)

    def load(i, j):
        return pltpu.make_async_copy(sources[i].at[j], places[i].at[j], in_sem.at[i, j])

    def save(i, j, k):
        src = (first, second)[i]
        dst = (nfirst_hbm, nsecond_hbm)[i]
        at = pl.ds(k * TILE, TILE)
        return pltpu.make_async_copy(src.at[j, :, at], dst.at[j, :, at], out_sem.at[i * nt + k, j])

    def save_rows(j, i):
        at = pl.ds(i * TILE, TILE)
        return pltpu.make_async_copy(master.at[j, at], nmaster_hbm.at[j, at], out_sem.at[2 * nt + i, j])

    for i in range(3):
        load(i, 0).start()

    smalls = (ssq, gs_all, sp, sf, ss)

    def small_load(i):
        return pltpu.make_async_copy((ssq_hbm, gs_hbm, sp_hbm, sf_hbm, ss_hbm)[i], smalls[i], small_sem.at[i])

    def small_save(i):
        return pltpu.make_async_copy(smalls[2 + i], (nsp_hbm, nsf_hbm, nss_hbm)[i], small_sem.at[i])

    for i in range(5):
        small_load(i).start()

    def small_update():
        for i in range(5):
            small_load(i).wait()
        gs = gs_all[...]
        norm = jnp.sqrt(
            jnp.sum(jnp.sum(ssq[...], axis=0, keepdims=True), axis=1, keepdims=True)
            + jnp.sum(jnp.sum(gs * gs, axis=0, keepdims=True), axis=1, keepdims=True)
        )
        norm_ref[...] = norm
        factor = jnp.minimum(1.0, CLIP_RATIO * ch * math.sqrt(NMAT) / (norm + 1e-06))
        small_first, small_second, small_dir = adam(gs * factor, sf[...], ss[...])
        sp[...] = sp[...] - SMALL_RATE * (small_dir + DECAY_RATE * sp[...])
        sf[...] = small_first
        ss[...] = small_second
        for i in range(3):
            small_save(i).start()
        return factor

    def over_tiles(fn):
        for n in range(nt):
            fn(slice(n * TILE, (n + 1) * TILE))

    for j in range(cap):
        slot = lax.axis_index("own") * cap + j
        used = slot_ref[0] == slot
        for k in range(1, NMAT):
            used = jnp.logical_or(used, slot_ref[k] == slot)
        load(0, j).wait()
        load(1, j).wait()
        for i in range(3, 6):
            load(i, j).start()
        right_low[...] = right[j].astype(BF16)

        def mid_tile(n):
            mid[:, n] = mm(g[j], right_low[:, n]).astype(BF16)

        over_tiles(mid_tile)
        if j == 0:
            factor = small_update()
        load(2, j).wait()
        if j + 1 < cap:
            load(0, j + 1).start()
            load(1, j + 1).start()
        left_low[...] = left[j].astype(BF16)
        for i in range(nt):
            left_t[i * TILE : (i + 1) * TILE, :] = left_low[:, i * TILE : (i + 1) * TILE].T
        load(3, j).wait()
        load(4, j).wait()
        if j + 1 < cap:
            load(2, j + 1).start()

        def moment_tile(n):
            grads = factor * mm(left_t[...], mid[:, n])
            f_old, s_old = first[j, :, n], second[j, :, n]
            f_new, s_new, direction = adam(grads, f_old, s_old)
            first[j, :, n] = jnp.where(used, f_new, f_old)
            second[j, :, n] = jnp.where(used, s_new, s_old)
            turn[:, n] = direction.astype(BF16)

        for k in range(nt):
            moment_tile(slice(k * TILE, (k + 1) * TILE))
            save(0, j, k).start()
            save(1, j, k).start()

        def back_tile(n):
            mid[:, n] = mm(left_low[...], turn[:, n]).astype(BF16)

        over_tiles(back_tile)
        load(5, j).wait()

        for i in range(nt):
            at = pl.ds(i * TILE, TILE)
            old = master[j, at, :]
            step = mm_t(mid[at, :], right_low[...]) + DECAY_RATE * old
            master[j, at, :] = jnp.where(used, old - LEARN_RATE * step, old)
            save_rows(j, i).start()
    for i in range(3):
        small_save(i).wait()
    for j in range(cap):
        for i in range(nt):
            save(0, j, i).wait()
            save(1, j, i).wait()
            save_rows(j, i).wait()


def optimizer(slots, squares, small_grad, small_params, small_first, small_second, *large):
    cap, ch, _ = large[5].shape
    vm, dma = pltpu.VMEM, pltpu.SemaphoreType.DMA
    in_vmem = pl.BlockSpec(memory_space=pltpu.VMEM)
    anywhere = pl.BlockSpec(memory_space=pl.ANY)
    big = jax.ShapeDtypeStruct((cap, ch, ch), F32)
    small = jax.ShapeDtypeStruct((6, ch), F32)
    return pl.pallas_call(
        optimizer_kernel,
        out_shape=(
            jax.ShapeDtypeStruct((1, 1), F32),
            small,
            small,
            small,
            big,
            big,
            big,
        ),
        in_specs=[pl.BlockSpec(memory_space=pltpu.SMEM)] + [anywhere] * 11,
        out_specs=(in_vmem,) + (anywhere,) * 6,
        scratch_shapes=[vm((cap, ch, ch), BF16)]
        + [vm((cap, ch, ch), F32)] * 5
        + [vm((ch, ch), BF16)] * 5
        + [vm((8, ch), F32)]
        + [vm((6, ch), F32)] * 4
        + [dma((6, cap)), dma((3 * (ch // TILE), cap)), dma((5,))],
        compiler_params=pltpu.CompilerParams(vmem_limit_bytes=60 * 2**20),
    )(slots, squares, small_grad, small_params, small_first, small_second, *large)


def block_and_grads(inputs, cotangent, small_params, slot_of_matrix, master):
    pos, ch = inputs.shape
    seq_n, own_n = lax.axis_size("seq"), lax.axis_size("own")
    nx = own_n // 2
    ny = nx
    nz = seq_n // ny
    cap = master.shape[0]
    hp = pos // 2
    slots = cap * own_n
    chips = seq_n * nx
    rb = ch // 2 // (nx * ny)
    plane = nx * ny * 2
    nn = max(nx, ny)
    halves = 2 if rb % 32 == 0 else 1
    rh = rb // halves
    dma = pltpu.SemaphoreType.DMA
    vm = pltpu.VMEM
    scratch = [
        vm((6, ch), F32),
        vm((hp, ch), BF16),
        vm((hp, ch), BF16),
        vm((pos, ch), BF16),
        vm((6, ch), F32),
        vm((8, ch), F32),
        vm((slots, ch, ch), BF16),
        vm((max(cap, 2), ch, ch), F32),
        vm((pos, ch), F32),
        vm((2, hp + 16, ch), F32),
        vm((pos, ch), F32),
        vm((pos, ch), F32),
        vm((pos, ch), BF16),
        vm((pos, ch), F32),
        vm((pos, ch), F32),
        vm((hp, ch), BF16),
        vm((hp, ch), BF16),
        vm((pos, ch), BF16),
        vm((6 * hp, ch), BF16),
        vm((ch, pos), BF16),
        vm((ch, hp), BF16),
        vm((NMAT, halves, nx, ny, rh, ch), BF16),
        vm((NMAT, halves, nx, ny, rh, ch), BF16),
        vm((NMAT, halves, nx, ny, rh, ch), BF16),
        vm((NMAT, halves, nn - 1, nn, rh, ch), BF16),
        vm((NMAT, halves, nn - 1, rh, ch), BF16),
        vm((NMAT, nz - 1, halves, rh, ch), BF16),
        vm((NMAT, halves, rh, ch), BF16),
        vm((NMAT, halves, rh, ch), BF16),
        vm((slots, halves, rh, ch), BF16),
        vm((4, ch), F32),
        vm((3, 2, ch), F32),
        vm((3, 2, ch), F32),
        vm((3 if chips <= 16 else 2, chips, 2, ch), F32),
        vm((4, ch), F32),
        vm((4, ch), F32),
        vm((chips, 4, ch), F32),
        vm((2, 2, ch), F32),
        vm((2, 2, ch), F32),
        vm((2, 8, ch), F32),
        vm((2, 8, ch), F32),
        vm((ch // 128, hp // 3 * 2, 128), F32),
        vm((plane, 8, ch), F32),
        dma((cap + 3,)),
        dma((4,)),
        dma((1,)),
        dma((1,)),
        dma((cap * 4,)),
        dma((cap * 4,)),
        dma((cap * 4,)),
        dma((cap * 4,)),
        dma((4,)),
        dma((4,)),
        dma((4,)),
        dma((4,)),
        dma((4,)),
        dma((4,)),
        dma((NMAT,)),
        dma((NMAT,)),
        dma((NMAT, halves, nn - 1)),
        dma((NMAT, halves, nn - 1)),
        dma((NMAT, halves, nn - 1)),
        dma((NMAT, halves, nn - 1)),
        dma((NMAT, 2)),
        dma((NMAT, 2 * nz - 2)),
        dma((NMAT, nz - 1)),
        dma((NMAT, 2)),
        dma((plane - 1,)),
        dma((plane,)),
        dma((2,)),
        dma((2,)),
        dma((1,)),
        dma((1,)),
        dma((1,)),
    ]
    anywhere = pl.BlockSpec(memory_space=pl.ANY)
    return pl.pallas_call(
        functools.partial(kernel, (nx, ny, nz, cap, pos * seq_n * own_n)),
        out_shape=(
            jax.ShapeDtypeStruct((hp, ch), BF16),
            jax.ShapeDtypeStruct((pos, ch), BF16),
            jax.ShapeDtypeStruct((cap, 2, nx, ny, halves, rh, ch), BF16),
            jax.ShapeDtypeStruct((6, ch), F32),
            jax.ShapeDtypeStruct((8, ch), F32),
        ),
        in_specs=[pl.BlockSpec(memory_space=pltpu.SMEM)] + [anywhere] * 4,
        out_specs=(anywhere,) * 5,
        scratch_shapes=scratch,
        compiler_params=pltpu.CompilerParams(
            collective_id=0, has_side_effects=True, vmem_limit_bytes=63 * 2**20
        ),
    )(slot_of_matrix, small_params, cotangent, inputs, master)


def per_device(
    inputs,
    cotangent,
    small_params,
    small_first,
    small_second,
    slot_of_matrix,
    master,
    first_moment,
    second_moment,
    left_basis,
    right_basis,
):
    cap, ch = master.shape[0], master.shape[2]
    pooled, input_grad, owned, small_grad, squares = block_and_grads(
        inputs, cotangent, small_params, slot_of_matrix, master
    )
    (
        grad_norm,
        new_small,
        small_first_new,
        small_second_new,
        new_master,
        new_first,
        new_second,
    ) = optimizer(
        slot_of_matrix,
        squares,
        small_grad,
        small_params,
        small_first,
        small_second,
        owned.reshape(cap, ch, ch),
        left_basis,
        right_basis,
        first_moment,
        second_moment,
        master,
    )
    return (
        pooled,
        input_grad,
        grad_norm.reshape(()),
        new_master,
        new_first,
        new_second,
        new_small,
        small_first_new,
        small_second_new,
    )


def solution(mesh):
    rows, owned, same = P(("seq", "own"), None), P("own", None, None), P()
    return jax.shard_map(
        per_device,
        mesh=mesh,
        in_specs=(rows, rows, same, same, same, same, owned, owned, owned, owned, owned),
        out_specs=(rows, rows, same, owned, owned, owned, same, same, same),
        check_vma=False,
    )
```
